256 devices in a mesh: ctx: 32 (over z, x_hi, core), head: 8 (over y, x_lo).
Axes of the slice: x: 4 (x_hi: 2, x_lo: 2; x = x_hi * 2 + x_lo), y: 4, z: 8, core: 2. Of those that a mesh axis runs over, the one named last changes fastest.
Arguments:
- inputs: bfloat16 [4096, 4096], P('ctx', 'head'), may hold values from -60 to 60
- out_grad: bfloat16 [4096, 4096], P('ctx', 'head'), may hold values from -6 to 6
- norm_gain: float32 [4096], replicated, may hold values from 0.5 to 1.5
- w_query: bfloat16 [4096, 4096], P(None, 'head'), may hold values from -2 to 2
- w_key: bfloat16 [4096, 1024], P(None, 'head'), may hold values from -2 to 2
- w_value: bfloat16 [4096, 1024], P(None, 'head'), may hold values from -0.09375 to 0.09375
- w_out: bfloat16 [4096, 4096], P('head'), may hold values from -0.09375 to 0.09375
- record_lengths: int32 [8], replicated, may hold values from 1 to 2048, 4096 in all
- block_order: int32 [64], replicated, may hold values from 0 to 63, each once
Outputs:
- input_grad: bfloat16 [4096, 4096], P('ctx', 'head')
- saliency: float32 [4096], P('ctx')
The draws below stay inside these ranges and needn't reach their ends.
Inputs may be any that keep to these rules, and one draw needn't show every extreme that they name: `record_lengths`: record lengths sum to 4096. `block_order`: each number once.
All inputs are finite; a program needn't handle non-finite values.
Results may differ from the reference program's by a relative error of at most 0.007.
Values may be sent and summed in bfloat16 or wider, within the bound.
No kernel may reach another device: no remote copies, remote signals or barrier semaphores. Data moves between devices by JAX's collectives and lax.ppermute only.
A program may use at most 128 MiB of HBM per device.

```python
import math
import jax
import jax.numpy as jnp
import numpy as np
from jax import lax

D = 4096
HEADS = 32
KV_HEADS = 8
HEAD_DIM = 128
BLOCK = 64
RECORDS = 8
BLOCKS = 64
SEQ = 4096
MOST_REC = 2048


def shared_projections(key):
    base = jax.random.fold_in(key, 7)
    key_weights = jax.random.normal(jax.random.fold_in(base, 1), (D, KV_HEADS * HEAD_DIM), jnp.float32) * D ** (-0.5)
    fresh = jax.random.normal(jax.random.fold_in(base, 2), (D, HEADS * HEAD_DIM), jnp.float32) * D ** (-0.5)
    query_weights = fresh
    return (jnp.clip(query_weights, -2.0, 2.0), jnp.clip(key_weights, -2.0, 2.0))


def draw_w_query(key, part):
    return shared_projections(key)[0].astype(jnp.bfloat16)


def draw_w_key(key, part):
    return shared_projections(key)[1].astype(jnp.bfloat16)


def draw_inputs(key, part):
    base = jax.random.fold_in(key, 31)
    row_scale = jnp.exp(jax.random.uniform(jax.random.fold_in(base, 1), (SEQ, 1), jnp.float32, 0.0, math.log(10.0)))
    column_scale = jnp.exp(jax.random.uniform(jax.random.fold_in(base, 2), (1, D), jnp.float32, -0.7, 0.7))
    noise = jax.random.normal(jax.random.fold_in(base, 3), (SEQ, D), jnp.float32)
    return jnp.clip(noise * row_scale * column_scale, -60.0, 60.0).astype(jnp.bfloat16)


def shard_levels(own_key, shape, cuts, low, largest):
    loudness = 1.0
    for axis_at, parts in cuts:
        heights = jax.random.uniform(jax.random.fold_in(jax.random.fold_in(own_key, 6), axis_at), (parts,), jnp.float32, low / len(cuts), largest / len(cuts))
        loudness = loudness * jnp.repeat(jnp.exp(heights), shape[axis_at] // parts).reshape((-1,) + (1,) * (len(shape) - 1 - axis_at))
    return loudness


def split_up(number_of, total, limit, skew):
    portions = [(1 << 20) // math.isqrt(rank ** skew) + 1 for rank in range(2, number_of + 1)]
    spare, given = total - limit - (number_of - 1), [1] * (number_of - 1)
    while spare > 0:
        candidates = [i for i in range(number_of - 1) if given[i] < limit]
        whole, remaining = sum([portions[i] for i in candidates]), spare
        for i in candidates:
            more = min(limit - given[i], max(1, remaining * portions[i] // whole), spare)
            given[i] = given[i] + more
            spare = spare - more
    return np.array([limit] + given)


def ragged_sizes(key, count, total, limit, skew):
    if count == 2:
        one = jax.random.randint(key, (), max(1, total - limit), min(limit, total - 1) + 1)
        return jnp.stack([one, total - one])
    sizes = jnp.asarray(split_up(count, total, limit, skew), jnp.int32)
    couples = (count - 1) // 2
    giver, receiver = sizes[1:1 + 2 * couples:2], sizes[2:2 + 2 * couples:2]
    room = jnp.minimum(giver - 1, limit - receiver)
    shifted = jax.random.randint(jax.random.fold_in(key, 1), (couples,), 0, 1 << 20) % (room + 1)
    sizes = sizes.at[1:1 + 2 * couples:2].set(giver - shifted).at[2:2 + 2 * couples:2].set(receiver + shifted)
    return sizes[jax.random.permutation(jax.random.fold_in(key, 2), count)]


def gaussian(own_key, dims, width, reach, shards=(), kind=jnp.bfloat16):
    array = width * jax.random.normal(own_key, dims, jnp.float32)
    if shards:
        array = array * shard_levels(own_key, dims, shards, -0.22, 0.18)
    return jnp.clip(array, -reach, reach).astype(kind)


def setup_inputs(seed: int = 0) -> dict:
    streams_of = jax.random.split(jax.random.key(seed), 10)
    inputs = draw_inputs(jax.random.fold_in(streams_of[9], 71), 0)
    out_grad = gaussian(streams_of[1], (SEQ, D), 1.0, 6.0, ((0, 32), (1, 8)))
    norm_gain = jnp.clip(1.0 + 0.1 * jax.random.normal(streams_of[2], (D,), jnp.float32), 0.5, 1.5)
    w_query = draw_w_query(jax.random.fold_in(streams_of[9], 71), 0)
    w_key = draw_w_key(jax.random.fold_in(streams_of[9], 71), 0)
    w_value = gaussian(streams_of[5], (D, KV_HEADS * HEAD_DIM), D ** -0.5, 0.09375, ((1, 8),))
    w_out = gaussian(streams_of[6], (HEADS * HEAD_DIM, D), (HEADS * HEAD_DIM) ** -0.5, 0.09375, ((0, 8),))
    record_lengths = ragged_sizes(streams_of[7], RECORDS, SEQ, MOST_REC, 2).astype(jnp.int32)
    block_order = jax.random.permutation(streams_of[8], BLOCKS).astype(jnp.int32)
    return dict(inputs=inputs, out_grad=out_grad, norm_gain=norm_gain, w_query=w_query, w_key=w_key, w_value=w_value, w_out=w_out, record_lengths=record_lengths, block_order=block_order)


def timeline_place(order, lengths):
    stored = jnp.arange(SEQ, dtype=jnp.int32)
    matches = (stored // BLOCK)[:, None] == jnp.arange(BLOCKS, dtype=jnp.int32)[None, :]
    position = (lax.optimization_barrier(jnp.sum(jnp.where(matches, order[None, :], 0), axis=1)).astype(jnp.int32) * BLOCK + stored % BLOCK).astype(jnp.int32)
    starts = (jnp.cumsum(lengths) - lengths).astype(jnp.int32)
    record = lax.optimization_barrier(jnp.sum((starts[None, :] <= position[:, None]).astype(jnp.int32), axis=1)).astype(jnp.int32)
    return (position, record)

def reference(inputs, out_grad, norm_gain, w_query, w_key, w_value, w_out, record_lengths, block_order):
    per_group = HEADS // KV_HEADS
    score_scale = HEAD_DIM ** (-0.5)
    position, record = timeline_place(block_order, record_lengths)
    allowed = (record[:, None] == record[None, :]) & (position[None, :] <= position[:, None])
    x_full = inputs.astype(jnp.float32)
    root_mean = jnp.sqrt(lax.optimization_barrier(jnp.mean(x_full * x_full, axis=1)) + 1e-05)
    unit_rows = x_full / root_mean[:, None]
    normed = (unit_rows * norm_gain[None, :]).astype(jnp.bfloat16)
    query = jnp.dot(normed, w_query, preferred_element_type=jnp.float32).astype(jnp.bfloat16)
    keys = jnp.dot(normed, w_key, preferred_element_type=jnp.float32).astype(jnp.bfloat16)
    values = jnp.dot(normed, w_value, preferred_element_type=jnp.float32).astype(jnp.bfloat16)
    contract = (((1,), (1,)), ((), ()))
    out_dir = lax.dot_general(out_grad, w_out, contract, preferred_element_type=jnp.float32).astype(jnp.bfloat16)
    query_groups = jnp.transpose(query.reshape(SEQ, KV_HEADS, per_group, HEAD_DIM), (1, 0, 2, 3))
    dir_groups = jnp.transpose(out_dir.reshape(SEQ, KV_HEADS, per_group, HEAD_DIM), (1, 0, 2, 3))
    key_groups = jnp.transpose(keys.reshape(SEQ, KV_HEADS, HEAD_DIM), (1, 0, 2))
    value_groups = jnp.transpose(values.reshape(SEQ, KV_HEADS, HEAD_DIM), (1, 0, 2))

    def one_group(operands):
        query_g, dir_g, key_g, value_g = operands
        query_f = query_g.astype(jnp.float32)
        dir_f = dir_g.astype(jnp.float32)
        key_f = key_g.astype(jnp.float32)
        value_f = value_g.astype(jnp.float32)
        scores = jnp.einsum('igd,jd->gij', query_f, key_f) * score_scale
        scores = jnp.where(allowed[None, :, :], scores, -1e+30)
        row_max = lax.optimization_barrier(jnp.max(scores, axis=-1))
        log_total = row_max + jnp.log(lax.optimization_barrier(jnp.sum(jnp.exp(scores - row_max[..., None]), axis=-1)))
        probs = jnp.exp(scores - log_total[..., None])
        prob_half = probs.astype(jnp.bfloat16)
        attended = jnp.einsum('gij,jd->igd', prob_half.astype(jnp.float32), value_f).astype(jnp.bfloat16)
        delta = jnp.transpose(lax.optimization_barrier(jnp.sum(dir_f * attended.astype(jnp.float32), axis=-1)), (1, 0))
        prob_grad = jnp.einsum('igd,jd->gij', dir_f, value_f)
        score_grad = (probs * (prob_grad - delta[:, :, None]) * score_scale).astype(jnp.bfloat16)
        query_grad = jnp.einsum('gij,jd->igd', score_grad.astype(jnp.float32), key_f).astype(jnp.bfloat16)
        key_grad = jnp.einsum('gij,igd->jd', score_grad.astype(jnp.float32), query_f).astype(jnp.bfloat16)
        value_grad = jnp.einsum('gij,igd->jd', prob_half.astype(jnp.float32), dir_f).astype(jnp.bfloat16)
        return (query_grad, key_grad, value_grad)
    query_grad, key_grad, value_grad = lax.map(one_group, (query_groups, dir_groups, key_groups, value_groups))
    query_grad = jnp.transpose(query_grad, (1, 0, 2, 3)).reshape(SEQ, HEADS * HEAD_DIM)
    key_grad = jnp.transpose(key_grad, (1, 0, 2)).reshape(SEQ, KV_HEADS * HEAD_DIM)
    value_grad = jnp.transpose(value_grad, (1, 0, 2)).reshape(SEQ, KV_HEADS * HEAD_DIM)
    hidden_grad = lax.dot_general(query_grad, w_query, contract, preferred_element_type=jnp.float32)
    hidden_grad = hidden_grad + lax.dot_general(key_grad, w_key, contract, preferred_element_type=jnp.float32)
    hidden_grad = hidden_grad + lax.dot_general(value_grad, w_value, contract, preferred_element_type=jnp.float32)
    scaled = hidden_grad * norm_gain[None, :]
    inner = lax.optimization_barrier(jnp.mean(scaled * unit_rows, axis=1))
    input_grad = out_grad.astype(jnp.float32) + (scaled - unit_rows * inner[:, None]) / root_mean[:, None]
    saliency = lax.optimization_barrier(jnp.sum(x_full * input_grad, axis=1))
    return (input_grad.astype(jnp.bfloat16), saliency)
```

```python
import functools

import jax
import jax.numpy as jnp
from jax import lax
from jax.experimental import pallas as pl
from jax.experimental.pallas import tpu as pltpu
from jax.sharding import PartitionSpec as P

D = 4096
HEAD_DIM = 128
BLOCK = 64
ROWS = 128
SHARE = 512
HEADS = 4
GROUPS = 8
RECORDS = 8
KEYS = 4096
TILE = 512
WIDE = 2 * HEAD_DIM
EPS = 1e-05
SCALE = HEAD_DIM ** (-0.5)
LOG2E = 1.4426950408889634
NEG = -1e30
HOPS = (0, 4, 3, 5, 2, 6, 1, 7)
EXTRA = 16

f32, bf16 = jnp.float32, jnp.bfloat16
NT = (((1,), (1,)), ((), ()))
NN = (((1,), (0,)), ((), ()))
TN = (((0,), (0,)), ((), ()))


def mm(a, b, dims=NN):
    return lax.dot_general(a, b, dims, preferred_element_type=f32)


def tree(parts):
    while len(parts) > 1:
        parts = [parts[i] + parts[i + 1] for i in range(0, len(parts), 2)]
    return parts[0]


def vmem(n):
    return [pl.BlockSpec(memory_space=pltpu.VMEM)] * n


def smem(n):
    return [pl.BlockSpec(memory_space=pltpu.SMEM)] * n


def call(body, scalars, arrays, outs, mib, flops=0, moved=0, exps=0, scratch=(), name=None):
    return pl.pallas_call(
        body,
        out_shape=outs,
        in_specs=smem(len(scalars)) + vmem(len(arrays)),
        out_specs=jax.tree.map(lambda _: pl.BlockSpec(memory_space=pltpu.VMEM), outs),
        scratch_shapes=list(scratch),
        compiler_params=pltpu.CompilerParams(vmem_limit_bytes=mib << 20),
        cost_estimate=pl.CostEstimate(flops=flops, bytes_accessed=moved, transcendentals=exps),
        name=name,
    )(*scalars, *arrays)


def shape(dims, dtype):
    return jax.ShapeDtypeStruct(dims, dtype)


def spot(head, k):
    return pl.multiple_of(lax.bitwise_xor(head, k) * SHARE, SHARE)


def as_row(column):
    return jnp.transpose(jnp.broadcast_to(column, (ROWS, ROWS)))[:8]


def norm_kernel(ids, *refs):
    xs, (gain, w_key, w_value, kv, normed, mean, mean_row) = refs[:GROUPS], refs[GROUPS:]
    head = ids[1]
    squares = []
    for x in xs:
        wide = x[...].astype(f32)
        squares.append(jnp.sum(wide * wide, axis=1, keepdims=True))
    average = tree(squares) * (1.0 / D)
    mean[...] = jnp.broadcast_to(average, (ROWS, ROWS))
    mean_row[...] = as_row(average)
    inverse = 1.0 / jnp.sqrt(average + EPS)
    for k, x in enumerate(xs):
        at = pl.ds(spot(head, k), SHARE)
        normed[:, at] = (x[...].astype(f32) * inverse * gain[:, at]).astype(bf16)
    kv[:, :HEAD_DIM] = mm(normed[...], w_key[...]).astype(bf16)
    kv[:, HEAD_DIM:] = mm(normed[...], w_value[...]).astype(bf16)


def query_kernel(normed, w_query, query):
    query[...] = mm(normed[...], w_query[...]).astype(bf16)


def out_dir_kernel(ids, *refs):
    xs, (dy, w_out, out_dir, dot_row) = refs[:GROUPS], refs[GROUPS:]
    head = ids[1]
    parts = []
    for k, x in enumerate(xs):
        at = pl.ds(spot(head, k), SHARE)
        parts.append(jnp.sum(x[...].astype(f32) * dy[:, at].astype(f32), axis=1, keepdims=True))
    dot_row[...] = as_row(tree(parts))
    out_dir[...] = mm(dy[...], w_out[...], NT).astype(bf16)


def attention_kernel(ids, order, lengths, query, out_dir, a0, a1, a2, b0, b1, b2, send, keep, dq, big, stacked, dirs):
    ctx = ids[0]
    z, x_hi, core = ctx // 4, (ctx // 2) % 2, ctx % 2
    i = lax.broadcasted_iota(jnp.int32, (ROWS, 1), 0)
    mine = jnp.where(i < BLOCK, order[2 * ctx] * BLOCK + i, order[2 * ctx + 1] * BLOCK + i - BLOCK)
    low = jnp.zeros((ROWS, 1), jnp.int32)
    start = 0
    for r in range(RECORDS):
        low = jnp.where(mine >= start, start, low)
        start = start + lengths[r]
    lane = lax.broadcasted_iota(jnp.int32, (1, ROWS), 1)

    def places(tile):
        found = []
        for n in range(TILE // ROWS):
            chunk = tile * (TILE // ROWS) + n
            cr, hr, hop = chunk // 16, (chunk // 8) % 2, HOPS[chunk % 8]
            owner = ((z + 8 - hop) % 8) * 4 + lax.bitwise_xor(x_hi, hr) * 2 + lax.bitwise_xor(core, cr)
            found.append(
                jnp.where(
                    lane < BLOCK,
                    order[2 * owner] * BLOCK + lane,
                    order[2 * owner + 1] * BLOCK + lane - BLOCK,
                )
            )
        return jnp.concatenate(found, axis=1)

    parts = ((a0, 0), (a0, TILE), (a1, 0), (a2, 0), (b0, 0), (b0, TILE), (b1, 0), (b2, 0))

    def key_tile(t):
        ref, at = parts[t]
        return ref[at : at + TILE, :HEAD_DIM]

    def value_tile(t):
        ref, at = parts[t]
        return ref[at : at + TILE, HEAD_DIM:]

    def rows(h):
        return slice(h * ROWS, (h + 1) * ROWS)

    def lanes(x, op):
        return functools.reduce(op, [x[:, n * ROWS : (n + 1) * ROWS] for n in range(TILE // ROWS)])

    tiles = KEYS // TILE
    for h in range(HEADS):
        stacked[rows(h), :] = query[:, rows(h)]
        dirs[rows(h), :] = out_dir[:, rows(h)]
    top = [jnp.full((ROWS, ROWS), NEG, f32)] * HEADS
    for t in range(tiles):
        place = places(t)
        seen = (place <= mine) & (place >= low)
        scores = mm(stacked[...], key_tile(t), NT)
        for h in range(HEADS):
            masked = jnp.where(seen, scores[rows(h)], NEG)
            big[rows(h), t * TILE : (t + 1) * TILE] = masked
            top[h] = jnp.maximum(top[h], lanes(masked, jnp.maximum))
    shift = [jnp.max(m, axis=1, keepdims=True) * (SCALE * LOG2E) for m in top]
    total = [jnp.zeros((ROWS, ROWS), f32)] * HEADS
    attended = jnp.zeros((HEADS * ROWS, HEAD_DIM), f32)
    halves = []
    for t in range(tiles):
        powers = []
        for h in range(HEADS):
            power = jnp.exp2(big[rows(h), t * TILE : (t + 1) * TILE] * (SCALE * LOG2E) - shift[h])
            total[h] = total[h] + lanes(power, jnp.add)
            big[rows(h), t * TILE : (t + 1) * TILE] = power
            powers.append(power.astype(bf16))
        attended = attended + mm(jnp.concatenate(powers, axis=0), value_tile(t))
    inverse, delta, query_t, dirs_t = [], [], [], []
    for h in range(HEADS):
        inverse.append(1.0 / jnp.sum(total[h], axis=1, keepdims=True))
        mixed = (attended[rows(h)] * inverse[h]).astype(bf16).astype(f32)
        wide = dirs[rows(h), :].astype(f32)
        delta.append(jnp.sum(wide * mixed, axis=1, keepdims=True))
        query_t.append(jnp.transpose(stacked[rows(h), :].astype(f32)).astype(bf16))
        dirs_t.append(jnp.transpose(wide).astype(bf16))
    query_t, dirs_t = jnp.concatenate(query_t, axis=1), jnp.concatenate(dirs_t, axis=1)
    query_grad = jnp.zeros((HEADS * ROWS, HEAD_DIM), f32)
    for t in (4, 5, 6, 7, 0, 1, 2, 3):
        slope = mm(dirs[...], value_tile(t), NT)
        grads, probs = [], []
        for h in range(HEADS):
            prob = big[rows(h), t * TILE : (t + 1) * TILE] * inverse[h]
            probs.append(prob.astype(bf16))
            grads.append((prob * (slope[rows(h)] - delta[h])).astype(bf16))
        grads, probs = jnp.concatenate(grads, axis=0), jnp.concatenate(probs, axis=0)
        query_grad = query_grad + mm(grads, key_tile(t))
        key_part = mm(query_t, grads) * SCALE
        value_part = mm(dirs_t, probs)
        for n in range(TILE // ROWS):
            chunk = (t % 4) * (TILE // ROWS) + n
            ref = send if t >= 4 else keep
            ref[chunk, :HEAD_DIM, :] = key_part[:, n * ROWS : (n + 1) * ROWS].astype(bf16)
            ref[chunk, HEAD_DIM:, :] = value_part[:, n * ROWS : (n + 1) * ROWS].astype(bf16)
    for h in range(HEADS):
        dq[:, rows(h)] = (query_grad[rows(h)] * SCALE).astype(bf16)


def back_query_kernel(dq, w_query, hidden):
    for k in range(GROUPS):
        at = slice(k * SHARE, (k + 1) * SHARE)
        hidden[:, at] = mm(dq[...], w_query[at, :], NT)


def back_kernel(ids, *refs):
    grads, xs = refs[:8], refs[8 : 8 + GROUPS]
    gain, hidden, w_key, w_value, own = refs[8 + GROUPS : 13 + GROUPS]
    sends = refs[13 + GROUPS :]
    head = ids[1]
    both = functools.reduce(lambda a, b: a + b, [g[...].astype(f32) for g in grads]).astype(bf16)
    key_grad, value_grad = both[:HEAD_DIM], both[HEAD_DIM:]
    inner = []
    for k, x in enumerate(xs):
        at = pl.ds(spot(head, k), SHARE)
        block = (
            hidden[:, at]
            + mm(key_grad, w_key[at, :], (((0,), (1,)), ((), ())))
            + mm(value_grad, w_value[at, :], (((0,), (1,)), ((), ())))
        )
        inner.append(jnp.sum(x[...].astype(f32) * gain[:, at] * block, axis=1, keepdims=True))
        if k == 0:
            own[...] = block
        else:
            sends[k][:ROWS, :] = block.astype(bf16)
    row = jnp.transpose(jnp.broadcast_to(tree(inner), (ROWS, ROWS)))[:EXTRA]
    high = row.astype(bf16)
    lower = (row - high.astype(f32)).astype(bf16)
    sends[0][:, :ROWS] = high
    sends[0][:, ROWS : 2 * ROWS] = lower
    for k in range(1, GROUPS):
        sends[k][ROWS:, :] = jnp.zeros((EXTRA, SHARE), bf16)
        sends[k][ROWS:, :ROWS] = high
        sends[k][ROWS:, ROWS : 2 * ROWS] = lower


def last_kernel(ids, *refs):
    own, own_row = refs[:2]
    got = refs[2 : 1 + GROUPS]
    x, dy, gain, mean, mean_row, dot_row, input_grad, saliency = refs[1 + GROUPS :]
    head = ids[1]
    hidden = functools.reduce(lambda a, b: a + b, [g[:ROWS, :].astype(f32) for g in got], own[...])

    def term(ref, at):
        return ref[at : at + EXTRA, :ROWS].astype(f32) + ref[at : at + EXTRA, ROWS : 2 * ROWS].astype(f32)

    total_row = tree([term(own_row, 0)] + [term(g, ROWS) for g in got])[:8]
    root_row = jnp.sqrt(mean_row[...] + EPS)
    inner_row = total_row / (root_row * D)
    saliency[...] = dot_row[...] + (total_row - inner_row * (mean_row[...] * D) / root_row) / root_row
    inner = jnp.transpose(jnp.broadcast_to(inner_row[:1], (ROWS, ROWS)))
    inverse = 1.0 / jnp.sqrt(mean[...] + EPS)
    for n in range(SHARE // ROWS):
        at = slice(n * ROWS, (n + 1) * ROWS)
        unit = x[:, at].astype(f32) * inverse
        scaled = hidden[:, at] * gain[:, pl.ds(pl.multiple_of(head * SHARE + n * ROWS, ROWS), ROWS)]
        input_grad[:, at] = (dy[:, at].astype(f32) + (scaled - unit * inner) * inverse).astype(bf16)


def xor_head(a, k):
    return lax.ppermute(a, "head", [(i, i ^ k) for i in range(GROUPS)])


def xor_ctx(a, k):
    return lax.ppermute(a, "ctx", [(i, i ^ k) for i in range(32)])


def turn(a, k):
    return lax.ppermute(a, "ctx", [(i, (i + 4 * k) % 32) for i in range(32)])


def plus(a, b):
    return (a.astype(f32) + b.astype(f32)).astype(bf16)


ORDER = (6, 7, 2, 3, 4, 5, 1)


def local(inputs, out_grad, norm_gain, w_query, w_key, w_value, w_out, record_lengths, block_order):
    ids = jnp.stack([lax.axis_index("ctx"), lax.axis_index("head")]).astype(jnp.int32)
    gain = norm_gain.reshape(1, D)
    dy = lax.all_gather(out_grad, "head", axis=1, tiled=True)
    came = {k: xor_head(inputs, k) for k in ORDER}
    xs = [inputs] + [came[k] for k in range(1, GROUPS)]
    kv, normed, mean, mean_row = call(
        norm_kernel,
        [ids],
        [*xs, gain, w_key, w_value],
        [
            shape((ROWS, WIDE), bf16),
            shape((ROWS, D), bf16),
            shape((ROWS, ROWS), f32),
            shape((8, ROWS), f32),
        ],
        16,
        flops=2 * ROWS * D * WIDE,
        moved=5 << 20,
        name="norm_kv",
    )
    ring = jnp.concatenate([kv] + [turn(kv, k) for k in HOPS[1:]], axis=0)
    query = call(
        query_kernel,
        [],
        [normed, w_query],
        shape((ROWS, SHARE), bf16),
        16,
        flops=2 * ROWS * D * SHARE,
        moved=5 << 20,
        name="query",
    )
    far0, far1 = xor_ctx(ring[:TILE], 2), xor_ctx(ring[TILE:], 2)
    out_dir, dot_row = call(
        out_dir_kernel,
        [ids],
        [*xs, dy, w_out],
        [shape((ROWS, SHARE), bf16), shape((8, ROWS), f32)],
        16,
        flops=2 * ROWS * D * SHARE,
        moved=6 << 20,
        name="out_dir",
    )
    twin, twin0, twin1 = xor_ctx(ring, 1), xor_ctx(far0, 1), xor_ctx(far1, 1)
    half = (16, WIDE, HEAD_DIM)
    send, keep, dq = call(
        attention_kernel,
        [ids, block_order, record_lengths],
        [query, out_dir, ring, far0, far1, twin, twin0, twin1],
        [shape(half, bf16), shape(half, bf16), shape((ROWS, SHARE), bf16)],
        40,
        flops=12 * SHARE * KEYS * HEAD_DIM,
        moved=5 << 20,
        exps=SHARE * KEYS,
        scratch=[
            pltpu.VMEM((SHARE, KEYS), f32),
            pltpu.VMEM((SHARE, HEAD_DIM), bf16),
            pltpu.VMEM((SHARE, HEAD_DIM), bf16),
        ],
        name="attention",
    )
    got = xor_ctx(send, 1)
    out0, out1 = plus(keep[8:12], got[8:12]), plus(keep[12:], got[12:])
    got0, got1 = xor_ctx(out0, 2), xor_ctx(out1, 2)
    hidden = call(
        back_query_kernel,
        [],
        [dq, w_query],
        shape((ROWS, D), f32),
        16,
        flops=2 * ROWS * D * SHARE,
        moved=6 << 20,
        name="back_query",
    )
    stay = keep[:8].astype(f32) + got[:8].astype(f32)
    grads = []
    for n, k in enumerate(HOPS):
        theirs = got0[n] if n < 4 else got1[n - 4]
        part = (stay[n] + theirs.astype(f32)).astype(bf16)
        grads.append(turn(part, -k) if k else part)
    block = shape((ROWS + EXTRA, SHARE), bf16)
    own, own_row, *sends = call(
        back_kernel,
        [ids],
        [*grads, *xs, gain, hidden, w_key, w_value],
        [shape((ROWS, SHARE), f32), shape((EXTRA, WIDE), bf16)] + [block] * (GROUPS - 1),
        24,
        flops=2 * ROWS * D * WIDE,
        moved=7 << 20,
        name="back_kv",
    )
    home = {k: xor_head(sends[k - 1], k) for k in ORDER}
    input_grad, saliency = call(
        last_kernel,
        [ids],
        [own, own_row, *[home[k] for k in range(1, GROUPS)], inputs, out_grad, gain, mean, mean_row, dot_row],
        [shape((ROWS, SHARE), bf16), shape((8, ROWS), f32)],
        16,
        flops=10 * ROWS * SHARE,
        moved=3 << 20,
        name="last",
    )
    return (input_grad, saliency[0])


def solution(mesh):
    placed = (
        P("ctx", "head"),
        P("ctx", "head"),
        P(),
        P(None, "head"),
        P(None, "head"),
        P(None, "head"),
        P("head", None),
        P(),
        P(),
    )
    return jax.shard_map(
        local, mesh=mesh, in_specs=placed, out_specs=(P("ctx", "head"), P("ctx")), check_vma=False
    )
```

```python
import functools

import jax
import jax.numpy as jnp
from jax import lax
from jax.experimental import pallas as pl
from jax.experimental.pallas import tpu as pltpu
from jax.sharding import PartitionSpec as P

D = 4096
HEAD_DIM = 128
BLOCK = 64
ROWS = 128
SHARE = 512
HEADS = 4
GROUPS = 8
RECORDS = 8
KEYS = 1024
WIDE = 2 * HEAD_DIM
EPS = 1e-05
SCALE = HEAD_DIM ** (-0.5)
LOG2E = 1.4426950408889634
NEG = -1e30
HOPS = (0, 4, 3, 5, 2, 6, 1, 7)
EXTRA = 16
QUAD, RING = 4, 8

f32, bf16 = jnp.float32, jnp.bfloat16
NT = (((1,), (1,)), ((), ()))
NN = (((1,), (0,)), ((), ()))
TN = (((0,), (0,)), ((), ()))


def mm(a, b, dims=NN):
    return lax.dot_general(a, b, dims, preferred_element_type=f32)


def tree(parts):
    while len(parts) > 1:
        parts = [parts[i] + parts[i + 1] for i in range(0, len(parts), 2)]
    return parts[0]


def vmem(n):
    return [pl.BlockSpec(memory_space=pltpu.VMEM)] * n


def smem(n):
    return [pl.BlockSpec(memory_space=pltpu.SMEM)] * n


def call(body, scalars, arrays, outs, mib, flops=0, moved=0, exps=0, scratch=(), name=None):
    return pl.pallas_call(
        body,
        out_shape=outs,
        in_specs=smem(len(scalars)) + vmem(len(arrays)),
        out_specs=jax.tree.map(lambda _: pl.BlockSpec(memory_space=pltpu.VMEM), outs),
        scratch_shapes=list(scratch),
        compiler_params=pltpu.CompilerParams(vmem_limit_bytes=mib << 20),
        cost_estimate=pl.CostEstimate(flops=flops, bytes_accessed=moved, transcendentals=exps),
        name=name,
    )(*scalars, *arrays)


def shape(dims, dtype):
    return jax.ShapeDtypeStruct(dims, dtype)


def spot(head, k):
    return pl.multiple_of(lax.bitwise_xor(head, k) * SHARE, SHARE)


def as_row(column):
    return jnp.transpose(jnp.broadcast_to(column, (ROWS, ROWS)))[:8]


def norm_kernel(ids, *refs):
    xs, (gain, w_key, w_value, kv, normed, mean, mean_row) = refs[:GROUPS], refs[GROUPS:]
    head = ids[1]
    squares = []
    for x in xs:
        wide = x[...].astype(f32)
        squares.append(jnp.sum(wide * wide, axis=1, keepdims=True))
    average = tree(squares) * (1.0 / D)
    mean[...] = jnp.broadcast_to(average, (ROWS, ROWS))
    mean_row[...] = as_row(average)
    inverse = 1.0 / jnp.sqrt(average + EPS)
    for k, x in enumerate(xs):
        at = pl.ds(spot(head, k), SHARE)
        normed[:, at] = (x[...].astype(f32) * inverse * gain[:, at]).astype(bf16)
    kv[:, :HEAD_DIM] = mm(normed[...], w_key[...]).astype(bf16)
    kv[:, HEAD_DIM:] = mm(normed[...], w_value[...]).astype(bf16)


def query_kernel(normed, w_query, query):
    query[...] = mm(normed[...], w_query[...]).astype(bf16)


def out_dir_kernel(ids, *refs):
    xs, dys, (w_out, out_dir, dot_row) = refs[:GROUPS], refs[GROUPS : 2 * GROUPS], refs[2 * GROUPS :]
    head = ids[1]
    parts = []
    total = jnp.zeros((ROWS, SHARE), f32)
    for k, (x, dy) in enumerate(zip(xs, dys)):
        parts.append(jnp.sum(x[...].astype(f32) * dy[...].astype(f32), axis=1, keepdims=True))
        total = total + mm(dy[...], w_out[:, pl.ds(spot(head, k), SHARE)], NT)
    dot_row[...] = as_row(tree(parts))
    out_dir[...] = total.astype(bf16)


def group(n):
    return slice(n * ROWS, (n + 1) * ROWS)


def lanes(x, op):
    return functools.reduce(op, [x[:, group(n)] for n in range(x.shape[1] // ROWS)])


def stack(ref, blocks):
    for b, block in enumerate(blocks):
        for h in range(HEADS):
            ref[group(b * HEADS + h), :] = block[:, group(h)]


def softmax_kernel(ids, order, lengths, *refs):
    queries, dirs, kvs = refs[:QUAD], refs[QUAD : 2 * QUAD], refs[2 * QUAD : 2 * QUAD + RING]
    powers, stats, stacked, key, value = refs[2 * QUAD + RING :]
    ctx = ids[0]
    z, place_in_quad = ctx // QUAD, ctx % QUAD
    lane = lax.broadcasted_iota(jnp.int32, (1, ROWS), 1)
    row = lax.broadcasted_iota(jnp.int32, (ROWS, 1), 0)

    def places(owner, i):
        first, second = order[2 * owner] * BLOCK, order[2 * owner + 1] * BLOCK - BLOCK
        return jnp.where(i < BLOCK, first + i, second + i)

    found = []
    for n, (kv, hop) in enumerate(zip(kvs, HOPS)):
        key[group(n), :] = kv[:, :HEAD_DIM]
        value[group(n), :] = kv[:, HEAD_DIM:]
        found.append(places(((z + RING - hop) % RING) * QUAD + place_in_quad, lane))
    place = jnp.concatenate(found, axis=1)
    stack(stacked, queries)
    packed = jnp.zeros((ROWS, ROWS), f32)
    spots = lax.broadcasted_iota(jnp.int32, (ROWS, ROWS), 1)
    for b in range(QUAD):
        mine = places(lax.bitwise_xor(ctx, b), row)
        low = jnp.zeros((ROWS, 1), jnp.int32)
        start = 0
        for r in range(RECORDS):
            low = jnp.where(mine >= start, start, low)
            start = start + lengths[r]
        seen = (place <= mine) & (place >= low)
        scores = mm(stacked[b * SHARE : (b + 1) * SHARE, :], key[...], NT)
        for h in range(HEADS):
            n = b * HEADS + h
            masked = jnp.where(seen, scores[group(h)], NEG)
            shift = jnp.max(lanes(masked, jnp.maximum), axis=1, keepdims=True) * (SCALE * LOG2E)
            power = jnp.exp2(masked * (SCALE * LOG2E) - shift)
            total = jnp.sum(lanes(power, jnp.add), axis=1, keepdims=True)
            half = power.astype(bf16)
            powers[group(n), :] = half
            mixed = mm(half, value[...])
            dot = jnp.sum(dirs[b][:, group(h)].astype(f32) * mixed, axis=1, keepdims=True)
            for m, column in enumerate((shift, total, dot)):
                packed = jnp.where(spots == 3 * n + m, column, packed)
    stats[...] = packed


def gradient_kernel(*refs):
    queries, dirs, kvs = refs[:QUAD], refs[QUAD : 2 * QUAD], refs[2 * QUAD : 2 * QUAD + RING]
    powers, *rest = refs[2 * QUAD + RING :]
    parts, outs, dq_own, dq_send, (grad, query_t, dirs_n, dirs_t, key, value) = (
        rest[:QUAD],
        rest[QUAD : QUAD + RING],
        rest[QUAD + RING],
        rest[QUAD + RING + 1],
        rest[QUAD + RING + 2 :],
    )
    for n, kv in enumerate(kvs):
        key[group(n), :] = kv[:, :HEAD_DIM]
        value[group(n), :] = kv[:, HEAD_DIM:]
    shifted = []
    for b in range(QUAD):
        for h in range(HEADS):
            n = b * HEADS + h

            def column(r, m):
                at = 3 * ((b ^ r) * HEADS + h) + m
                return parts[r][:, at : at + 1]

            tops = [column(r, 0) for r in range(QUAD)]
            top = functools.reduce(jnp.maximum, tops)
            weights = [jnp.exp2(t - top) for t in tops]
            total = functools.reduce(jnp.add, [w * column(r, 1) for r, w in enumerate(weights)])
            delta = functools.reduce(jnp.add, [w * column(r, 2) for r, w in enumerate(weights)]) / total
            factor = weights[0] / total
            shifted.append(delta * factor)
            scaled = dirs[b][:, group(h)].astype(f32) * factor
            dirs_n[group(n), :] = scaled.astype(bf16)
            dirs_t[:, group(n)] = jnp.transpose(scaled).astype(bf16)
            query_t[:, group(n)] = jnp.transpose(queries[b][:, group(h)].astype(f32)).astype(bf16)
    for b in (1, 3, 0, 2):
        rows = slice(b * SHARE, (b + 1) * SHARE)
        slope = mm(dirs_n[rows, :], value[...], NT)
        for h in range(HEADS):
            n = b * HEADS + h
            grad[group(n), :] = (powers[group(n), :].astype(f32) * (slope[group(h)] - shifted[n])).astype(bf16)
        query_grad = mm(grad[rows, :], key[...]) * SCALE
        for h in range(HEADS):
            if b % 2:
                dq_send[group(b // 2), group(h)] = query_grad[group(h)].astype(bf16)
            else:
                dq_own[group(b // 2), group(h)] = query_grad[group(h)]
    for t in range(2):
        at = slice(t * SHARE, (t + 1) * SHARE)
        key_part = mm(query_t[...], grad[:, at]) * SCALE
        value_part = mm(dirs_t[...], powers[:, at])
        for n in range(SHARE // ROWS):
            out = outs[t * (SHARE // ROWS) + n]
            out[:HEAD_DIM, :] = key_part[:, group(n)].astype(bf16)
            out[HEAD_DIM:, :] = value_part[:, group(n)].astype(bf16)


def add_kernel(own, got, stay, send):
    stay[...] = own[:ROWS, :] + got[:ROWS, :].astype(f32)
    send[...] = (own[ROWS:, :] + got[ROWS:, :].astype(f32)).astype(bf16)


def back_query_kernel(stay, got, w_query, hidden):
    query_grad = (stay[...] + got[...].astype(f32)).astype(bf16)
    for k in range(GROUPS):
        at = slice(k * SHARE, (k + 1) * SHARE)
        hidden[:, at] = mm(query_grad, w_query[at, :], NT)


def back_kernel(ids, *refs):
    grads, xs = refs[:8], refs[8 : 8 + GROUPS]
    gain, hidden, w_key, w_value, own = refs[8 + GROUPS : 13 + GROUPS]
    sends = refs[13 + GROUPS :]
    head = ids[1]
    both = functools.reduce(lambda a, b: a + b, [g[...].astype(f32) for g in grads]).astype(bf16)
    key_grad, value_grad = both[:HEAD_DIM], both[HEAD_DIM:]
    inner = []
    for k, x in enumerate(xs):
        at = pl.ds(spot(head, k), SHARE)
        block = (
            hidden[:, at]
            + mm(key_grad, w_key[at, :], (((0,), (1,)), ((), ())))
            + mm(value_grad, w_value[at, :], (((0,), (1,)), ((), ())))
        )
        inner.append(jnp.sum(x[...].astype(f32) * gain[:, at] * block, axis=1, keepdims=True))
        if k == 0:
            own[...] = block
        else:
            sends[k][:ROWS, :] = block.astype(bf16)
    row = jnp.transpose(jnp.broadcast_to(tree(inner), (ROWS, ROWS)))[:EXTRA]
    high = row.astype(bf16)
    lower = (row - high.astype(f32)).astype(bf16)
    sends[0][:, :ROWS] = high
    sends[0][:, ROWS : 2 * ROWS] = lower
    for k in range(1, GROUPS):
        sends[k][ROWS:, :] = jnp.zeros((EXTRA, SHARE), bf16)
        sends[k][ROWS:, :ROWS] = high
        sends[k][ROWS:, ROWS : 2 * ROWS] = lower


def last_kernel(ids, *refs):
    own, own_row = refs[:2]
    got = refs[2 : 1 + GROUPS]
    x, dy, gain, mean, mean_row, dot_row, input_grad, saliency = refs[1 + GROUPS :]
    head = ids[1]
    hidden = functools.reduce(lambda a, b: a + b, [g[:ROWS, :].astype(f32) for g in got], own[...])

    def term(ref, at):
        return ref[at : at + EXTRA, :ROWS].astype(f32) + ref[at : at + EXTRA, ROWS : 2 * ROWS].astype(f32)

    total_row = tree([term(own_row, 0)] + [term(g, ROWS) for g in got])[:8]
    root_row = jnp.sqrt(mean_row[...] + EPS)
    inner_row = total_row / (root_row * D)
    sums = dot_row[...] + (total_row - inner_row * (mean_row[...] * D) / root_row) / root_row
    saliency[...] = sums[:1]
    inner = jnp.transpose(jnp.broadcast_to(inner_row[:1], (ROWS, ROWS)))
    inverse = 1.0 / jnp.sqrt(mean[...] + EPS)
    for n in range(SHARE // ROWS):
        at = slice(n * ROWS, (n + 1) * ROWS)
        unit = x[:, at].astype(f32) * inverse
        scaled = hidden[:, at] * gain[:, pl.ds(pl.multiple_of(head * SHARE + n * ROWS, ROWS), ROWS)]
        input_grad[:, at] = (dy[:, at].astype(f32) + (scaled - unit * inner) * inverse).astype(bf16)


def xor_head(a, k):
    return lax.ppermute(a, "head", [(i, i ^ k) for i in range(GROUPS)])


def xor_ctx(a, k):
    return lax.ppermute(a, "ctx", [(i, i ^ k) for i in range(32)])


def turn(a, k):
    return lax.ppermute(a, "ctx", [(i, (i + 4 * k) % 32) for i in range(32)])


def spread(a):
    across = xor_ctx(a, 2)
    return [a, xor_ctx(a, 1), across, xor_ctx(across, 1)]


ORDER = (6, 7, 2, 3, 4, 5, 1)


def local(inputs, out_grad, norm_gain, w_query, w_key, w_value, w_out, record_lengths, block_order):
    ids = jnp.stack([lax.axis_index("ctx"), lax.axis_index("head")]).astype(jnp.int32)
    gain = norm_gain.reshape(1, D)
    came = {k: xor_head(inputs, k) for k in ORDER}
    xs = [inputs] + [came[k] for k in range(1, GROUPS)]
    came_dy = {k: xor_head(out_grad, k) for k in ORDER}
    dys = [out_grad] + [came_dy[k] for k in range(1, GROUPS)]
    kv, normed, mean, mean_row = call(
        norm_kernel,
        [ids],
        [*xs, gain, w_key, w_value],
        [
            shape((ROWS, WIDE), bf16),
            shape((ROWS, D), bf16),
            shape((ROWS, ROWS), f32),
            shape((8, ROWS), f32),
        ],
        16,
        flops=2 * ROWS * D * WIDE,
        moved=5 << 20,
        name="norm_kv",
    )
    kvs = [kv] + [turn(kv, k) for k in HOPS[1:]]
    query = call(
        query_kernel,
        [],
        [normed, w_query],
        shape((ROWS, SHARE), bf16),
        16,
        flops=2 * ROWS * D * SHARE,
        moved=5 << 20,
        name="query",
    )
    queries = spread(query)
    out_dir, dot_row = call(
        out_dir_kernel,
        [ids],
        [*xs, *dys, w_out],
        [shape((ROWS, SHARE), bf16), shape((8, ROWS), f32)],
        16,
        flops=2 * ROWS * D * SHARE,
        moved=6 << 20,
        name="out_dir",
    )
    dirs = spread(out_dir)
    tall = QUAD * HEADS * ROWS
    powers, stats = call(
        softmax_kernel,
        [ids, block_order, record_lengths],
        [*queries, *dirs, *kvs],
        [shape((tall, KEYS), bf16), shape((ROWS, ROWS), f32)],
        24,
        flops=4 * tall * KEYS * HEAD_DIM,
        moved=6 << 20,
        exps=tall * KEYS,
        scratch=[pltpu.VMEM((tall, HEAD_DIM), bf16)] + [pltpu.VMEM((KEYS, HEAD_DIM), bf16)] * 2,
        name="softmax",
    )
    parts = [stats, xor_ctx(stats, 1), xor_ctx(stats, 2), xor_ctx(stats, 3)]
    *outs, dq_own, dq_send = call(
        gradient_kernel,
        [],
        [*queries, *dirs, *kvs, powers, *parts],
        [shape((WIDE, HEAD_DIM), bf16)] * RING + [shape((2 * ROWS, SHARE), f32), shape((2 * ROWS, SHARE), bf16)],
        32,
        flops=8 * tall * KEYS * HEAD_DIM,
        moved=6 << 20,
        scratch=[
            pltpu.VMEM((tall, KEYS), bf16),
            pltpu.VMEM((HEAD_DIM, tall), bf16),
            pltpu.VMEM((tall, HEAD_DIM), bf16),
            pltpu.VMEM((HEAD_DIM, tall), bf16),
            pltpu.VMEM((KEYS, HEAD_DIM), bf16),
            pltpu.VMEM((KEYS, HEAD_DIM), bf16),
        ],
        name="gradient",
    )
    grads = [turn(part, -k) if k else part for part, k in zip(outs, HOPS)]
    stay, dq_far = call(
        add_kernel,
        [],
        [dq_own, xor_ctx(dq_send, 1)],
        [shape((ROWS, SHARE), f32), shape((ROWS, SHARE), bf16)],
        16,
        flops=4 * ROWS * SHARE,
        moved=2 << 20,
        name="add",
    )
    hidden = call(
        back_query_kernel,
        [],
        [stay, xor_ctx(dq_far, 2), w_query],
        shape((ROWS, D), f32),
        16,
        flops=2 * ROWS * D * SHARE,
        moved=6 << 20,
        name="back_query",
    )
    block = shape((ROWS + EXTRA, SHARE), bf16)
    own, own_row, *sends = call(
        back_kernel,
        [ids],
        [*grads, *xs, gain, hidden, w_key, w_value],
        [shape((ROWS, SHARE), f32), shape((EXTRA, WIDE), bf16)] + [block] * (GROUPS - 1),
        24,
        flops=2 * ROWS * D * WIDE,
        moved=7 << 20,
        name="back_kv",
    )
    home = {k: xor_head(sends[k - 1], k) for k in ORDER}
    input_grad, saliency = call(
        last_kernel,
        [ids],
        [own, own_row, *[home[k] for k in range(1, GROUPS)], inputs, out_grad, gain, mean, mean_row, dot_row],
        [shape((ROWS, SHARE), bf16), shape((1, ROWS), f32)],
        16,
        flops=10 * ROWS * SHARE,
        moved=3 << 20,
        name="last",
    )
    return (input_grad, saliency.reshape(ROWS))


def solution(mesh):
    placed = (
        P("ctx", "head"),
        P("ctx", "head"),
        P(),
        P(None, "head"),
        P(None, "head"),
        P(None, "head"),
        P("head", None),
        P(),
        P(),
    )
    return jax.shard_map(
        local, mesh=mesh, in_specs=placed, out_specs=(P("ctx", "head"), P("ctx")), check_vma=False
    )
```

```python
import functools

import jax
import jax.numpy as jnp
from jax import lax
from jax.experimental import pallas as pl
from jax.experimental.pallas import tpu as pltpu
from jax.sharding import PartitionSpec as P

D = 4096
HEAD_DIM = 128
BLOCK = 64
ROWS = 128
SHARE = 512
HEADS = 4
GROUPS = 8
RECORDS = 8
KEYS = 1024
WIDE = 2 * HEAD_DIM
EPS = 1e-05
SCALE = HEAD_DIM ** (-0.5)
LOG2E = 1.4426950408889634
NEG = -1e30
HOPS = (0, 4, 3, 5, 2, 6, 1, 7)
EXTRA = 16
QUAD, RING = 4, 8

f32, bf16 = jnp.float32, jnp.bfloat16
NT = (((1,), (1,)), ((), ()))
NN = (((1,), (0,)), ((), ()))
TT = (((0,), (1,)), ((), ()))


def mm(a, b, dims=NN):
    return lax.dot_general(a, b, dims, preferred_element_type=f32)


def tree(parts):
    while len(parts) > 1:
        parts = [parts[i] + parts[i + 1] for i in range(0, len(parts), 2)]
    return parts[0]


def vmem(n):
    return [pl.BlockSpec(memory_space=pltpu.VMEM)] * n


def smem(n):
    return [pl.BlockSpec(memory_space=pltpu.SMEM)] * n


def call(body, scalars, arrays, outs, mib, flops=0, moved=0, exps=0, scratch=(), name=None):
    return pl.pallas_call(
        body,
        out_shape=outs,
        in_specs=smem(len(scalars)) + vmem(len(arrays)),
        out_specs=jax.tree.map(lambda _: pl.BlockSpec(memory_space=pltpu.VMEM), outs),
        scratch_shapes=list(scratch),
        compiler_params=pltpu.CompilerParams(vmem_limit_bytes=mib << 20),
        cost_estimate=pl.CostEstimate(flops=flops, bytes_accessed=moved, transcendentals=exps),
        name=name,
    )(*scalars, *arrays)


def shape(dims, dtype):
    return jax.ShapeDtypeStruct(dims, dtype)


def spot(head, k):
    return pl.multiple_of(lax.bitwise_xor(head, k) * SHARE, SHARE)


def as_row(column):
    return jnp.transpose(jnp.broadcast_to(column, (ROWS, ROWS)))[:8]


def touch_kernel(*refs):
    refs[-1][...] = jnp.zeros((8, ROWS), f32)


def norm_kernel(ids, *refs):
    xs = [r.at[:ROWS, :] for r in refs[:GROUPS]]
    gain, w_key, w_value, w_query, _, kv, query, mean, mean_row, normed = refs[GROUPS:]
    head = ids[1]
    squares = []
    for x in xs:
        wide = x[...].astype(f32)
        squares.append(jnp.sum(wide * wide, axis=1, keepdims=True))
    average = tree(squares) * (1.0 / D)
    mean[...] = jnp.broadcast_to(average, (ROWS, ROWS))
    mean_row[...] = as_row(average)
    inverse = 1.0 / jnp.sqrt(average + EPS)
    for k, x in enumerate(xs):
        at = pl.ds(spot(head, k), SHARE)
        normed[:, at] = (x[...].astype(f32) * inverse * gain[:, at]).astype(bf16)
    kv[:, :HEAD_DIM] = mm(normed[...], w_key[...]).astype(bf16)
    kv[:, HEAD_DIM:] = mm(normed[...], w_value[...]).astype(bf16)
    query[...] = mm(normed[...], w_query[...]).astype(bf16)


def out_dir_kernel(ids, *refs):
    pairs, w_out, out_dir, dot_row = refs[:GROUPS], refs[GROUPS], refs[-2], refs[-1]
    head = ids[1]
    total = jnp.zeros((ROWS, SHARE), f32)
    parts = []
    for k, pair in enumerate(pairs):
        dy = pair[ROWS:, :]
        total = total + mm(dy, w_out[:, pl.ds(spot(head, k), SHARE)], NT)
        parts.append(jnp.sum(pair[:ROWS, :].astype(f32) * dy.astype(f32), axis=1, keepdims=True))
    out_dir[...] = total.astype(bf16)
    dot_row[...] = as_row(tree(parts))


def group(n):
    return slice(n * ROWS, (n + 1) * ROWS)


def lanes(x, op):
    return functools.reduce(op, [x[:, group(n)] for n in range(x.shape[1] // ROWS)])


def stack(ref, blocks):
    for b, block in enumerate(blocks):
        for h in range(HEADS):
            ref[group(b * HEADS + h), :] = block[:, group(h)]


def softmax_kernel(ids, order, lengths, *refs):
    queries, kvs = refs[:QUAD], refs[QUAD : QUAD + RING]
    powers, mixed, stats, stacked, key, value = refs[QUAD + RING :]
    ctx = ids[0]
    z, place_in_quad = ctx // QUAD, ctx % QUAD
    lane = lax.broadcasted_iota(jnp.int32, (1, ROWS), 1)
    row = lax.broadcasted_iota(jnp.int32, (ROWS, 1), 0)

    def places(owner, i):
        first, second = order[2 * owner] * BLOCK, order[2 * owner + 1] * BLOCK - BLOCK
        return jnp.where(i < BLOCK, first + i, second + i)

    found = []
    for n, (kv, hop) in enumerate(zip(kvs, HOPS)):
        key[group(n), :] = kv[:, :HEAD_DIM]
        value[group(n), :] = kv[:, HEAD_DIM:]
        found.append(places(((z + RING - hop) % RING) * QUAD + place_in_quad, lane))
    place = jnp.concatenate(found, axis=1)
    stack(stacked, queries)
    packed = jnp.zeros((ROWS, ROWS), f32)
    spots = lax.broadcasted_iota(jnp.int32, (ROWS, ROWS), 1)
    for b in range(QUAD):
        mine = places(lax.bitwise_xor(ctx, b), row)
        low = jnp.zeros((ROWS, 1), jnp.int32)
        start = 0
        for r in range(RECORDS):
            low = jnp.where(mine >= start, start, low)
            start = start + lengths[r]
        seen = (place <= mine) & (place >= low)
        scores = mm(stacked[b * SHARE : (b + 1) * SHARE, :], key[...], NT)
        for h in range(HEADS):
            n = b * HEADS + h
            masked = jnp.where(seen, scores[group(h)], NEG)
            shift = jnp.max(lanes(masked, jnp.maximum), axis=1, keepdims=True) * (SCALE * LOG2E)
            power = jnp.exp2(masked * (SCALE * LOG2E) - shift)
            total = jnp.sum(lanes(power, jnp.add), axis=1, keepdims=True)
            half = power.astype(bf16)
            powers[group(n), :] = half
            mixed[group(n), :] = mm(half, value[...])
            for m, column in enumerate((shift, total)):
                packed = jnp.where(spots == QUAD * HEADS * m + n, column, packed)
    stats[...] = packed


def pack_kernel(stats, mixed, *refs):
    dirs, out = refs[:QUAD], refs[QUAD]
    packed = stats[...]
    spots = lax.broadcasted_iota(jnp.int32, (ROWS, ROWS), 1)
    for b in range(QUAD):
        for h in range(HEADS):
            n = b * HEADS + h
            dot = jnp.sum(dirs[b][:, group(h)].astype(f32) * mixed[group(n), :], axis=1, keepdims=True)
            packed = jnp.where(spots == 2 * QUAD * HEADS + n, dot, packed)
    out[...] = packed


def gradient_kernel(*refs):
    queries, dirs, kvs = refs[:QUAD], refs[QUAD : 2 * QUAD], refs[2 * QUAD : 2 * QUAD + RING]
    powers, *rest = refs[2 * QUAD + RING :]
    parts, outs, dq_own, dq_send, (grad, query_t, dirs_n, dirs_t, key, value) = (
        rest[:QUAD],
        rest[QUAD : QUAD + RING],
        rest[QUAD + RING],
        rest[QUAD + RING + 1],
        rest[QUAD + RING + 2 :],
    )
    for n, kv in enumerate(kvs):
        key[group(n), :] = kv[:, :HEAD_DIM]
        value[group(n), :] = kv[:, HEAD_DIM:]
    lane = lax.broadcasted_iota(jnp.int32, (ROWS, ROWS), 1)
    groups = QUAD * HEADS

    def toward(x, n):
        return pltpu.roll(x, (ROWS - n) % ROWS, 1)

    def swap(x, n):
        return jnp.where(lane & n == 0, toward(x, n), toward(x, -n))

    same = []
    for r in range(QUAD):
        x = parts[r][...]
        for bit in (1, 2):
            if r & bit:
                x = swap(x, bit * HEADS)
        same.append(x)
    top = functools.reduce(jnp.maximum, same)
    weights = [jnp.exp2(jnp.where(lane < groups, x - top, 0.0)) for x in same]
    total = functools.reduce(jnp.add, [w * toward(x, groups) for w, x in zip(weights, same)])
    total = jnp.where(lane < groups, total, 1.0)
    dot = functools.reduce(jnp.add, [w * toward(x, 2 * groups) for w, x in zip(weights, same)])
    factors = weights[0] / total
    shifts = dot / total * factors
    shifted = []
    for b in range(QUAD):
        for h in range(HEADS):
            n = b * HEADS + h
            shifted.append(shifts[:, n : n + 1])
            scaled = dirs[b][:, group(h)].astype(f32) * factors[:, n : n + 1]
            dirs_n[group(n), :] = scaled.astype(bf16)
            dirs_t[:, group(n)] = jnp.transpose(scaled).astype(bf16)
            query_t[:, group(n)] = jnp.transpose(queries[b][:, group(h)].astype(f32)).astype(bf16)
    for b in (1, 3, 0, 2):
        rows = slice(b * SHARE, (b + 1) * SHARE)
        slope = mm(dirs_n[rows, :], value[...], NT)
        for h in range(HEADS):
            n = b * HEADS + h
            grad[group(n), :] = (powers[group(n), :].astype(f32) * (slope[group(h)] - shifted[n])).astype(bf16)
        query_grad = mm(grad[rows, :], key[...]) * SCALE
        for h in range(HEADS):
            if b % 2:
                dq_send[group(b // 2), group(h)] = query_grad[group(h)].astype(bf16)
            else:
                dq_own[group(b // 2), group(h)] = query_grad[group(h)]
    for t in range(2):
        at = slice(t * SHARE, (t + 1) * SHARE)
        key_part = mm(query_t[...], grad[:, at]) * SCALE
        value_part = mm(dirs_t[...], powers[:, at])
        for n in range(SHARE // ROWS):
            out = outs[t * (SHARE // ROWS) + n]
            out[:HEAD_DIM, :] = key_part[:, group(n)].astype(bf16)
            out[HEAD_DIM:, :] = value_part[:, group(n)].astype(bf16)


def add_kernel(own, got, stay, send):
    stay[...] = own[:ROWS, :] + got[:ROWS, :].astype(f32)
    send[...] = (own[ROWS:, :] + got[ROWS:, :].astype(f32)).astype(bf16)


def back_query_kernel(stay, got, w_query, hidden):
    query_grad = (stay[...] + got[...].astype(f32)).astype(bf16)
    for k in range(GROUPS):
        at = slice(k * SHARE, (k + 1) * SHARE)
        hidden[:, at] = mm(query_grad, w_query[at, :], NT)


def back_kernel(ids, *refs):
    grads, pairs = refs[:RING], refs[RING : RING + GROUPS]
    gain, hidden, w_key, w_value, own, own_row, *sends = refs[RING + GROUPS :]
    head = ids[1]
    both = functools.reduce(lambda a, b: a + b, [g[...].astype(f32) for g in grads]).astype(bf16)
    key_grad, value_grad = both[:HEAD_DIM], both[HEAD_DIM:]
    inner = []
    for k, pair in enumerate(pairs):
        at = pl.ds(spot(head, k), SHARE)
        block = hidden[:, at] + mm(key_grad, w_key[at, :], TT) + mm(value_grad, w_value[at, :], TT)
        inner.append(jnp.sum(pair[:ROWS, :].astype(f32) * gain[:, at] * block, axis=1, keepdims=True))
        if k == 0:
            own[...] = block
        else:
            sends[k - 1][:ROWS, :] = block.astype(bf16)
    row = jnp.transpose(jnp.broadcast_to(tree(inner), (ROWS, ROWS)))[:EXTRA]
    high = row.astype(bf16)
    lower = (row - high.astype(f32)).astype(bf16)
    own_row[:, :ROWS] = high
    own_row[:, ROWS:] = lower
    for send in sends:
        send[ROWS:, :] = jnp.zeros((EXTRA, SHARE), bf16)
        send[ROWS:, :ROWS] = high
        send[ROWS:, ROWS : 2 * ROWS] = lower


def last_kernel(ids, own, own_row, *refs):
    got = refs[: GROUPS - 1]
    x, dy, gain, mean, mean_row, dot_row, input_grad, saliency = refs[GROUPS - 1 :]
    head = ids[1]
    hidden = functools.reduce(lambda a, b: a + b, [g[:ROWS, :].astype(f32) for g in got], own[...])

    def term(ref, at):
        return ref[at : at + EXTRA, :ROWS].astype(f32) + ref[at : at + EXTRA, ROWS : 2 * ROWS].astype(f32)

    total_row = tree([term(own_row, 0)] + [term(g, ROWS) for g in got])[:8]
    root_row = jnp.sqrt(mean_row[...] + EPS)
    inner_row = total_row / (root_row * D)
    sums = dot_row[...] + (total_row - inner_row * (mean_row[...] * D) / root_row) / root_row
    saliency[...] = sums[:1]
    inner = jnp.transpose(jnp.broadcast_to(inner_row[:1], (ROWS, ROWS)))
    inverse = 1.0 / jnp.sqrt(mean[...] + EPS)
    for n in range(SHARE // ROWS):
        at = slice(n * ROWS, (n + 1) * ROWS)
        unit = x[:, at].astype(f32) * inverse
        scaled = hidden[:, at] * gain[:, pl.ds(pl.multiple_of(head * SHARE + n * ROWS, ROWS), ROWS)]
        input_grad[:, at] = (dy[:, at].astype(f32) + (scaled - unit * inner) * inverse).astype(bf16)


def xor_head(a, k):
    return lax.ppermute(a, "head", [(i, i ^ k) for i in range(GROUPS)])


def xor_ctx(a, k):
    return lax.ppermute(a, "ctx", [(i, i ^ k) for i in range(32)])


def touch(arrays):
    return call(touch_kernel, [], arrays, shape((8, ROWS), f32), 16, moved=6 << 20, name="touch")


def turn(a, k):
    return lax.ppermute(a, "ctx", [(i, (i + 4 * k) % 32) for i in range(32)])


def spread(a):
    across = xor_ctx(a, 2)
    return [a, xor_ctx(a, 1), across, xor_ctx(across, 1)]


ORDER = (6, 7, 2, 3, 4, 5, 1)


def local(inputs, out_grad, norm_gain, w_query, w_key, w_value, w_out, record_lengths, block_order):
    ids = jnp.stack([lax.axis_index("ctx"), lax.axis_index("head")]).astype(jnp.int32)
    gain = norm_gain.reshape(1, D)
    pair = jnp.concatenate([inputs, out_grad], axis=0)
    came = {k: xor_head(pair, k) for k in ORDER}
    pairs = [pair] + [came[k] for k in range(1, GROUPS)]
    ready = touch([w_key, w_value, w_query, gain])
    kv, query, mean, mean_row = call(
        norm_kernel,
        [ids],
        [*pairs, gain, w_key, w_value, w_query, ready],
        [
            shape((ROWS, WIDE), bf16),
            shape((ROWS, SHARE), bf16),
            shape((ROWS, ROWS), f32),
            shape((8, ROWS), f32),
        ],
        16,
        flops=2 * ROWS * D * (WIDE + SHARE),
        moved=8 << 20,
        scratch=[pltpu.VMEM((ROWS, D), bf16)],
        name="norm_kvq",
    )
    kvs = [kv] + [turn(kv, k) for k in HOPS[1:]]
    queries = spread(query)
    ready_out = touch([w_out, query])
    out_dir, dot_row = call(
        out_dir_kernel,
        [ids],
        [*pairs, w_out, ready_out],
        [shape((ROWS, SHARE), bf16), shape((8, ROWS), f32)],
        16,
        flops=2 * ROWS * D * SHARE,
        moved=6 << 20,
        name="out_dir",
    )
    dirs = spread(out_dir)
    tall = QUAD * HEADS * ROWS
    powers, mixed, stats = call(
        softmax_kernel,
        [ids, block_order, record_lengths],
        [*queries, *kvs],
        [shape((tall, KEYS), bf16), shape((tall, HEAD_DIM), f32), shape((ROWS, ROWS), f32)],
        24,
        flops=4 * tall * KEYS * HEAD_DIM,
        moved=6 << 20,
        exps=tall * KEYS,
        scratch=[pltpu.VMEM((tall, HEAD_DIM), bf16)] + [pltpu.VMEM((KEYS, HEAD_DIM), bf16)] * 2,
        name="softmax",
    )
    stats = call(
        pack_kernel,
        [],
        [stats, mixed, *dirs],
        shape((ROWS, ROWS), f32),
        16,
        flops=4 * tall * HEAD_DIM,
        moved=3 << 20,
        name="pack",
    )
    parts = [stats, xor_ctx(stats, 1), xor_ctx(stats, 2), xor_ctx(stats, 3)]
    *outs, dq_own, dq_send = call(
        gradient_kernel,
        [],
        [*queries, *dirs, *kvs, powers, *parts],
        [shape((WIDE, HEAD_DIM), bf16)] * RING + [shape((2 * ROWS, SHARE), f32), shape((2 * ROWS, SHARE), bf16)],
        32,
        flops=8 * tall * KEYS * HEAD_DIM,
        moved=6 << 20,
        scratch=[
            pltpu.VMEM((tall, KEYS), bf16),
            pltpu.VMEM((HEAD_DIM, tall), bf16),
            pltpu.VMEM((tall, HEAD_DIM), bf16),
            pltpu.VMEM((HEAD_DIM, tall), bf16),
            pltpu.VMEM((KEYS, HEAD_DIM), bf16),
            pltpu.VMEM((KEYS, HEAD_DIM), bf16),
        ],
        name="gradient",
    )
    grads = [turn(part, -k) if k else part for part, k in zip(outs, HOPS)]
    stay, dq_far = call(
        add_kernel,
        [],
        [dq_own, xor_ctx(dq_send, 1)],
        [shape((ROWS, SHARE), f32), shape((ROWS, SHARE), bf16)],
        16,
        flops=4 * ROWS * SHARE,
        moved=2 << 20,
        name="add",
    )
    hidden = call(
        back_query_kernel,
        [],
        [stay, xor_ctx(dq_far, 2), w_query],
        shape((ROWS, D), f32),
        16,
        flops=2 * ROWS * D * SHARE,
        moved=6 << 20,
        name="back_query",
    )
    own, own_row, *sends = call(
        back_kernel,
        [ids],
        [*grads, *pairs, gain, hidden, w_key, w_value],
        [shape((ROWS, SHARE), f32), shape((EXTRA, WIDE), bf16)]
        + [shape((ROWS + EXTRA, SHARE), bf16)] * (GROUPS - 1),
        24,
        flops=2 * ROWS * D * WIDE,
        moved=7 << 20,
        name="back_kv",
    )
    home = {k: xor_head(sends[k - 1], k) for k in ORDER}
    input_grad, saliency = call(
        last_kernel,
        [ids],
        [own, own_row, *[home[k] for k in range(1, GROUPS)], inputs, out_grad, gain, mean, mean_row, dot_row],
        [shape((ROWS, SHARE), bf16), shape((1, ROWS), f32)],
        16,
        flops=10 * ROWS * SHARE,
        moved=3 << 20,
        name="last",
    )
    return (input_grad, saliency.reshape(ROWS))


def solution(mesh):
    placed = (
        P("ctx", "head"),
        P("ctx", "head"),
        P(),
        P(None, "head"),
        P(None, "head"),
        P(None, "head"),
        P("head", None),
        P(),
        P(),
    )
    return jax.shard_map(
        local, mesh=mesh, in_specs=placed, out_specs=(P("ctx", "head"), P("ctx")), check_vma=False
    )
```

```python
import functools

import jax
import jax.numpy as jnp
from jax import lax
from jax.experimental import pallas as pl
from jax.experimental.pallas import tpu as pltpu
from jax.sharding import PartitionSpec as P

D = 4096
HEAD_DIM = 128
BLOCK = 64
ROWS = 128
SHARE = 512
HEADS = 4
GROUPS = 8
RECORDS = 8
KEYS = 1024
WIDE = 2 * HEAD_DIM
EPS = 1e-05
SCALE = HEAD_DIM ** (-0.5)
LOG2E = 1.4426950408889634
NEG = -1e30
HOPS = (0, 2, 6, 5, 3, 4, 1, 7)
KS = (0, 7, 6, 3, 5, 4, 2, 1)
BACK = (1, 2, 4, 5, 3, 6, 7)
EXTRA = 16
QUAD, RING = 4, 8

f32, bf16 = jnp.float32, jnp.bfloat16
NT = (((1,), (1,)), ((), ()))
NN = (((1,), (0,)), ((), ()))
TT = (((0,), (1,)), ((), ()))


def mm(a, b, dims=NN):
    return lax.dot_general(a, b, dims, preferred_element_type=f32)


def tree(parts):
    while len(parts) > 1:
        parts = [parts[i] + parts[i + 1] for i in range(0, len(parts), 2)]
    return parts[0]


def vmem(n):
    return [pl.BlockSpec(memory_space=pltpu.VMEM)] * n


def smem(n):
    return [pl.BlockSpec(memory_space=pltpu.SMEM)] * n


def call(body, scalars, arrays, outs, mib, flops=0, moved=0, exps=0, scratch=(), name=None):
    return pl.pallas_call(
        body,
        out_shape=outs,
        in_specs=smem(len(scalars)) + vmem(len(arrays)),
        out_specs=jax.tree.map(lambda _: pl.BlockSpec(memory_space=pltpu.VMEM), outs),
        scratch_shapes=list(scratch),
        compiler_params=pltpu.CompilerParams(vmem_limit_bytes=mib << 20),
        cost_estimate=pl.CostEstimate(flops=flops, bytes_accessed=moved, transcendentals=exps),
        name=name,
    )(*scalars, *arrays)


def shape(dims, dtype):
    return jax.ShapeDtypeStruct(dims, dtype)


def spot(head, k):
    return pl.multiple_of(lax.bitwise_xor(head, k) * SHARE, SHARE)


def in_order(ks, refs):
    return [ref for _, ref in sorted(zip(ks, refs), key=lambda pair: pair[0])]


def as_row(column):
    return jnp.transpose(jnp.broadcast_to(column, (ROWS, ROWS)))[:8]


def touch_kernel(*refs):
    refs[-1][...] = jnp.zeros((8, ROWS), f32)


def pair_kernel(x, dy, pair):
    pair[:ROWS, :] = x[...]
    pair[ROWS:, :] = dy[...]


def norm_kernel(ids, *refs):
    xs = [r.at[:ROWS, :] for r in in_order(KS, refs[:GROUPS])]
    gain, w_key, w_value, w_query, _, kv, query, mean, mean_row, normed = refs[GROUPS:]
    head = ids[1]
    squares = []
    for x in xs:
        wide = x[...].astype(f32)
        squares.append(jnp.sum(wide * wide, axis=1, keepdims=True))
    average = tree(squares) * (1.0 / D)
    mean[...] = jnp.broadcast_to(average, (ROWS, ROWS))
    mean_row[...] = as_row(average)
    inverse = 1.0 / jnp.sqrt(average + EPS)
    for k, x in enumerate(xs):
        at = pl.ds(spot(head, k), SHARE)
        normed[:, at] = (x[...].astype(f32) * inverse * gain[:, at]).astype(bf16)
    kv[:, :HEAD_DIM] = mm(normed[...], w_key[...]).astype(bf16)
    kv[:, HEAD_DIM:] = mm(normed[...], w_value[...]).astype(bf16)
    query[...] = mm(normed[...], w_query[...]).astype(bf16)


def out_dir_kernel(ids, *refs):
    pairs, w_out, out_dir, dot_row = in_order(KS, refs[:GROUPS]), refs[GROUPS], refs[-2], refs[-1]
    head = ids[1]
    total = jnp.zeros((ROWS, SHARE), f32)
    parts = []
    for k, pair in enumerate(pairs):
        dy = pair[ROWS:, :]
        total = total + mm(dy, w_out[:, pl.ds(spot(head, k), SHARE)], NT)
        parts.append(jnp.sum(pair[:ROWS, :].astype(f32) * dy.astype(f32), axis=1, keepdims=True))
    out_dir[...] = total.astype(bf16)
    dot_row[...] = as_row(tree(parts))


def group(n):
    return slice(n * ROWS, (n + 1) * ROWS)


def lanes(x, op):
    return functools.reduce(op, [x[:, group(n)] for n in range(x.shape[1] // ROWS)])


def stack(ref, blocks):
    for b, block in enumerate(blocks):
        for h in range(HEADS):
            ref[group(b * HEADS + h), :] = block[:, group(h)]


def softmax_kernel(ids, order, lengths, *refs):
    queries, kvs = refs[:QUAD], refs[QUAD : QUAD + RING]
    powers, mixed, stats, stacked, key, value = refs[QUAD + RING :]
    ctx = ids[0]
    z, place_in_quad = ctx // QUAD, ctx % QUAD
    lane = lax.broadcasted_iota(jnp.int32, (1, ROWS), 1)
    row = lax.broadcasted_iota(jnp.int32, (ROWS, 1), 0)

    def places(owner, i):
        first, second = order[2 * owner] * BLOCK, order[2 * owner + 1] * BLOCK - BLOCK
        return jnp.where(i < BLOCK, first + i, second + i)

    found = []
    for n, (kv, hop) in enumerate(zip(kvs, HOPS)):
        key[group(n), :] = kv[:, :HEAD_DIM]
        value[group(n), :] = kv[:, HEAD_DIM:]
        found.append(places(((z + RING - hop) % RING) * QUAD + place_in_quad, lane))
    place = jnp.concatenate(found, axis=1)
    stack(stacked, queries)
    packed = jnp.zeros((ROWS, ROWS), f32)
    spots = lax.broadcasted_iota(jnp.int32, (ROWS, ROWS), 1)
    for b in range(QUAD):
        mine = places(lax.bitwise_xor(ctx, b), row)
        low = jnp.zeros((ROWS, 1), jnp.int32)
        start = 0
        for r in range(RECORDS):
            low = jnp.where(mine >= start, start, low)
            start = start + lengths[r]
        seen = (place <= mine) & (place >= low)
        scores = mm(stacked[b * SHARE : (b + 1) * SHARE, :], key[...], NT)
        for h in range(HEADS):
            n = b * HEADS + h
            masked = jnp.where(seen, scores[group(h)], NEG)
            shift = jnp.max(lanes(masked, jnp.maximum), axis=1, keepdims=True) * (SCALE * LOG2E)
            power = jnp.exp2(masked * (SCALE * LOG2E) - shift)
            total = jnp.sum(lanes(power, jnp.add), axis=1, keepdims=True)
            half = power.astype(bf16)
            powers[group(n), :] = half
            mixed[group(n), :] = mm(half, value[...])
            for m, column in enumerate((shift, total)):
                packed = jnp.where(spots == QUAD * HEADS * m + n, column, packed)
    stats[...] = packed


def pack_kernel(stats, mixed, *refs):
    dirs, out = refs[:QUAD], refs[QUAD]
    packed = stats[...]
    spots = lax.broadcasted_iota(jnp.int32, (ROWS, ROWS), 1)
    for b in range(QUAD):
        for h in range(HEADS):
            n = b * HEADS + h
            dot = jnp.sum(dirs[b][:, group(h)].astype(f32) * mixed[group(n), :], axis=1, keepdims=True)
            packed = jnp.where(spots == 2 * QUAD * HEADS + n, dot, packed)
    out[...] = packed


def gradient_kernel(*refs):
    queries, dirs, kvs = refs[:QUAD], refs[QUAD : 2 * QUAD], refs[2 * QUAD : 2 * QUAD + RING]
    powers, *rest = refs[2 * QUAD + RING :]
    parts, outs, dq_own, dq_send, (grad, query_t, dirs_n, dirs_t, key, value) = (
        rest[:QUAD],
        rest[QUAD : QUAD + RING],
        rest[QUAD + RING],
        rest[QUAD + RING + 1],
        rest[QUAD + RING + 2 :],
    )
    for n, kv in enumerate(kvs):
        key[group(n), :] = kv[:, :HEAD_DIM]
        value[group(n), :] = kv[:, HEAD_DIM:]
    lane = lax.broadcasted_iota(jnp.int32, (ROWS, ROWS), 1)
    groups = QUAD * HEADS

    def toward(x, n):
        return pltpu.roll(x, (ROWS - n) % ROWS, 1)

    def swap(x, n):
        return jnp.where(lane & n == 0, toward(x, n), toward(x, -n))

    same = []
    for r in range(QUAD):
        x = parts[r][...]
        for bit in (1, 2):
            if r & bit:
                x = swap(x, bit * HEADS)
        same.append(x)
    top = functools.reduce(jnp.maximum, same)
    weights = [jnp.exp2(jnp.where(lane < groups, x - top, 0.0)) for x in same]
    total = functools.reduce(jnp.add, [w * toward(x, groups) for w, x in zip(weights, same)])
    total = jnp.where(lane < groups, total, 1.0)
    dot = functools.reduce(jnp.add, [w * toward(x, 2 * groups) for w, x in zip(weights, same)])
    factors = weights[0] / total
    shifts = dot / total * factors
    shifted = []
    for b in range(QUAD):
        for h in range(HEADS):
            n = b * HEADS + h
            shifted.append(shifts[:, n : n + 1])
            scaled = dirs[b][:, group(h)].astype(f32) * factors[:, n : n + 1]
            dirs_n[group(n), :] = scaled.astype(bf16)
            dirs_t[:, group(n)] = jnp.transpose(scaled).astype(bf16)
            query_t[:, group(n)] = jnp.transpose(queries[b][:, group(h)].astype(f32)).astype(bf16)
    for b in (1, 3, 0, 2):
        rows = slice(b * SHARE, (b + 1) * SHARE)
        slope = mm(dirs_n[rows, :], value[...], NT)
        for h in range(HEADS):
            n = b * HEADS + h
            grad[group(n), :] = (powers[group(n), :].astype(f32) * (slope[group(h)] - shifted[n])).astype(bf16)
        query_grad = mm(grad[rows, :], key[...]) * SCALE
        for h in range(HEADS):
            if b % 2:
                dq_send[group(b // 2), group(h)] = query_grad[group(h)].astype(bf16)
            else:
                dq_own[group(b // 2), group(h)] = query_grad[group(h)]
    for t in range(2):
        at = slice(t * SHARE, (t + 1) * SHARE)
        key_part = mm(query_t[...], grad[:, at]) * SCALE
        value_part = mm(dirs_t[...], powers[:, at])
        for n in range(SHARE // ROWS):
            out = outs[t * (SHARE // ROWS) + n]
            out[:HEAD_DIM, :] = key_part[:, group(n)].astype(bf16)
            out[HEAD_DIM:, :] = value_part[:, group(n)].astype(bf16)


def add_kernel(own, got, stay, send):
    stay[...] = own[:ROWS, :] + got[:ROWS, :].astype(f32)
    send[...] = (own[ROWS:, :] + got[ROWS:, :].astype(f32)).astype(bf16)


def back_query_kernel(stay, got, w_query, hidden):
    query_grad = (stay[...] + got[...].astype(f32)).astype(bf16)
    for k in range(GROUPS):
        at = slice(k * SHARE, (k + 1) * SHARE)
        hidden[:, at] = mm(query_grad, w_query[at, :], NT)


def back_kernel(ids, *refs):
    grads, pairs = refs[:RING], in_order(KS, refs[RING : RING + GROUPS])
    gain, hidden, w_key, w_value, own, own_row, *sends = refs[RING + GROUPS :]
    head = ids[1]
    both = functools.reduce(lambda a, b: a + b, [g[...].astype(f32) for g in grads]).astype(bf16)
    key_grad, value_grad = both[:HEAD_DIM], both[HEAD_DIM:]
    inner = []
    for k, pair in enumerate(pairs):
        at = pl.ds(spot(head, k), SHARE)
        block = hidden[:, at] + mm(key_grad, w_key[at, :], TT) + mm(value_grad, w_value[at, :], TT)
        inner.append(jnp.sum(pair[:ROWS, :].astype(f32) * gain[:, at] * block, axis=1, keepdims=True))
        if k == 0:
            own[...] = block
        else:
            sends[k - 1][:ROWS, :] = block.astype(bf16)
    row = jnp.transpose(jnp.broadcast_to(tree(inner), (ROWS, ROWS)))[:EXTRA]
    high = row.astype(bf16)
    lower = (row - high.astype(f32)).astype(bf16)
    own_row[:, :ROWS] = high
    own_row[:, ROWS:] = lower
    for send in sends:
        send[ROWS:, :] = jnp.zeros((EXTRA, SHARE), bf16)
        send[ROWS:, :ROWS] = high
        send[ROWS:, ROWS : 2 * ROWS] = lower


def last_kernel(ids, own, own_row, *refs):
    got = in_order(BACK, refs[: GROUPS - 1])
    x, dy, gain, mean, mean_row, dot_row, input_grad, saliency = refs[GROUPS - 1 :]
    head = ids[1]
    hidden = functools.reduce(lambda a, b: a + b, [g[:ROWS, :].astype(f32) for g in got], own[...])

    def term(ref, at):
        return ref[at : at + EXTRA, :ROWS].astype(f32) + ref[at : at + EXTRA, ROWS : 2 * ROWS].astype(f32)

    total_row = tree([term(own_row, 0)] + [term(g, ROWS) for g in got])[:8]
    root_row = jnp.sqrt(mean_row[...] + EPS)
    inner_row = total_row / (root_row * D)
    sums = dot_row[...] + (total_row - inner_row * (mean_row[...] * D) / root_row) / root_row
    saliency[...] = sums[:1]
    inner = jnp.transpose(jnp.broadcast_to(inner_row[:1], (ROWS, ROWS)))
    inverse = 1.0 / jnp.sqrt(mean[...] + EPS)
    for n in range(SHARE // ROWS):
        at = slice(n * ROWS, (n + 1) * ROWS)
        unit = x[:, at].astype(f32) * inverse
        scaled = hidden[:, at] * gain[:, pl.ds(pl.multiple_of(head * SHARE + n * ROWS, ROWS), ROWS)]
        input_grad[:, at] = (dy[:, at].astype(f32) + (scaled - unit * inner) * inverse).astype(bf16)


def xor_head(a, k):
    return lax.ppermute(a, "head", [(i, i ^ k) for i in range(GROUPS)])


def xor_ctx(a, k):
    return lax.ppermute(a, "ctx", [(i, i ^ k) for i in range(32)])


def touch(arrays):
    return call(touch_kernel, [], arrays, shape((8, ROWS), f32), 16, moved=6 << 20, name="touch")


def turn(a, k):
    return lax.ppermute(a, "ctx", [(i, (i + 4 * k) % 32) for i in range(32)])


def spread(a):
    across = xor_ctx(a, 2)
    return [a, xor_ctx(a, 1), across, xor_ctx(across, 1)]


def local(inputs, out_grad, norm_gain, w_query, w_key, w_value, w_out, record_lengths, block_order):
    ids = jnp.stack([lax.axis_index("ctx"), lax.axis_index("head")]).astype(jnp.int32)
    gain = norm_gain.reshape(1, D)
    pair = call(pair_kernel, [], [inputs, out_grad], shape((2 * ROWS, SHARE), bf16), 58, moved=1 << 19, name="pair")
    pairs = [xor_head(pair, k) if k else pair for k in KS]
    ready = touch([w_key, w_value, w_query, gain])
    kv, query, mean, mean_row = call(
        norm_kernel,
        [ids],
        [*pairs, gain, w_key, w_value, w_query, ready],
        [
            shape((ROWS, WIDE), bf16),
            shape((ROWS, SHARE), bf16),
            shape((ROWS, ROWS), f32),
            shape((8, ROWS), f32),
        ],
        16,
        flops=2 * ROWS * D * (WIDE + SHARE),
        moved=8 << 20,
        scratch=[pltpu.VMEM((ROWS, D), bf16)],
        name="norm_kvq",
    )
    kvs = [kv] + [turn(kv, k) for k in HOPS[1:]]
    queries = spread(query)
    ready_out = touch([w_out, query, *kvs[3:]])
    out_dir, dot_row = call(
        out_dir_kernel,
        [ids],
        [*pairs, w_out, ready_out],
        [shape((ROWS, SHARE), bf16), shape((8, ROWS), f32)],
        16,
        flops=2 * ROWS * D * SHARE,
        moved=6 << 20,
        name="out_dir",
    )
    dirs = spread(out_dir)
    tall = QUAD * HEADS * ROWS
    powers, mixed, stats = call(
        softmax_kernel,
        [ids, block_order, record_lengths],
        [*queries, *kvs],
        [shape((tall, KEYS), bf16), shape((tall, HEAD_DIM), f32), shape((ROWS, ROWS), f32)],
        24,
        flops=4 * tall * KEYS * HEAD_DIM,
        moved=6 << 20,
        exps=tall * KEYS,
        scratch=[pltpu.VMEM((tall, HEAD_DIM), bf16)] + [pltpu.VMEM((KEYS, HEAD_DIM), bf16)] * 2,
        name="softmax",
    )
    stats = call(
        pack_kernel,
        [],
        [stats, mixed, *dirs],
        shape((ROWS, ROWS), f32),
        16,
        flops=4 * tall * HEAD_DIM,
        moved=3 << 20,
        name="pack",
    )
    parts = [stats, xor_ctx(stats, 1), xor_ctx(stats, 2), xor_ctx(stats, 3)]
    *outs, dq_own, dq_send = call(
        gradient_kernel,
        [],
        [*queries, *dirs, *kvs, powers, *parts],
        [shape((WIDE, HEAD_DIM), bf16)] * RING + [shape((2 * ROWS, SHARE), f32), shape((2 * ROWS, SHARE), bf16)],
        32,
        flops=8 * tall * KEYS * HEAD_DIM,
        moved=6 << 20,
        scratch=[
            pltpu.VMEM((tall, KEYS), bf16),
            pltpu.VMEM((HEAD_DIM, tall), bf16),
            pltpu.VMEM((tall, HEAD_DIM), bf16),
            pltpu.VMEM((HEAD_DIM, tall), bf16),
            pltpu.VMEM((KEYS, HEAD_DIM), bf16),
            pltpu.VMEM((KEYS, HEAD_DIM), bf16),
        ],
        name="gradient",
    )
    grads = [turn(part, -k) if k else part for part, k in zip(outs, HOPS)]
    stay, dq_far = call(
        add_kernel,
        [],
        [dq_own, xor_ctx(dq_send, 1)],
        [shape((ROWS, SHARE), f32), shape((ROWS, SHARE), bf16)],
        16,
        flops=4 * ROWS * SHARE,
        moved=2 << 20,
        name="add",
    )
    hidden = call(
        back_query_kernel,
        [],
        [stay, xor_ctx(dq_far, 2), w_query],
        shape((ROWS, D), f32),
        16,
        flops=2 * ROWS * D * SHARE,
        moved=6 << 20,
        name="back_query",
    )
    own, own_row, *sends = call(
        back_kernel,
        [ids],
        [*grads, *pairs, gain, hidden, w_key, w_value],
        [shape((ROWS, SHARE), f32), shape((EXTRA, WIDE), bf16)]
        + [shape((ROWS + EXTRA, SHARE), bf16)] * (GROUPS - 1),
        24,
        flops=2 * ROWS * D * WIDE,
        moved=7 << 20,
        name="back_kv",
    )
    home = [xor_head(sends[k - 1], k) for k in BACK]
    input_grad, saliency = call(
        last_kernel,
        [ids],
        [own, own_row, *home, inputs, out_grad, gain, mean, mean_row, dot_row],
        [shape((ROWS, SHARE), bf16), shape((1, ROWS), f32)],
        16,
        flops=10 * ROWS * SHARE,
        moved=3 << 20,
        name="last",
    )
    return (input_grad, saliency.reshape(ROWS))


def solution(mesh):
    placed = (
        P("ctx", "head"),
        P("ctx", "head"),
        P(),
        P(None, "head"),
        P(None, "head"),
        P(None, "head"),
        P("head", None),
        P(),
        P(),
    )
    return jax.shard_map(
        local, mesh=mesh, in_specs=placed, out_specs=(P("ctx", "head"), P("ctx")), check_vma=False
    )
```

```python
import functools

import jax
import jax.numpy as jnp
from jax import lax
from jax.experimental import pallas as pl
from jax.experimental.pallas import tpu as pltpu
from jax.sharding import PartitionSpec as P

D = 4096
HEAD_DIM = 128
BLOCK = 64
ROWS = 128
SHARE = 512
HEADS = 4
GROUPS = 8
RECORDS = 8
KEYS = 1024
WIDE = 2 * HEAD_DIM
EPS = 1e-05
SCALE = HEAD_DIM ** (-0.5)
LOG2E = 1.4426950408889634
NEG = -1e30
HOPS = (0, 2, 6, 5, 3, 4, 1, 7)
KS = (0, 7, 6, 3, 5, 4, 2, 1)
BACK = (1, 2, 4, 5, 3, 6, 7)
EXTRA = 16
QUAD, RING = 4, 8

f32, bf16 = jnp.float32, jnp.bfloat16
NT = (((1,), (1,)), ((), ()))
NN = (((1,), (0,)), ((), ()))
TT = (((0,), (1,)), ((), ()))


def mm(a, b, dims=NN):
    return lax.dot_general(a, b, dims, preferred_element_type=f32)


def tree(parts):
    while len(parts) > 1:
        parts = [parts[i] + parts[i + 1] for i in range(0, len(parts), 2)]
    return parts[0]


def vmem(n):
    return [pl.BlockSpec(memory_space=pltpu.VMEM)] * n


def smem(n):
    return [pl.BlockSpec(memory_space=pltpu.SMEM)] * n


def call(body, scalars, arrays, outs, mib, flops=0, moved=0, exps=0, scratch=(), name=None):
    return pl.pallas_call(
        body,
        out_shape=outs,
        in_specs=smem(len(scalars)) + vmem(len(arrays)),
        out_specs=jax.tree.map(lambda _: pl.BlockSpec(memory_space=pltpu.VMEM), outs),
        scratch_shapes=list(scratch),
        compiler_params=pltpu.CompilerParams(vmem_limit_bytes=mib << 20),
        cost_estimate=pl.CostEstimate(flops=flops, bytes_accessed=moved, transcendentals=exps),
        name=name,
    )(*scalars, *arrays)


def shape(dims, dtype):
    return jax.ShapeDtypeStruct(dims, dtype)


def spot(head, k):
    return pl.multiple_of(lax.bitwise_xor(head, k) * SHARE, SHARE)


def in_order(ks, refs):
    return [ref for _, ref in sorted(zip(ks, refs), key=lambda pair: pair[0])]


def as_row(column):
    return jnp.transpose(jnp.broadcast_to(column, (ROWS, ROWS)))[:8]


def touch_kernel(*refs):
    refs[-1][...] = jnp.zeros((8, ROWS), f32)


def hold_kernel(own, other, _, both):
    both[:ROWS, :] = own[...]
    both[ROWS:, :] = other[...]


def norm_kernel(ids, *refs):
    xs = in_order(KS, refs[:GROUPS])
    gain, w_key, w_value, w_query, _, kv, query, mean, mean_row, normed = refs[GROUPS:]
    head = ids[1]
    squares = []
    for x in xs:
        wide = x[...].astype(f32)
        squares.append(jnp.sum(wide * wide, axis=1, keepdims=True))
    average = tree(squares) * (1.0 / D)
    mean[...] = jnp.broadcast_to(average, (ROWS, ROWS))
    mean_row[...] = as_row(average)
    inverse = 1.0 / jnp.sqrt(average + EPS)
    for k, x in enumerate(xs):
        at = pl.ds(spot(head, k), SHARE)
        normed[:, at] = (x[...].astype(f32) * inverse * gain[:, at]).astype(bf16)
    kv[:, :HEAD_DIM] = mm(normed[...], w_key[...]).astype(bf16)
    kv[:, HEAD_DIM:] = mm(normed[...], w_value[...]).astype(bf16)
    query[...] = mm(normed[...], w_query[...]).astype(bf16)


def out_dir_kernel(ids, *refs):
    xs, dys, w_out = in_order(KS, refs[:GROUPS]), refs[GROUPS : GROUPS + 4], refs[GROUPS + 4]
    out_dir, dot_row = refs[-2:]
    head = ids[1]
    total = jnp.zeros((ROWS, SHARE), f32)
    parts = []
    for k, x in enumerate(xs):
        dy = dys[k // 2][(k % 2) * ROWS : (k % 2 + 1) * ROWS, :]
        total = total + mm(dy, w_out[:, pl.ds(spot(head, k), SHARE)], NT)
        parts.append(jnp.sum(x[...].astype(f32) * dy.astype(f32), axis=1, keepdims=True))
    out_dir[...] = total.astype(bf16)
    dot_row[...] = as_row(tree(parts))


def group(n):
    return slice(n * ROWS, (n + 1) * ROWS)


def lanes(x, op):
    return functools.reduce(op, [x[:, group(n)] for n in range(x.shape[1] // ROWS)])


def stack(ref, blocks):
    for b, block in enumerate(blocks):
        for h in range(HEADS):
            ref[group(b * HEADS + h), :] = block[:, group(h)]


def softmax_kernel(ids, order, lengths, *refs):
    queries, kvs = refs[:QUAD], refs[QUAD : QUAD + RING]
    powers, mixed, stats, stacked, key, value = refs[QUAD + RING :]
    ctx = ids[0]
    z, place_in_quad = ctx // QUAD, ctx % QUAD
    lane = lax.broadcasted_iota(jnp.int32, (1, ROWS), 1)
    row = lax.broadcasted_iota(jnp.int32, (ROWS, 1), 0)

    def places(owner, i):
        first, second = order[2 * owner] * BLOCK, order[2 * owner + 1] * BLOCK - BLOCK
        return jnp.where(i < BLOCK, first + i, second + i)

    found = []
    for n, (kv, hop) in enumerate(zip(kvs, HOPS)):
        key[group(n), :] = kv[:, :HEAD_DIM]
        value[group(n), :] = kv[:, HEAD_DIM:]
        found.append(places(((z + RING - hop) % RING) * QUAD + place_in_quad, lane))
    place = jnp.concatenate(found, axis=1)
    stack(stacked, queries)
    packed = jnp.zeros((ROWS, ROWS), f32)
    spots = lax.broadcasted_iota(jnp.int32, (ROWS, ROWS), 1)
    for b in range(QUAD):
        mine = places(lax.bitwise_xor(ctx, b), row)
        low = jnp.zeros((ROWS, 1), jnp.int32)
        start = 0
        for r in range(RECORDS):
            low = jnp.where(mine >= start, start, low)
            start = start + lengths[r]
        seen = (place <= mine) & (place >= low)
        scores = mm(stacked[b * SHARE : (b + 1) * SHARE, :], key[...], NT)
        for h in range(HEADS):
            n = b * HEADS + h
            masked = jnp.where(seen, scores[group(h)], NEG)
            shift = jnp.max(lanes(masked, jnp.maximum), axis=1, keepdims=True) * (SCALE * LOG2E)
            power = jnp.exp2(masked * (SCALE * LOG2E) - shift)
            total = jnp.sum(lanes(power, jnp.add), axis=1, keepdims=True)
            half = power.astype(bf16)
            powers[group(n), :] = half
            mixed[group(n), :] = mm(half, value[...])
            for m, column in enumerate((shift, total)):
                packed = jnp.where(spots == QUAD * HEADS * m + n, column, packed)
    stats[...] = packed


def pack_kernel(stats, mixed, *refs):
    dirs, out = refs[:QUAD], refs[QUAD]
    packed = stats[...]
    spots = lax.broadcasted_iota(jnp.int32, (ROWS, ROWS), 1)
    for b in range(QUAD):
        for h in range(HEADS):
            n = b * HEADS + h
            dot = jnp.sum(dirs[b][:, group(h)].astype(f32) * mixed[group(n), :], axis=1, keepdims=True)
            packed = jnp.where(spots == 2 * QUAD * HEADS + n, dot, packed)
    out[...] = packed


def gradient_kernel(*refs):
    queries, dirs, kvs = refs[:QUAD], refs[QUAD : 2 * QUAD], refs[2 * QUAD : 2 * QUAD + RING]
    powers, *rest = refs[2 * QUAD + RING :]
    parts, outs, dq_own, dq_send, (grad, query_t, dirs_n, dirs_t, key, value) = (
        rest[:QUAD],
        rest[QUAD : QUAD + RING],
        rest[QUAD + RING],
        rest[QUAD + RING + 1],
        rest[QUAD + RING + 2 :],
    )
    for n, kv in enumerate(kvs):
        key[group(n), :] = kv[:, :HEAD_DIM]
        value[group(n), :] = kv[:, HEAD_DIM:]
    lane = lax.broadcasted_iota(jnp.int32, (ROWS, ROWS), 1)
    groups = QUAD * HEADS

    def toward(x, n):
        return pltpu.roll(x, (ROWS - n) % ROWS, 1)

    def swap(x, n):
        return jnp.where(lane & n == 0, toward(x, n), toward(x, -n))

    same = []
    for r in range(QUAD):
        x = parts[r][...]
        for bit in (1, 2):
            if r & bit:
                x = swap(x, bit * HEADS)
        same.append(x)
    top = functools.reduce(jnp.maximum, same)
    weights = [jnp.exp2(jnp.where(lane < groups, x - top, 0.0)) for x in same]
    total = functools.reduce(jnp.add, [w * toward(x, groups) for w, x in zip(weights, same)])
    total = jnp.where(lane < groups, total, 1.0)
    dot = functools.reduce(jnp.add, [w * toward(x, 2 * groups) for w, x in zip(weights, same)])
    factors = weights[0] / total
    shifts = dot / total * factors
    shifted = []
    for b in range(QUAD):
        for h in range(HEADS):
            n = b * HEADS + h
            shifted.append(shifts[:, n : n + 1])
            scaled = dirs[b][:, group(h)].astype(f32) * factors[:, n : n + 1]
            dirs_n[group(n), :] = scaled.astype(bf16)
            dirs_t[:, group(n)] = jnp.transpose(scaled).astype(bf16)
            query_t[:, group(n)] = jnp.transpose(queries[b][:, group(h)].astype(f32)).astype(bf16)
    for b in (1, 3, 0, 2):
        rows = slice(b * SHARE, (b + 1) * SHARE)
        slope = mm(dirs_n[rows, :], value[...], NT)
        for h in range(HEADS):
            n = b * HEADS + h
            grad[group(n), :] = (powers[group(n), :].astype(f32) * (slope[group(h)] - shifted[n])).astype(bf16)
        query_grad = mm(grad[rows, :], key[...]) * SCALE
        for h in range(HEADS):
            if b % 2:
                dq_send[group(b // 2), group(h)] = query_grad[group(h)].astype(bf16)
            else:
                dq_own[group(b // 2), group(h)] = query_grad[group(h)]
    for t in range(2):
        at = slice(t * SHARE, (t + 1) * SHARE)
        key_part = mm(query_t[...], grad[:, at]) * SCALE
        value_part = mm(dirs_t[...], powers[:, at])
        for n in range(SHARE // ROWS):
            out = outs[t * (SHARE // ROWS) + n]
            out[:HEAD_DIM, :] = key_part[:, group(n)].astype(bf16)
            out[HEAD_DIM:, :] = value_part[:, group(n)].astype(bf16)


def add_kernel(own, got, stay, send):
    stay[...] = own[:ROWS, :] + got[:ROWS, :].astype(f32)
    send[...] = (own[ROWS:, :] + got[ROWS:, :].astype(f32)).astype(bf16)


def back_query_kernel(stay, got, w_query, hidden):
    query_grad = (stay[...] + got[...].astype(f32)).astype(bf16)
    for k in range(GROUPS):
        at = slice(k * SHARE, (k + 1) * SHARE)
        hidden[:, at] = mm(query_grad, w_query[at, :], NT)


def back_kernel(ids, *refs):
    grads, xs = refs[:RING], in_order(KS, refs[RING : RING + GROUPS])
    gain, hidden, w_key, w_value, own, own_row, *sends = refs[RING + GROUPS :]
    head = ids[1]
    both = functools.reduce(lambda a, b: a + b, [g[...].astype(f32) for g in grads]).astype(bf16)
    key_grad, value_grad = both[:HEAD_DIM], both[HEAD_DIM:]
    inner = []
    for k, x in enumerate(xs):
        at = pl.ds(spot(head, k), SHARE)
        block = hidden[:, at] + mm(key_grad, w_key[at, :], TT) + mm(value_grad, w_value[at, :], TT)
        inner.append(jnp.sum(x[...].astype(f32) * gain[:, at] * block, axis=1, keepdims=True))
        if k == 0:
            own[...] = block
        else:
            sends[k - 1][:ROWS, :] = block.astype(bf16)
    row = jnp.transpose(jnp.broadcast_to(tree(inner), (ROWS, ROWS)))[:EXTRA]
    high = row.astype(bf16)
    lower = (row - high.astype(f32)).astype(bf16)
    own_row[:, :ROWS] = high
    own_row[:, ROWS:] = lower
    for send in sends:
        send[ROWS:, :] = jnp.zeros((EXTRA, SHARE), bf16)
        send[ROWS:, :ROWS] = high
        send[ROWS:, ROWS : 2 * ROWS] = lower


def last_kernel(ids, own, own_row, *refs):
    got = in_order(BACK, refs[: GROUPS - 1])
    x, dy, gain, mean, mean_row, dot_row, input_grad, saliency = refs[GROUPS - 1 :]
    head = ids[1]
    hidden = functools.reduce(lambda a, b: a + b, [g[:ROWS, :].astype(f32) for g in got], own[...])

    def term(ref, at):
        return ref[at : at + EXTRA, :ROWS].astype(f32) + ref[at : at + EXTRA, ROWS : 2 * ROWS].astype(f32)

    total_row = tree([term(own_row, 0)] + [term(g, ROWS) for g in got])[:8]
    root_row = jnp.sqrt(mean_row[...] + EPS)
    inner_row = total_row / (root_row * D)
    sums = dot_row[...] + (total_row - inner_row * (mean_row[...] * D) / root_row) / root_row
    saliency[...] = sums[:1]
    inner = jnp.transpose(jnp.broadcast_to(inner_row[:1], (ROWS, ROWS)))
    inverse = 1.0 / jnp.sqrt(mean[...] + EPS)
    for n in range(SHARE // ROWS):
        at = slice(n * ROWS, (n + 1) * ROWS)
        unit = x[:, at].astype(f32) * inverse
        scaled = hidden[:, at] * gain[:, pl.ds(pl.multiple_of(head * SHARE + n * ROWS, ROWS), ROWS)]
        input_grad[:, at] = (dy[:, at].astype(f32) + (scaled - unit * inner) * inverse).astype(bf16)


def xor_head(a, k):
    return lax.ppermute(a, "head", [(i, i ^ k) for i in range(GROUPS)])


def xor_ctx(a, k):
    return lax.ppermute(a, "ctx", [(i, i ^ k) for i in range(32)])


def touch(arrays):
    return call(touch_kernel, [], arrays, shape((8, ROWS), f32), 16, moved=6 << 20, name="touch")


def turn(a, k):
    return lax.ppermute(a, "ctx", [(i, (i + 4 * k) % 32) for i in range(32)])


def spread(a):
    across = xor_ctx(a, 2)
    return [a, xor_ctx(a, 1), across, xor_ctx(across, 1)]


def local(inputs, out_grad, norm_gain, w_query, w_key, w_value, w_out, record_lengths, block_order):
    ids = jnp.stack([lax.axis_index("ctx"), lax.axis_index("head")]).astype(jnp.int32)
    gain = norm_gain.reshape(1, D)
    xs = [xor_head(inputs, k) if k else inputs for k in KS]
    ready = touch([w_key, w_value, w_query, gain])
    kv, query, mean, mean_row = call(
        norm_kernel,
        [ids],
        [*xs, gain, w_key, w_value, w_query, ready],
        [
            shape((ROWS, WIDE), bf16),
            shape((ROWS, SHARE), bf16),
            shape((ROWS, ROWS), f32),
            shape((8, ROWS), f32),
        ],
        16,
        flops=2 * ROWS * D * (WIDE + SHARE),
        moved=8 << 20,
        scratch=[pltpu.VMEM((ROWS, D), bf16)],
        name="norm_kvq",
    )
    kvs = [kv] + [turn(kv, k) for k in HOPS[1:]]
    queries = spread(query)
    held = call(
        hold_kernel,
        [],
        [out_grad, xor_head(out_grad, 1), kv],
        shape((2 * ROWS, SHARE), bf16),
        4,
        moved=1 << 19,
        name="hold",
    )
    dys = [held] + [xor_head(held, k) for k in (2, 4, 6)]
    ready_out = touch([w_out, query])
    out_dir, dot_row = call(
        out_dir_kernel,
        [ids],
        [*xs, *dys, w_out, ready_out],
        [shape((ROWS, SHARE), bf16), shape((8, ROWS), f32)],
        16,
        flops=2 * ROWS * D * SHARE,
        moved=6 << 20,
        name="out_dir",
    )
    dirs = spread(out_dir)
    tall = QUAD * HEADS * ROWS
    powers, mixed, stats = call(
        softmax_kernel,
        [ids, block_order, record_lengths],
        [*queries, *kvs],
        [shape((tall, KEYS), bf16), shape((tall, HEAD_DIM), f32), shape((ROWS, ROWS), f32)],
        24,
        flops=4 * tall * KEYS * HEAD_DIM,
        moved=6 << 20,
        exps=tall * KEYS,
        scratch=[pltpu.VMEM((tall, HEAD_DIM), bf16)] + [pltpu.VMEM((KEYS, HEAD_DIM), bf16)] * 2,
        name="softmax",
    )
    stats = call(
        pack_kernel,
        [],
        [stats, mixed, *dirs],
        shape((ROWS, ROWS), f32),
        16,
        flops=4 * tall * HEAD_DIM,
        moved=3 << 20,
        name="pack",
    )
    parts = spread(stats)
    *outs, dq_own, dq_send = call(
        gradient_kernel,
        [],
        [*queries, *dirs, *kvs, powers, *parts],
        [shape((WIDE, HEAD_DIM), bf16)] * RING + [shape((2 * ROWS, SHARE), f32), shape((2 * ROWS, SHARE), bf16)],
        32,
        flops=8 * tall * KEYS * HEAD_DIM,
        moved=6 << 20,
        scratch=[
            pltpu.VMEM((tall, KEYS), bf16),
            pltpu.VMEM((HEAD_DIM, tall), bf16),
            pltpu.VMEM((tall, HEAD_DIM), bf16),
            pltpu.VMEM((HEAD_DIM, tall), bf16),
            pltpu.VMEM((KEYS, HEAD_DIM), bf16),
            pltpu.VMEM((KEYS, HEAD_DIM), bf16),
        ],
        name="gradient",
    )
    grads = [turn(part, -k) if k else part for part, k in zip(outs, HOPS)]
    stay, dq_far = call(
        add_kernel,
        [],
        [dq_own, xor_ctx(dq_send, 1)],
        [shape((ROWS, SHARE), f32), shape((ROWS, SHARE), bf16)],
        16,
        flops=4 * ROWS * SHARE,
        moved=2 << 20,
        name="add",
    )
    hidden = call(
        back_query_kernel,
        [],
        [stay, xor_ctx(dq_far, 2), w_query],
        shape((ROWS, D), f32),
        16,
        flops=2 * ROWS * D * SHARE,
        moved=6 << 20,
        name="back_query",
    )
    own, own_row, *sends = call(
        back_kernel,
        [ids],
        [*grads, *xs, gain, hidden, w_key, w_value],
        [shape((ROWS, SHARE), f32), shape((EXTRA, WIDE), bf16)]
        + [shape((ROWS + EXTRA, SHARE), bf16)] * (GROUPS - 1),
        24,
        flops=2 * ROWS * D * WIDE,
        moved=7 << 20,
        name="back_kv",
    )
    home = [xor_head(sends[k - 1], k) for k in BACK]
    input_grad, saliency = call(
        last_kernel,
        [ids],
        [own, own_row, *home, inputs, out_grad, gain, mean, mean_row, dot_row],
        [shape((ROWS, SHARE), bf16), shape((1, ROWS), f32)],
        16,
        flops=10 * ROWS * SHARE,
        moved=3 << 20,
        name="last",
    )
    return (input_grad, saliency.reshape(ROWS))


def solution(mesh):
    placed = (
        P("ctx", "head"),
        P("ctx", "head"),
        P(),
        P(None, "head"),
        P(None, "head"),
        P(None, "head"),
        P("head", None),
        P(),
        P(),
    )
    return jax.shard_map(
        local, mesh=mesh, in_specs=placed, out_specs=(P("ctx", "head"), P("ctx")), check_vma=False
    )
```

```python
import functools

import jax
import jax.numpy as jnp
from jax import lax
from jax.experimental import pallas as pl
from jax.experimental.pallas import tpu as pltpu
from jax.sharding import PartitionSpec as P

D = 4096
HEAD_DIM = 128
BLOCK = 64
ROWS = 128
SHARE = 512
HEADS = 4
GROUPS = 8
RECORDS = 8
KEYS = 1024
WIDE = 2 * HEAD_DIM
EPS = 1e-05
SCALE = HEAD_DIM ** (-0.5)
LOG2E = 1.4426950408889634
NEG = -1e30
KS = (0, 7, 6, 3, 5, 4, 2, 1)
BACK = (1, 2, 4, 5, 3, 6, 7)
EXTRA = 16
QUAD, RING = 4, 8
SIDE = 3

f32, bf16 = jnp.float32, jnp.bfloat16
NT = (((1,), (1,)), ((), ()))
NN = (((1,), (0,)), ((), ()))
TT = (((0,), (1,)), ((), ()))


def mm(a, b, dims=NN):
    return lax.dot_general(a, b, dims, preferred_element_type=f32)


def tree(parts):
    while len(parts) > 1:
        parts = [parts[i] + parts[i + 1] for i in range(0, len(parts), 2)]
    return parts[0]


def vmem(n):
    return [pl.BlockSpec(memory_space=pltpu.VMEM)] * n


def smem(n):
    return [pl.BlockSpec(memory_space=pltpu.SMEM)] * n


def call(body, scalars, arrays, outs, mib, flops=0, moved=0, exps=0, scratch=(), name=None):
    return pl.pallas_call(
        body,
        out_shape=outs,
        in_specs=smem(len(scalars)) + vmem(len(arrays)),
        out_specs=jax.tree.map(lambda _: pl.BlockSpec(memory_space=pltpu.VMEM), outs),
        scratch_shapes=list(scratch),
        compiler_params=pltpu.CompilerParams(vmem_limit_bytes=mib << 20),
        cost_estimate=pl.CostEstimate(flops=flops, bytes_accessed=moved, transcendentals=exps),
        name=name,
    )(*scalars, *arrays)


def shape(dims, dtype):
    return jax.ShapeDtypeStruct(dims, dtype)


def spot(head, k):
    return pl.multiple_of(lax.bitwise_xor(head, k) * SHARE, SHARE)


def in_order(ks, refs):
    return [ref for _, ref in sorted(zip(ks, refs), key=lambda pair: pair[0])]


def as_row(column):
    return jnp.transpose(jnp.broadcast_to(column, (ROWS, ROWS)))[:8]


def touch_kernel(*refs):
    refs[-1][...] = jnp.zeros((8, ROWS), f32)


def hold_kernel(own, other, *refs):
    both = refs[-1]
    both[:ROWS, :] = own[...]
    both[ROWS:, :] = other[...]


def norm_kernel(ids, *refs):
    xs = in_order(KS, refs[:GROUPS])
    gain, w_key, w_value, _, kv, normed, mean, mean_row = refs[GROUPS:]
    head = ids[1]
    squares = []
    for x in xs:
        wide = x[...].astype(f32)
        squares.append(jnp.sum(wide * wide, axis=1, keepdims=True))
    average = tree(squares) * (1.0 / D)
    mean[...] = jnp.broadcast_to(average, (ROWS, ROWS))
    mean_row[...] = as_row(average)
    inverse = 1.0 / jnp.sqrt(average + EPS)
    for k, x in enumerate(xs):
        at = pl.ds(spot(head, k), SHARE)
        normed[:, at] = (x[...].astype(f32) * inverse * gain[:, at]).astype(bf16)
    kv[:, :HEAD_DIM] = mm(normed[...], w_key[...]).astype(bf16)
    kv[:, HEAD_DIM:] = mm(normed[...], w_value[...]).astype(bf16)


def query_kernel(normed, w_query, query):
    query[...] = mm(normed[...], w_query[...]).astype(bf16)


def out_dir_kernel(ids, *refs):
    xs, dys, w_out = in_order(KS, refs[:GROUPS]), refs[GROUPS : GROUPS + 4], refs[GROUPS + 4]
    out_dir, dot_row = refs[-2:]
    head = ids[1]
    total = jnp.zeros((ROWS, SHARE), f32)
    parts = []
    for k, x in enumerate(xs):
        dy = dys[k // 2][(k % 2) * ROWS : (k % 2 + 1) * ROWS, :]
        total = total + mm(dy, w_out[:, pl.ds(spot(head, k), SHARE)], NT)
        parts.append(jnp.sum(x[...].astype(f32) * dy.astype(f32), axis=1, keepdims=True))
    out_dir[...] = total.astype(bf16)
    dot_row[...] = as_row(tree(parts))


def group(n):
    return slice(n * ROWS, (n + 1) * ROWS)


def lanes(x, op):
    return functools.reduce(op, [x[:, group(n)] for n in range(x.shape[1] // ROWS)])


def stack(ref, blocks):
    for b, block in enumerate(blocks):
        for h in range(HEADS):
            ref[group(b * HEADS + h), :] = block[:, group(h)]


def slot(core):
    return pl.ds(pl.multiple_of(core * ROWS, ROWS), ROWS)


def join_kernel(ids, mine, other, both):
    core = ids[0] % 2
    both[slot(core), :] = mine[...]
    both[slot(1 - core), :] = other[...]


def sort_kernel(ids, *refs):
    core = ids[0] % 2
    for n, ref in enumerate(refs[:SIDE]):
        refs[-1][group(n), :] = ref[slot(1 - core), :]


def softmax_kernel(ids, order, lengths, *refs):
    queries, (kv, across, *near, others) = refs[:QUAD], refs[QUAD : QUAD + SIDE + 3]
    powers, mixed, stats, key, value, stacked = refs[QUAD + SIDE + 3 :]
    ctx = ids[0]
    z, place_in_quad, core = ctx // QUAD, ctx % QUAD, ctx % 2
    lane = lax.broadcasted_iota(jnp.int32, (1, ROWS), 1)
    row = lax.broadcasted_iota(jnp.int32, (ROWS, 1), 0)

    def places(owner, i):
        first, second = order[2 * owner] * BLOCK, order[2 * owner + 1] * BLOCK - BLOCK
        return jnp.where(i < BLOCK, first + i, second + i)

    sign = 1 - 2 * core
    blocks = [(kv[...], 0), (across[...], RING // 2)]
    blocks += [(ref[slot(core), :], sign * (n + 1)) for n, ref in enumerate(near)]
    blocks += [(others[group(n), :], -sign * (n + 1)) for n in range(SIDE)]
    found = []
    for n, (block, hop) in enumerate(blocks):
        key[group(n), :] = block[:, :HEAD_DIM]
        value[group(n), :] = block[:, HEAD_DIM:]
        found.append(places(((z + RING - hop) % RING) * QUAD + place_in_quad, lane))
    place = jnp.concatenate(found, axis=1)
    stack(stacked, queries)
    packed = jnp.zeros((ROWS, ROWS), f32)
    spots = lax.broadcasted_iota(jnp.int32, (ROWS, ROWS), 1)
    for b in range(QUAD):
        mine = places(lax.bitwise_xor(ctx, b), row)
        low = jnp.zeros((ROWS, 1), jnp.int32)
        start = 0
        for r in range(RECORDS):
            low = jnp.where(mine >= start, start, low)
            start = start + lengths[r]
        seen = (place <= mine) & (place >= low)
        scores = mm(stacked[b * SHARE : (b + 1) * SHARE, :], key[...], NT)
        for h in range(HEADS):
            n = b * HEADS + h
            masked = jnp.where(seen, scores[group(h)], NEG)
            shift = jnp.max(lanes(masked, jnp.maximum), axis=1, keepdims=True) * (SCALE * LOG2E)
            power = jnp.exp2(masked * (SCALE * LOG2E) - shift)
            total = jnp.sum(lanes(power, jnp.add), axis=1, keepdims=True)
            half = power.astype(bf16)
            powers[group(n), :] = half
            mixed[group(n), :] = mm(half, value[...])
            for m, column in enumerate((shift, total)):
                packed = jnp.where(spots == QUAD * HEADS * m + n, column, packed)
    stats[...] = packed


def pack_kernel(stats, mixed, *refs):
    dirs, out = refs[:QUAD], refs[QUAD]
    packed = stats[...]
    spots = lax.broadcasted_iota(jnp.int32, (ROWS, ROWS), 1)
    for b in range(QUAD):
        for h in range(HEADS):
            n = b * HEADS + h
            dot = jnp.sum(dirs[b][:, group(h)].astype(f32) * mixed[group(n), :], axis=1, keepdims=True)
            packed = jnp.where(spots == 2 * QUAD * HEADS + n, dot, packed)
    out[...] = packed


def gradient_kernel(*refs):
    queries, dirs, (key, value, powers) = refs[:QUAD], refs[QUAD : 2 * QUAD], refs[2 * QUAD : 2 * QUAD + 3]
    parts = refs[2 * QUAD + 3 : 3 * QUAD + 3]
    own, across, near, others, dq_own, dq_send, grad, query_t, dirs_n, dirs_t = refs[3 * QUAD + 3 :]
    outs = [own, across] + [near.at[n] for n in range(SIDE)] + [others.at[n] for n in range(SIDE)]
    lane = lax.broadcasted_iota(jnp.int32, (ROWS, ROWS), 1)
    groups = QUAD * HEADS

    def toward(x, n):
        return pltpu.roll(x, (ROWS - n) % ROWS, 1)

    def swap(x, n):
        return jnp.where(lane & n == 0, toward(x, n), toward(x, -n))

    same = []
    for r in range(QUAD):
        x = parts[r][...]
        for bit in (1, 2):
            if r & bit:
                x = swap(x, bit * HEADS)
        same.append(x)
    top = functools.reduce(jnp.maximum, same)
    weights = [jnp.exp2(jnp.where(lane < groups, x - top, 0.0)) for x in same]
    total = functools.reduce(jnp.add, [w * toward(x, groups) for w, x in zip(weights, same)])
    total = jnp.where(lane < groups, total, 1.0)
    dot = functools.reduce(jnp.add, [w * toward(x, 2 * groups) for w, x in zip(weights, same)])
    factors = weights[0] / total
    shifts = dot / total * factors
    shifted = []
    for b in range(QUAD):
        for h in range(HEADS):
            n = b * HEADS + h
            shifted.append(shifts[:, n : n + 1])
            scaled = dirs[b][:, group(h)].astype(f32) * factors[:, n : n + 1]
            dirs_n[group(n), :] = scaled.astype(bf16)
            dirs_t[:, group(n)] = jnp.transpose(scaled).astype(bf16)
            query_t[:, group(n)] = jnp.transpose(queries[b][:, group(h)].astype(f32)).astype(bf16)
    for b in (1, 3, 0, 2):
        rows = slice(b * SHARE, (b + 1) * SHARE)
        slope = mm(dirs_n[rows, :], value[...], NT)
        for h in range(HEADS):
            n = b * HEADS + h
            grad[group(n), :] = (powers[group(n), :].astype(f32) * (slope[group(h)] - shifted[n])).astype(bf16)
        query_grad = mm(grad[rows, :], key[...]) * SCALE
        for h in range(HEADS):
            if b % 2:
                dq_send[group(b // 2), group(h)] = query_grad[group(h)].astype(bf16)
            else:
                dq_own[group(b // 2), group(h)] = query_grad[group(h)]
    for t in range(2):
        at = slice(t * SHARE, (t + 1) * SHARE)
        key_part = mm(query_t[...], grad[:, at]) * SCALE
        value_part = mm(dirs_t[...], powers[:, at])
        for n in range(SHARE // ROWS):
            out = outs[t * (SHARE // ROWS) + n]
            out[:HEAD_DIM, :] = key_part[:, group(n)].astype(bf16)
            out[HEAD_DIM:, :] = value_part[:, group(n)].astype(bf16)


def pair_kernel(ids, near, got, *sends):
    core = ids[0] % 2
    for n, send in enumerate(sends):
        send[core] = near[n]
        send[1 - core] = got[n]


def sum_kernel(ids, *refs):
    core = ids[0] % 2
    parts, (own, across, keep, send) = refs[:SIDE], refs[SIDE:]
    mine = functools.reduce(jnp.add, [p[core].astype(f32) for p in parts])
    keep[...] = own[...].astype(f32) + across[...].astype(f32) + mine
    send[...] = functools.reduce(jnp.add, [p[1 - core].astype(f32) for p in parts]).astype(bf16)


def add_kernel(own, got, stay, send):
    stay[...] = own[:ROWS, :] + got[:ROWS, :].astype(f32)
    send[...] = (own[ROWS:, :] + got[ROWS:, :].astype(f32)).astype(bf16)


def back_query_kernel(stay, got, w_query, hidden):
    query_grad = (stay[...] + got[...].astype(f32)).astype(bf16)
    for k in range(GROUPS):
        at = slice(k * SHARE, (k + 1) * SHARE)
        hidden[:, at] = mm(query_grad, w_query[at, :], NT)


def back_kernel(ids, *refs):
    grads, xs = refs[:2], in_order(KS, refs[2 : 2 + GROUPS])
    gain, hidden, w_key, w_value, own, own_row, *sends = refs[2 + GROUPS :]
    head = ids[1]
    both = functools.reduce(lambda a, b: a + b, [g[...].astype(f32) for g in grads]).astype(bf16)
    key_grad, value_grad = both[:HEAD_DIM], both[HEAD_DIM:]
    inner = []
    for k, x in enumerate(xs):
        at = pl.ds(spot(head, k), SHARE)
        block = hidden[:, at] + mm(key_grad, w_key[at, :], TT) + mm(value_grad, w_value[at, :], TT)
        inner.append(jnp.sum(x[...].astype(f32) * gain[:, at] * block, axis=1, keepdims=True))
        if k == 0:
            own[...] = block
        else:
            sends[k - 1][:ROWS, :] = block.astype(bf16)
    row = jnp.transpose(jnp.broadcast_to(tree(inner), (ROWS, ROWS)))[:EXTRA]
    high = row.astype(bf16)
    lower = (row - high.astype(f32)).astype(bf16)
    own_row[:, :ROWS] = high
    own_row[:, ROWS:] = lower
    for send in sends:
        send[ROWS:, :] = jnp.zeros((EXTRA, SHARE), bf16)
        send[ROWS:, :ROWS] = high
        send[ROWS:, ROWS : 2 * ROWS] = lower


def last_kernel(ids, own, own_row, *refs):
    got = in_order(BACK, refs[: GROUPS - 1])
    x, dy, gain, mean, mean_row, dot_row, input_grad, saliency = refs[GROUPS - 1 :]
    head = ids[1]
    hidden = functools.reduce(lambda a, b: a + b, [g[:ROWS, :].astype(f32) for g in got], own[...])

    def term(ref, at):
        return ref[at : at + EXTRA, :ROWS].astype(f32) + ref[at : at + EXTRA, ROWS : 2 * ROWS].astype(f32)

    total_row = tree([term(own_row, 0)] + [term(g, ROWS) for g in got])[:8]
    root_row = jnp.sqrt(mean_row[...] + EPS)
    inner_row = total_row / (root_row * D)
    sums = dot_row[...] + (total_row - inner_row * (mean_row[...] * D) / root_row) / root_row
    saliency[...] = sums[:1]
    inner = jnp.transpose(jnp.broadcast_to(inner_row[:1], (ROWS, ROWS)))
    inverse = 1.0 / jnp.sqrt(mean[...] + EPS)
    for n in range(SHARE // ROWS):
        at = slice(n * ROWS, (n + 1) * ROWS)
        unit = x[:, at].astype(f32) * inverse
        scaled = hidden[:, at] * gain[:, pl.ds(pl.multiple_of(head * SHARE + n * ROWS, ROWS), ROWS)]
        input_grad[:, at] = (dy[:, at].astype(f32) + (scaled - unit * inner) * inverse).astype(bf16)


def xor_head(a, k):
    return lax.ppermute(a, "head", [(i, i ^ k) for i in range(GROUPS)])


def xor_ctx(a, k):
    return lax.ppermute(a, "ctx", [(i, i ^ k) for i in range(32)])


def touch(arrays):
    return call(touch_kernel, [], arrays, shape((8, ROWS), f32), 16, moved=6 << 20, name="touch")


def turn(a, k):
    return lax.ppermute(a, "ctx", [(i, (i + 4 * k) % 32) for i in range(32)])


def apart(a, k):
    return lax.ppermute(a, "ctx", [(i, (i + 4 * k * (1 - 2 * (i % 2))) % 32) for i in range(32)])


def spread(a):
    across = xor_ctx(a, 2)
    return [a, xor_ctx(a, 1), across, xor_ctx(across, 1)]


def local(inputs, out_grad, norm_gain, w_query, w_key, w_value, w_out, record_lengths, block_order):
    ids = jnp.stack([lax.axis_index("ctx"), lax.axis_index("head")]).astype(jnp.int32)
    gain = norm_gain.reshape(1, D)
    xs = [xor_head(inputs, k) if k else inputs for k in KS]
    ready = touch([w_key, w_value, gain])
    kv, normed, mean, mean_row = call(
        norm_kernel,
        [ids],
        [*xs, gain, w_key, w_value, ready],
        [
            shape((ROWS, WIDE), bf16),
            shape((ROWS, D), bf16),
            shape((ROWS, ROWS), f32),
            shape((8, ROWS), f32),
        ],
        16,
        flops=2 * ROWS * D * WIDE,
        moved=5 << 20,
        name="norm_kv",
    )
    query = call(
        query_kernel,
        [],
        [normed, w_query],
        shape((ROWS, SHARE), bf16),
        16,
        flops=2 * ROWS * D * SHARE,
        moved=5 << 20,
        name="query",
    )
    both = call(join_kernel, [ids], [kv, xor_ctx(kv, 1)], shape((2 * ROWS, WIDE), bf16), 4, moved=1 << 18, name="join")
    near = [apart(both, n) for n in range(1, SIDE + 1)]
    kvs = [kv, turn(kv, RING // 2), *near]
    given = call(sort_kernel, [ids], [*near, kvs[1]], shape((SIDE * ROWS, WIDE), bf16), 4, moved=1 << 19, name="sort")
    kvs.append(xor_ctx(given, 1))
    queries = spread(query)
    held = call(
        hold_kernel,
        [],
        [out_grad, xor_head(out_grad, 1), kv],
        shape((2 * ROWS, SHARE), bf16),
        4,
        moved=1 << 19,
        name="hold",
    )
    dys = [held] + [xor_head(held, k) for k in (2, 4, 6)]
    ready_out = touch([w_out, normed])
    out_dir, dot_row = call(
        out_dir_kernel,
        [ids],
        [*xs, *dys, w_out, ready_out],
        [shape((ROWS, SHARE), bf16), shape((8, ROWS), f32)],
        16,
        flops=2 * ROWS * D * SHARE,
        moved=6 << 20,
        name="out_dir",
    )
    dirs = spread(out_dir)
    tall = QUAD * HEADS * ROWS
    powers, mixed, stats, key, value = call(
        softmax_kernel,
        [ids, block_order, record_lengths],
        [*queries, *kvs],
        [
            shape((tall, KEYS), bf16),
            shape((tall, HEAD_DIM), f32),
            shape((ROWS, ROWS), f32),
            shape((KEYS, HEAD_DIM), bf16),
            shape((KEYS, HEAD_DIM), bf16),
        ],
        24,
        flops=4 * tall * KEYS * HEAD_DIM,
        moved=6 << 20,
        exps=tall * KEYS,
        scratch=[pltpu.VMEM((tall, HEAD_DIM), bf16)],
        name="softmax",
    )
    stats = call(
        pack_kernel,
        [],
        [stats, mixed, *dirs],
        shape((ROWS, ROWS), f32),
        16,
        flops=4 * tall * HEAD_DIM,
        moved=3 << 20,
        name="pack",
    )
    parts = spread(stats)
    part = shape((WIDE, HEAD_DIM), bf16)
    side = shape((SIDE, WIDE, HEAD_DIM), bf16)
    own, across, near, others, dq_own, dq_send = call(
        gradient_kernel,
        [],
        [*queries, *dirs, key, value, powers, *parts],
        [part, part, side, side, shape((2 * ROWS, SHARE), f32), shape((2 * ROWS, SHARE), bf16)],
        32,
        flops=8 * tall * KEYS * HEAD_DIM,
        moved=6 << 20,
        scratch=[
            pltpu.VMEM((tall, KEYS), bf16),
            pltpu.VMEM((HEAD_DIM, tall), bf16),
            pltpu.VMEM((tall, HEAD_DIM), bf16),
            pltpu.VMEM((HEAD_DIM, tall), bf16),
        ],
        name="gradient",
    )
    sends = call(
        pair_kernel,
        [ids],
        [near, xor_ctx(others, 1)],
        [shape((2, WIDE, HEAD_DIM), bf16)] * SIDE,
        8,
        moved=1 << 20,
        name="pair",
    )
    keep, give = call(
        sum_kernel,
        [ids],
        [*[apart(a, -n) for n, a in enumerate(sends, 1)], own, turn(across, RING // 2)],
        [shape((WIDE, HEAD_DIM), f32), part],
        8,
        moved=1 << 20,
        name="sum",
    )
    grads = [keep, xor_ctx(give, 1)]
    stay, dq_far = call(
        add_kernel,
        [],
        [dq_own, xor_ctx(dq_send, 1)],
        [shape((ROWS, SHARE), f32), shape((ROWS, SHARE), bf16)],
        16,
        flops=4 * ROWS * SHARE,
        moved=2 << 20,
        name="add",
    )
    hidden = call(
        back_query_kernel,
        [],
        [stay, xor_ctx(dq_far, 2), w_query],
        shape((ROWS, D), f32),
        16,
        flops=2 * ROWS * D * SHARE,
        moved=6 << 20,
        name="back_query",
    )
    own, own_row, *sends = call(
        back_kernel,
        [ids],
        [*grads, *xs, gain, hidden, w_key, w_value],
        [shape((ROWS, SHARE), f32), shape((EXTRA, WIDE), bf16)]
        + [shape((ROWS + EXTRA, SHARE), bf16)] * (GROUPS - 1),
        24,
        flops=2 * ROWS * D * WIDE,
        moved=7 << 20,
        name="back_kv",
    )
    home = [xor_head(sends[k - 1], k) for k in BACK]
    input_grad, saliency = call(
        last_kernel,
        [ids],
        [own, own_row, *home, inputs, out_grad, gain, mean, mean_row, dot_row],
        [shape((ROWS, SHARE), bf16), shape((1, ROWS), f32)],
        16,
        flops=10 * ROWS * SHARE,
        moved=3 << 20,
        name="last",
    )
    return (input_grad, saliency.reshape(ROWS))


def solution(mesh):
    placed = (
        P("ctx", "head"),
        P("ctx", "head"),
        P(),
        P(None, "head"),
        P(None, "head"),
        P(None, "head"),
        P("head", None),
        P(),
        P(),
    )
    return jax.shard_map(
        local, mesh=mesh, in_specs=placed, out_specs=(P("ctx", "head"), P("ctx")), check_vma=False
    )
```

```python
import functools

import jax
import jax.numpy as jnp
from jax import lax
from jax.experimental import pallas as pl
from jax.experimental.pallas import tpu as pltpu
from jax.sharding import PartitionSpec as P

D = 4096
HEAD_DIM = 128
BLOCK = 64
ROWS = 128
SHARE = 512
HEADS = 4
GROUPS = 8
RECORDS = 8
KEYS = 1024
WIDE = 2 * HEAD_DIM
EPS = 1e-05
SCALE = HEAD_DIM ** (-0.5)
LOG2E = 1.4426950408889634
NEG = -1e30
KS = (0, 7, 6, 3, 5, 4, 2, 1)
BACK = (1, 2, 4, 5, 3, 6, 7)
EXTRA = 16
QUAD, RING = 4, 8
SIDE = 3

f32, bf16 = jnp.float32, jnp.bfloat16
NT = (((1,), (1,)), ((), ()))
NN = (((1,), (0,)), ((), ()))
TT = (((0,), (1,)), ((), ()))


def mm(a, b, dims=NN):
    return lax.dot_general(a, b, dims, preferred_element_type=f32)


def tree(parts):
    while len(parts) > 1:
        parts = [parts[i] + parts[i + 1] for i in range(0, len(parts), 2)]
    return parts[0]


def vmem(n):
    return [pl.BlockSpec(memory_space=pltpu.VMEM)] * n


def smem(n):
    return [pl.BlockSpec(memory_space=pltpu.SMEM)] * n


def call(body, scalars, arrays, outs, mib, flops=0, moved=0, exps=0, scratch=(), name=None):
    return pl.pallas_call(
        body,
        out_shape=outs,
        in_specs=smem(len(scalars)) + vmem(len(arrays)),
        out_specs=jax.tree.map(lambda _: pl.BlockSpec(memory_space=pltpu.VMEM), outs),
        scratch_shapes=list(scratch),
        compiler_params=pltpu.CompilerParams(vmem_limit_bytes=mib << 20),
        cost_estimate=pl.CostEstimate(flops=flops, bytes_accessed=moved, transcendentals=exps),
        name=name,
    )(*scalars, *arrays)


def shape(dims, dtype):
    return jax.ShapeDtypeStruct(dims, dtype)


def spot(head, k):
    return pl.multiple_of(lax.bitwise_xor(head, k) * SHARE, SHARE)


def in_order(ks, refs):
    return [ref for _, ref in sorted(zip(ks, refs), key=lambda pair: pair[0])]


def as_row(column):
    return jnp.transpose(jnp.broadcast_to(column, (ROWS, ROWS)))[:8]


def touch_kernel(*refs):
    refs[-1][...] = jnp.zeros((8, ROWS), f32)


def hold_kernel(own, other, *refs):
    both = refs[-1]
    both[:ROWS, :] = own[...]
    both[ROWS:, :] = other[...]


def norm_kernel(ids, *refs):
    xs = in_order(KS, refs[:GROUPS])
    gain, w_key, w_value, _, kv, normed, mean, mean_row = refs[GROUPS:]
    head = ids[1]
    squares = []
    for x in xs:
        wide = x[...].astype(f32)
        squares.append(jnp.sum(wide * wide, axis=1, keepdims=True))
    average = tree(squares) * (1.0 / D)
    mean[...] = jnp.broadcast_to(average, (ROWS, ROWS))
    mean_row[...] = as_row(average)
    inverse = 1.0 / jnp.sqrt(average + EPS)
    for k, x in enumerate(xs):
        at = pl.ds(spot(head, k), SHARE)
        normed[:, at] = (x[...].astype(f32) * inverse * gain[:, at]).astype(bf16)
    kv[:, :HEAD_DIM] = mm(normed[...], w_key[...]).astype(bf16)
    kv[:, HEAD_DIM:] = mm(normed[...], w_value[...]).astype(bf16)


def project_kernel(ids, *refs):
    xs, dys, (w_out, normed, w_query) = in_order(KS, refs[:GROUPS]), refs[GROUPS : GROUPS + 4], refs[GROUPS + 4 : GROUPS + 7]
    both, dot_row = refs[-2:]
    head = ids[1]
    total = jnp.zeros((ROWS, SHARE), f32)
    parts = []
    for k, x in enumerate(xs):
        dy = dys[k // 2][(k % 2) * ROWS : (k % 2 + 1) * ROWS, :]
        total = total + mm(dy, w_out[:, pl.ds(spot(head, k), SHARE)], NT)
        parts.append(jnp.sum(x[...].astype(f32) * dy.astype(f32), axis=1, keepdims=True))
    both[:ROWS, :] = mm(normed[...], w_query[...]).astype(bf16)
    both[ROWS:, :] = total.astype(bf16)
    dot_row[...] = as_row(tree(parts))


def group(n):
    return slice(n * ROWS, (n + 1) * ROWS)


def lanes(x, op):
    return functools.reduce(op, [x[:, group(n)] for n in range(x.shape[1] // ROWS)])


def stack(ref, blocks):
    for b, block in enumerate(blocks):
        for h in range(HEADS):
            ref[group(b * HEADS + h), :] = block[:, group(h)]


def slot(core):
    return pl.ds(pl.multiple_of(core * ROWS, ROWS), ROWS)


def join_kernel(ids, mine, other, both):
    core = ids[0] % 2
    both[slot(core), :] = mine[...]
    both[slot(1 - core), :] = other[...]


def sort_kernel(ids, *refs):
    core = ids[0] % 2
    for n, ref in enumerate(refs[:SIDE]):
        refs[-1][group(n), :] = ref[slot(1 - core), :]


def softmax_kernel(ids, order, lengths, *refs):
    projections, (kv, across, *near, others) = refs[:QUAD], refs[QUAD : QUAD + SIDE + 3]
    powers, stats, key, value, stacked = refs[QUAD + SIDE + 3 :]
    ctx = ids[0]
    z, place_in_quad, core = ctx // QUAD, ctx % QUAD, ctx % 2
    lane = lax.broadcasted_iota(jnp.int32, (1, ROWS), 1)
    row = lax.broadcasted_iota(jnp.int32, (ROWS, 1), 0)

    def places(owner, i):
        first, second = order[2 * owner] * BLOCK, order[2 * owner + 1] * BLOCK - BLOCK
        return jnp.where(i < BLOCK, first + i, second + i)

    sign = 1 - 2 * core
    blocks = [(kv[...], 0), (across[...], RING // 2)]
    blocks += [(ref[slot(core), :], sign * (n + 1)) for n, ref in enumerate(near)]
    blocks += [(others[group(n), :], -sign * (n + 1)) for n in range(SIDE)]
    found = []
    for n, (block, hop) in enumerate(blocks):
        key[group(n), :] = block[:, :HEAD_DIM]
        value[group(n), :] = block[:, HEAD_DIM:]
        found.append(places(((z + RING - hop) % RING) * QUAD + place_in_quad, lane))
    place = jnp.concatenate(found, axis=1)
    stack(stacked, [p.at[:ROWS, :] for p in projections])
    packed = jnp.zeros((ROWS, ROWS), f32)
    spots = lax.broadcasted_iota(jnp.int32, (ROWS, ROWS), 1)
    for b in range(QUAD):
        mine = places(lax.bitwise_xor(ctx, b), row)
        low = jnp.zeros((ROWS, 1), jnp.int32)
        start = 0
        for r in range(RECORDS):
            low = jnp.where(mine >= start, start, low)
            start = start + lengths[r]
        seen = (place <= mine) & (place >= low)
        scores = mm(stacked[b * SHARE : (b + 1) * SHARE, :], key[...], NT)
        for h in range(HEADS):
            n = b * HEADS + h
            masked = jnp.where(seen, scores[group(h)], NEG)
            shift = jnp.max(lanes(masked, jnp.maximum), axis=1, keepdims=True) * (SCALE * LOG2E)
            power = jnp.exp2(masked * (SCALE * LOG2E) - shift)
            total = jnp.sum(lanes(power, jnp.add), axis=1, keepdims=True)
            half = power.astype(bf16)
            powers[group(n), :] = half
            mixed = mm(half, value[...])
            dot = jnp.sum(projections[b][ROWS:, group(h)].astype(f32) * mixed, axis=1, keepdims=True)
            for m, column in enumerate((shift, total, dot)):
                packed = jnp.where(spots == QUAD * HEADS * m + n, column, packed)
    stats[...] = packed


def gradient_kernel(*refs):
    projections, (key, value, powers), parts = refs[:QUAD], refs[QUAD : QUAD + 3], refs[QUAD + 3 : 2 * QUAD + 3]
    queries, dirs = [p.at[:ROWS, :] for p in projections], [p.at[ROWS:, :] for p in projections]
    own, across, near, others, dq_own, dq_send, grad, query_t, dirs_n, dirs_t = refs[2 * QUAD + 3 :]
    outs = [own, across] + [near.at[n] for n in range(SIDE)] + [others.at[n] for n in range(SIDE)]
    lane = lax.broadcasted_iota(jnp.int32, (ROWS, ROWS), 1)
    groups = QUAD * HEADS

    def toward(x, n):
        return pltpu.roll(x, (ROWS - n) % ROWS, 1)

    def swap(x, n):
        return jnp.where(lane & n == 0, toward(x, n), toward(x, -n))

    same = []
    for r in range(QUAD):
        x = parts[r][...]
        for bit in (1, 2):
            if r & bit:
                x = swap(x, bit * HEADS)
        same.append(x)
    top = functools.reduce(jnp.maximum, same)
    weights = [jnp.exp2(jnp.where(lane < groups, x - top, 0.0)) for x in same]
    total = functools.reduce(jnp.add, [w * toward(x, groups) for w, x in zip(weights, same)])
    total = jnp.where(lane < groups, total, 1.0)
    dot = functools.reduce(jnp.add, [w * toward(x, 2 * groups) for w, x in zip(weights, same)])
    factors = weights[0] / total
    shifts = dot / total * factors
    shifted = []
    for b in range(QUAD):
        for h in range(HEADS):
            n = b * HEADS + h
            shifted.append(shifts[:, n : n + 1])
            scaled = dirs[b][:, group(h)].astype(f32) * factors[:, n : n + 1]
            dirs_n[group(n), :] = scaled.astype(bf16)
            dirs_t[:, group(n)] = jnp.transpose(scaled).astype(bf16)
            query_t[:, group(n)] = jnp.transpose(queries[b][:, group(h)].astype(f32)).astype(bf16)
    for b in (1, 3, 0, 2):
        rows = slice(b * SHARE, (b + 1) * SHARE)
        slope = mm(dirs_n[rows, :], value[...], NT)
        for h in range(HEADS):
            n = b * HEADS + h
            grad[group(n), :] = (powers[group(n), :].astype(f32) * (slope[group(h)] - shifted[n])).astype(bf16)
        query_grad = mm(grad[rows, :], key[...]) * SCALE
        for h in range(HEADS):
            if b % 2:
                dq_send[group(b // 2), group(h)] = query_grad[group(h)].astype(bf16)
            else:
                dq_own[group(b // 2), group(h)] = query_grad[group(h)]
    for t in range(2):
        at = slice(t * SHARE, (t + 1) * SHARE)
        key_part = mm(query_t[...], grad[:, at]) * SCALE
        value_part = mm(dirs_t[...], powers[:, at])
        for n in range(SHARE // ROWS):
            out = outs[t * (SHARE // ROWS) + n]
            out[:HEAD_DIM, :] = key_part[:, group(n)].astype(bf16)
            out[HEAD_DIM:, :] = value_part[:, group(n)].astype(bf16)


def pair_kernel(ids, near, got, *sends):
    core = ids[0] % 2
    for n, send in enumerate(sends):
        send[core] = near[n]
        send[1 - core] = got[n]


def sum_kernel(ids, *refs):
    core = ids[0] % 2
    parts, (own, across, keep, send) = refs[:SIDE], refs[SIDE:]
    mine = functools.reduce(jnp.add, [p[core].astype(f32) for p in parts])
    keep[...] = own[...].astype(f32) + across[...].astype(f32) + mine
    send[...] = functools.reduce(jnp.add, [p[1 - core].astype(f32) for p in parts]).astype(bf16)


def add_kernel(own, got, stay, send):
    stay[...] = own[:ROWS, :] + got[:ROWS, :].astype(f32)
    send[...] = (own[ROWS:, :] + got[ROWS:, :].astype(f32)).astype(bf16)


def back_query_kernel(stay, got, w_query, hidden):
    query_grad = (stay[...] + got[...].astype(f32)).astype(bf16)
    for k in range(GROUPS):
        at = slice(k * SHARE, (k + 1) * SHARE)
        hidden[:, at] = mm(query_grad, w_query[at, :], NT)


def back_kernel(ids, *refs):
    grads, xs = refs[:2], in_order(KS, refs[2 : 2 + GROUPS])
    gain, hidden, w_key, w_value, own, own_row, *sends = refs[2 + GROUPS :]
    head = ids[1]
    both = functools.reduce(lambda a, b: a + b, [g[...].astype(f32) for g in grads]).astype(bf16)
    key_grad, value_grad = both[:HEAD_DIM], both[HEAD_DIM:]
    inner = []
    for k, x in enumerate(xs):
        at = pl.ds(spot(head, k), SHARE)
        block = hidden[:, at] + mm(key_grad, w_key[at, :], TT) + mm(value_grad, w_value[at, :], TT)
        inner.append(jnp.sum(x[...].astype(f32) * gain[:, at] * block, axis=1, keepdims=True))
        if k == 0:
            own[...] = block
        else:
            sends[k - 1][:ROWS, :] = block.astype(bf16)
    row = jnp.transpose(jnp.broadcast_to(tree(inner), (ROWS, ROWS)))[:EXTRA]
    high = row.astype(bf16)
    lower = (row - high.astype(f32)).astype(bf16)
    own_row[:, :ROWS] = high
    own_row[:, ROWS:] = lower
    for send in sends:
        send[ROWS:, :] = jnp.zeros((EXTRA, SHARE), bf16)
        send[ROWS:, :ROWS] = high
        send[ROWS:, ROWS : 2 * ROWS] = lower


def last_kernel(ids, own, own_row, *refs):
    got = in_order(BACK, refs[: GROUPS - 1])
    x, dy, gain, mean, mean_row, dot_row, input_grad, saliency = refs[GROUPS - 1 :]
    head = ids[1]
    hidden = functools.reduce(lambda a, b: a + b, [g[:ROWS, :].astype(f32) for g in got], own[...])

    def term(ref, at):
        return ref[at : at + EXTRA, :ROWS].astype(f32) + ref[at : at + EXTRA, ROWS : 2 * ROWS].astype(f32)

    total_row = tree([term(own_row, 0)] + [term(g, ROWS) for g in got])[:8]
    root_row = jnp.sqrt(mean_row[...] + EPS)
    inner_row = total_row / (root_row * D)
    sums = dot_row[...] + (total_row - inner_row * (mean_row[...] * D) / root_row) / root_row
    saliency[...] = sums[:1]
    inner = jnp.transpose(jnp.broadcast_to(inner_row[:1], (ROWS, ROWS)))
    inverse = 1.0 / jnp.sqrt(mean[...] + EPS)
    for n in range(SHARE // ROWS):
        at = slice(n * ROWS, (n + 1) * ROWS)
        unit = x[:, at].astype(f32) * inverse
        scaled = hidden[:, at] * gain[:, pl.ds(pl.multiple_of(head * SHARE + n * ROWS, ROWS), ROWS)]
        input_grad[:, at] = (dy[:, at].astype(f32) + (scaled - unit * inner) * inverse).astype(bf16)


def xor_head(a, k):
    return lax.ppermute(a, "head", [(i, i ^ k) for i in range(GROUPS)])


def xor_ctx(a, k):
    return lax.ppermute(a, "ctx", [(i, i ^ k) for i in range(32)])


def touch(arrays):
    return call(touch_kernel, [], arrays, shape((8, ROWS), f32), 16, moved=6 << 20, name="touch")


def turn(a, k):
    return lax.ppermute(a, "ctx", [(i, (i + 4 * k) % 32) for i in range(32)])


def apart(a, k):
    return lax.ppermute(a, "ctx", [(i, (i + 4 * k * (1 - 2 * (i % 2))) % 32) for i in range(32)])


def spread(a):
    across = xor_ctx(a, 2)
    return [a, xor_ctx(a, 1), across, xor_ctx(across, 1)]


def local(inputs, out_grad, norm_gain, w_query, w_key, w_value, w_out, record_lengths, block_order):
    ids = jnp.stack([lax.axis_index("ctx"), lax.axis_index("head")]).astype(jnp.int32)
    gain = norm_gain.reshape(1, D)
    xs = [xor_head(inputs, k) if k else inputs for k in KS]
    ready = touch([w_key, w_value, gain])
    kv, normed, mean, mean_row = call(
        norm_kernel,
        [ids],
        [*xs, gain, w_key, w_value, ready],
        [
            shape((ROWS, WIDE), bf16),
            shape((ROWS, D), bf16),
            shape((ROWS, ROWS), f32),
            shape((8, ROWS), f32),
        ],
        16,
        flops=2 * ROWS * D * WIDE,
        moved=5 << 20,
        name="norm_kv",
    )
    both = call(join_kernel, [ids], [kv, xor_ctx(kv, 1)], shape((2 * ROWS, WIDE), bf16), 4, moved=1 << 18, name="join")
    near = [apart(both, n) for n in range(1, SIDE + 1)]
    kvs = [kv, turn(kv, RING // 2), *near]
    given = call(sort_kernel, [ids], [*near, kvs[1]], shape((SIDE * ROWS, WIDE), bf16), 4, moved=1 << 19, name="sort")
    kvs.append(xor_ctx(given, 1))
    held = call(
        hold_kernel,
        [],
        [out_grad, xor_head(out_grad, 1), kv],
        shape((2 * ROWS, SHARE), bf16),
        4,
        moved=1 << 19,
        name="hold",
    )
    dys = [held] + [xor_head(held, k) for k in (2, 4, 6)]
    ready_out = touch([w_out, w_query, normed])
    projected, dot_row = call(
        project_kernel,
        [ids],
        [*xs, *dys, w_out, normed, w_query, ready_out, kvs[1], near[2]],
        [shape((2 * ROWS, SHARE), bf16), shape((8, ROWS), f32)],
        24,
        flops=4 * ROWS * D * SHARE,
        moved=10 << 20,
        name="project",
    )
    projections = spread(projected)
    tall = QUAD * HEADS * ROWS
    powers, stats, key, value = call(
        softmax_kernel,
        [ids, block_order, record_lengths],
        [*projections, *kvs],
        [
            shape((tall, KEYS), bf16),
            shape((ROWS, ROWS), f32),
            shape((KEYS, HEAD_DIM), bf16),
            shape((KEYS, HEAD_DIM), bf16),
        ],
        24,
        flops=4 * tall * KEYS * HEAD_DIM,
        moved=6 << 20,
        exps=tall * KEYS,
        scratch=[pltpu.VMEM((tall, HEAD_DIM), bf16)],
        name="softmax",
    )
    parts = spread(stats)
    part = shape((WIDE, HEAD_DIM), bf16)
    side = shape((SIDE, WIDE, HEAD_DIM), bf16)
    own, across, near, others, dq_own, dq_send = call(
        gradient_kernel,
        [],
        [*projections, key, value, powers, *parts],
        [part, part, side, side, shape((2 * ROWS, SHARE), f32), shape((2 * ROWS, SHARE), bf16)],
        32,
        flops=8 * tall * KEYS * HEAD_DIM,
        moved=6 << 20,
        scratch=[
            pltpu.VMEM((tall, KEYS), bf16),
            pltpu.VMEM((HEAD_DIM, tall), bf16),
            pltpu.VMEM((tall, HEAD_DIM), bf16),
            pltpu.VMEM((HEAD_DIM, tall), bf16),
        ],
        name="gradient",
    )
    sends = call(
        pair_kernel,
        [ids],
        [near, xor_ctx(others, 1)],
        [shape((2, WIDE, HEAD_DIM), bf16)] * SIDE,
        8,
        moved=1 << 20,
        name="pair",
    )
    keep, give = call(
        sum_kernel,
        [ids],
        [*[apart(a, -n) for n, a in enumerate(sends, 1)], own, turn(across, RING // 2)],
        [shape((WIDE, HEAD_DIM), f32), part],
        8,
        moved=1 << 20,
        name="sum",
    )
    grads = [keep, xor_ctx(give, 1)]
    stay, dq_far = call(
        add_kernel,
        [],
        [dq_own, xor_ctx(dq_send, 1)],
        [shape((ROWS, SHARE), f32), shape((ROWS, SHARE), bf16)],
        16,
        flops=4 * ROWS * SHARE,
        moved=2 << 20,
        name="add",
    )
    hidden = call(
        back_query_kernel,
        [],
        [stay, xor_ctx(dq_far, 2), w_query],
        shape((ROWS, D), f32),
        16,
        flops=2 * ROWS * D * SHARE,
        moved=6 << 20,
        name="back_query",
    )
    own, own_row, *sends = call(
        back_kernel,
        [ids],
        [*grads, *xs, gain, hidden, w_key, w_value],
        [shape((ROWS, SHARE), f32), shape((EXTRA, WIDE), bf16)]
        + [shape((ROWS + EXTRA, SHARE), bf16)] * (GROUPS - 1),
        24,
        flops=2 * ROWS * D * WIDE,
        moved=7 << 20,
        name="back_kv",
    )
    home = [xor_head(sends[k - 1], k) for k in BACK]
    input_grad, saliency = call(
        last_kernel,
        [ids],
        [own, own_row, *home, inputs, out_grad, gain, mean, mean_row, dot_row],
        [shape((ROWS, SHARE), bf16), shape((1, ROWS), f32)],
        16,
        flops=10 * ROWS * SHARE,
        moved=3 << 20,
        name="last",
    )
    return (input_grad, saliency.reshape(ROWS))


def solution(mesh):
    placed = (
        P("ctx", "head"),
        P("ctx", "head"),
        P(),
        P(None, "head"),
        P(None, "head"),
        P(None, "head"),
        P("head", None),
        P(),
        P(),
    )
    return jax.shard_map(
        local, mesh=mesh, in_specs=placed, out_specs=(P("ctx", "head"), P("ctx")), check_vma=False
    )
```

```python
import functools

import jax
import jax.numpy as jnp
from jax import lax
from jax.experimental import pallas as pl
from jax.experimental.pallas import tpu as pltpu
from jax.sharding import PartitionSpec as P

D = 4096
HEAD_DIM = 128
BLOCK = 64
ROWS = 128
SHARE = 512
HEADS = 4
GROUPS = 8
RECORDS = 8
KEYS = 1024
WIDE = 2 * HEAD_DIM
EPS = 1e-05
SCALE = HEAD_DIM ** (-0.5)
LOG2E = 1.4426950408889634
NEG = -1e30
KS = (0, 7, 6, 3, 5, 4, 2, 1)
BACK = (1, 2, 4, 5, 3, 6, 7)
EXTRA = 16
QUAD, RING = 4, 8
SIDE = 3

f32, bf16 = jnp.float32, jnp.bfloat16
NT = (((1,), (1,)), ((), ()))
NN = (((1,), (0,)), ((), ()))
TT = (((0,), (1,)), ((), ()))


def mm(a, b, dims=NN):
    return lax.dot_general(a, b, dims, preferred_element_type=f32)


def tree(parts):
    while len(parts) > 1:
        parts = [parts[i] + parts[i + 1] for i in range(0, len(parts), 2)]
    return parts[0]


def vmem(n):
    return [pl.BlockSpec(memory_space=pltpu.VMEM)] * n


def smem(n):
    return [pl.BlockSpec(memory_space=pltpu.SMEM)] * n


def call(body, scalars, arrays, outs, mib, flops=0, moved=0, exps=0, scratch=(), name=None):
    return pl.pallas_call(
        body,
        out_shape=outs,
        in_specs=smem(len(scalars)) + vmem(len(arrays)),
        out_specs=jax.tree.map(lambda _: pl.BlockSpec(memory_space=pltpu.VMEM), outs),
        scratch_shapes=list(scratch),
        compiler_params=pltpu.CompilerParams(vmem_limit_bytes=mib << 20),
        cost_estimate=pl.CostEstimate(flops=flops, bytes_accessed=moved, transcendentals=exps),
        name=name,
    )(*scalars, *arrays)


def shape(dims, dtype):
    return jax.ShapeDtypeStruct(dims, dtype)


def spot(head, k):
    return pl.multiple_of(lax.bitwise_xor(head, k) * SHARE, SHARE)


def in_order(ks, refs):
    return [ref for _, ref in sorted(zip(ks, refs), key=lambda pair: pair[0])]


def as_row(column):
    return jnp.transpose(jnp.broadcast_to(column, (ROWS, ROWS)))[:8]


def touch_kernel(*refs):
    refs[-1][...] = jnp.zeros((8, ROWS), f32)


def hold_kernel(own, other, *refs):
    both = refs[-1]
    both[:ROWS, :] = own[...]
    both[ROWS:, :] = other[...]


def norm_kernel(ids, *refs):
    xs = in_order(KS, refs[:GROUPS])
    gain, w_key, w_value, _, kv, normed, mean, mean_row = refs[GROUPS:]
    head = ids[1]
    squares = []
    for x in xs:
        wide = x[...].astype(f32)
        squares.append(jnp.sum(wide * wide, axis=1, keepdims=True))
    average = tree(squares) * (1.0 / D)
    mean[...] = jnp.broadcast_to(average, (ROWS, ROWS))
    mean_row[...] = as_row(average)
    inverse = 1.0 / jnp.sqrt(average + EPS)
    for k, x in enumerate(xs):
        at = pl.ds(spot(head, k), SHARE)
        normed[:, at] = (x[...].astype(f32) * inverse * gain[:, at]).astype(bf16)
    kv[:, :HEAD_DIM] = mm(normed[...], w_key[...]).astype(bf16)
    kv[:, HEAD_DIM:] = mm(normed[...], w_value[...]).astype(bf16)


def project_kernel(ids, *refs):
    xs, dys, (w_out, normed, w_query) = in_order(KS, refs[:GROUPS]), refs[GROUPS : GROUPS + 4], refs[GROUPS + 4 : GROUPS + 7]
    both, dot_row = refs[-2:]
    head = ids[1]
    total = jnp.zeros((ROWS, SHARE), f32)
    parts = []
    for k, x in enumerate(xs):
        dy = dys[k // 2][(k % 2) * ROWS : (k % 2 + 1) * ROWS, :]
        total = total + mm(dy, w_out[:, pl.ds(spot(head, k), SHARE)], NT)
        parts.append(jnp.sum(x[...].astype(f32) * dy.astype(f32), axis=1, keepdims=True))
    both[:ROWS, :] = mm(normed[...], w_query[...]).astype(bf16)
    both[ROWS:, :] = total.astype(bf16)
    dot_row[...] = as_row(tree(parts))


def group(n):
    return slice(n * ROWS, (n + 1) * ROWS)


def lanes(x, op):
    return functools.reduce(op, [x[:, group(n)] for n in range(x.shape[1] // ROWS)])


def stack(ref, blocks):
    for b, block in enumerate(blocks):
        for h in range(HEADS):
            ref[group(b * HEADS + h), :] = block[:, group(h)]


def slot(core):
    return pl.ds(pl.multiple_of(core * ROWS, ROWS), ROWS)


def join_kernel(ids, mine, other, both):
    core = ids[0] % 2
    both[slot(core), :] = mine[...]
    both[slot(1 - core), :] = other[...]


def sort_kernel(ids, *refs):
    core = ids[0] % 2
    for n, ref in enumerate(refs[:SIDE]):
        refs[-1][group(n), :] = ref[slot(1 - core), :]


def softmax_kernel(ids, order, lengths, *refs):
    projections, (kv, across, *near, others) = refs[:QUAD], refs[QUAD : QUAD + SIDE + 3]
    powers, stats, key, value, stacked = refs[QUAD + SIDE + 3 :]
    ctx = ids[0]
    z, place_in_quad, core = ctx // QUAD, ctx % QUAD, ctx % 2
    lane = lax.broadcasted_iota(jnp.int32, (1, ROWS), 1)
    row = lax.broadcasted_iota(jnp.int32, (ROWS, 1), 0)

    def places(owner, i):
        first, second = order[2 * owner] * BLOCK, order[2 * owner + 1] * BLOCK - BLOCK
        return jnp.where(i < BLOCK, first + i, second + i)

    sign = 1 - 2 * core
    blocks = [(kv[...], 0), (across[...], RING // 2)]
    blocks += [(ref[slot(core), :], sign * (n + 1)) for n, ref in enumerate(near)]
    blocks += [(others[group(n), :], -sign * (n + 1)) for n in range(SIDE)]
    found = []
    for n, (block, hop) in enumerate(blocks):
        key[group(n), :] = block[:, :HEAD_DIM]
        value[group(n), :] = block[:, HEAD_DIM:]
        found.append(places(((z + RING - hop) % RING) * QUAD + place_in_quad, lane))
    place = jnp.concatenate(found, axis=1)
    stack(stacked, [p.at[:ROWS, :] for p in projections])
    packed = jnp.zeros((ROWS, ROWS), f32)
    spots = lax.broadcasted_iota(jnp.int32, (ROWS, ROWS), 1)
    for b in range(QUAD):
        mine = places(lax.bitwise_xor(ctx, b), row)
        low = jnp.zeros((ROWS, 1), jnp.int32)
        start = 0
        for r in range(RECORDS):
            low = jnp.where(mine >= start, start, low)
            start = start + lengths[r]
        seen = (place <= mine) & (place >= low)
        scores = mm(stacked[b * SHARE : (b + 1) * SHARE, :], key[...], NT)
        for h in range(HEADS):
            n = b * HEADS + h
            masked = jnp.where(seen, scores[group(h)], NEG)
            shift = jnp.max(lanes(masked, jnp.maximum), axis=1, keepdims=True) * (SCALE * LOG2E)
            power = jnp.exp2(masked * (SCALE * LOG2E) - shift)
            total = jnp.sum(lanes(power, jnp.add), axis=1, keepdims=True)
            half = power.astype(bf16)
            powers[group(n), :] = half
            mixed = mm(half, value[...])
            dot = jnp.sum(projections[b][ROWS:, group(h)].astype(f32) * mixed, axis=1, keepdims=True)
            for m, column in enumerate((shift, total, dot)):
                packed = jnp.where(spots == QUAD * HEADS * m + n, column, packed)
    stats[...] = packed


def gradient_kernel(*refs):
    projections, (key, value, powers), parts = refs[:QUAD], refs[QUAD : QUAD + 3], refs[QUAD + 3 : 2 * QUAD + 3]
    queries, dirs = [p.at[:ROWS, :] for p in projections], [p.at[ROWS:, :] for p in projections]
    own, across, near, others, dq_own, dq_send, grad, query_t, dirs_n, dirs_t = refs[2 * QUAD + 3 :]
    outs = [own, across] + [near.at[n] for n in range(SIDE)] + [others.at[n] for n in range(SIDE)]
    lane = lax.broadcasted_iota(jnp.int32, (ROWS, ROWS), 1)
    groups = QUAD * HEADS

    def toward(x, n):
        return pltpu.roll(x, (ROWS - n) % ROWS, 1)

    def swap(x, n):
        return jnp.where(lane & n == 0, toward(x, n), toward(x, -n))

    same = []
    for r in range(QUAD):
        x = parts[r][...]
        for bit in (1, 2):
            if r & bit:
                x = swap(x, bit * HEADS)
        same.append(x)
    top = functools.reduce(jnp.maximum, same)
    weights = [jnp.exp2(jnp.where(lane < groups, x - top, 0.0)) for x in same]
    total = functools.reduce(jnp.add, [w * toward(x, groups) for w, x in zip(weights, same)])
    total = jnp.where(lane < groups, total, 1.0)
    dot = functools.reduce(jnp.add, [w * toward(x, 2 * groups) for w, x in zip(weights, same)])
    factors = weights[0] / total
    shifts = dot / total * factors
    shifted = []
    for b in range(QUAD):
        for h in range(HEADS):
            n = b * HEADS + h
            shifted.append(shifts[:, n : n + 1])
            scaled = dirs[b][:, group(h)].astype(f32) * factors[:, n : n + 1]
            dirs_n[group(n), :] = scaled.astype(bf16)
            dirs_t[:, group(n)] = jnp.transpose(scaled).astype(bf16)
            query_t[:, group(n)] = jnp.transpose(queries[b][:, group(h)].astype(f32)).astype(bf16)
    for b in (1, 3, 0, 2):
        rows = slice(b * SHARE, (b + 1) * SHARE)
        slope = mm(dirs_n[rows, :], value[...], NT)
        for h in range(HEADS):
            n = b * HEADS + h
            grad[group(n), :] = (powers[group(n), :].astype(f32) * (slope[group(h)] - shifted[n])).astype(bf16)
        query_grad = mm(grad[rows, :], key[...]) * SCALE
        for h in range(HEADS):
            if b % 2:
                dq_send[group(b // 2), group(h)] = query_grad[group(h)].astype(bf16)
            else:
                dq_own[group(b // 2), group(h)] = query_grad[group(h)]
    for t in range(2):
        at = slice(t * SHARE, (t + 1) * SHARE)
        key_part = mm(query_t[...], grad[:, at]) * SCALE
        value_part = mm(dirs_t[...], powers[:, at])
        for n in range(SHARE // ROWS):
            out = outs[t * (SHARE // ROWS) + n]
            out[:HEAD_DIM, :] = key_part[:, group(n)].astype(bf16)
            out[HEAD_DIM:, :] = value_part[:, group(n)].astype(bf16)


def pair_kernel(ids, near, got, *sends):
    core = ids[0] % 2
    for n, send in enumerate(sends):
        send[core] = near[n]
        send[1 - core] = got[n]


def sum_kernel(ids, *refs):
    core = ids[0] % 2
    across, *parts = refs[: 1 + SIDE]
    own, keep, send = refs[1 + SIDE :]
    mine = functools.reduce(jnp.add, [p[core].astype(f32) for p in parts])
    keep[...] = own[...].astype(f32) + across[...].astype(f32) + mine
    send[...] = functools.reduce(jnp.add, [p[1 - core].astype(f32) for p in parts]).astype(bf16)


def add_kernel(own, got, _, stay, send):
    stay[...] = own[:ROWS, :] + got[:ROWS, :].astype(f32)
    send[...] = (own[ROWS:, :] + got[ROWS:, :].astype(f32)).astype(bf16)


def back_query_kernel(stay, got, w_query, hidden):
    query_grad = (stay[...] + got[...].astype(f32)).astype(bf16)
    for k in range(GROUPS):
        at = slice(k * SHARE, (k + 1) * SHARE)
        hidden[:, at] = mm(query_grad, w_query[at, :], NT)


def back_kernel(ids, *refs):
    grads, xs = refs[:2], in_order(KS, refs[2 : 2 + GROUPS])
    gain, hidden, w_key, w_value, own, own_row, *sends = refs[2 + GROUPS :]
    head = ids[1]
    both = functools.reduce(lambda a, b: a + b, [g[...].astype(f32) for g in grads]).astype(bf16)
    key_grad, value_grad = both[:HEAD_DIM], both[HEAD_DIM:]
    inner = []
    for k, x in enumerate(xs):
        at = pl.ds(spot(head, k), SHARE)
        block = hidden[:, at] + mm(key_grad, w_key[at, :], TT) + mm(value_grad, w_value[at, :], TT)
        inner.append(jnp.sum(x[...].astype(f32) * gain[:, at] * block, axis=1, keepdims=True))
        if k == 0:
            own[...] = block
        else:
            sends[k - 1][:ROWS, :] = block.astype(bf16)
    row = jnp.transpose(jnp.broadcast_to(tree(inner), (ROWS, ROWS)))[:EXTRA]
    high = row.astype(bf16)
    lower = (row - high.astype(f32)).astype(bf16)
    own_row[:, :ROWS] = high
    own_row[:, ROWS:] = lower
    for send in sends:
        send[ROWS:, :] = jnp.zeros((EXTRA, SHARE), bf16)
        send[ROWS:, :ROWS] = high
        send[ROWS:, ROWS : 2 * ROWS] = lower


def last_kernel(ids, own, own_row, *refs):
    got = in_order(BACK, refs[: GROUPS - 1])
    x, dy, gain, mean, mean_row, dot_row, input_grad, saliency = refs[GROUPS - 1 :]
    head = ids[1]
    hidden = functools.reduce(lambda a, b: a + b, [g[:ROWS, :].astype(f32) for g in got], own[...])

    def term(ref, at):
        return ref[at : at + EXTRA, :ROWS].astype(f32) + ref[at : at + EXTRA, ROWS : 2 * ROWS].astype(f32)

    total_row = tree([term(own_row, 0)] + [term(g, ROWS) for g in got])[:8]
    root_row = jnp.sqrt(mean_row[...] + EPS)
    inner_row = total_row / (root_row * D)
    sums = dot_row[...] + (total_row - inner_row * (mean_row[...] * D) / root_row) / root_row
    saliency[...] = sums[:1]
    inner = jnp.transpose(jnp.broadcast_to(inner_row[:1], (ROWS, ROWS)))
    inverse = 1.0 / jnp.sqrt(mean[...] + EPS)
    for n in range(SHARE // ROWS):
        at = slice(n * ROWS, (n + 1) * ROWS)
        unit = x[:, at].astype(f32) * inverse
        scaled = hidden[:, at] * gain[:, pl.ds(pl.multiple_of(head * SHARE + n * ROWS, ROWS), ROWS)]
        input_grad[:, at] = (dy[:, at].astype(f32) + (scaled - unit * inner) * inverse).astype(bf16)


def xor_head(a, k):
    return lax.ppermute(a, "head", [(i, i ^ k) for i in range(GROUPS)])


def xor_ctx(a, k):
    return lax.ppermute(a, "ctx", [(i, i ^ k) for i in range(32)])


def touch(arrays):
    return call(touch_kernel, [], arrays, shape((8, ROWS), f32), 16, moved=6 << 20, name="touch")


def turn(a, k):
    return lax.ppermute(a, "ctx", [(i, (i + 4 * k) % 32) for i in range(32)])


def apart(a, k):
    return lax.ppermute(a, "ctx", [(i, (i + 4 * k * (1 - 2 * (i % 2))) % 32) for i in range(32)])


def spread(a):
    across = xor_ctx(a, 2)
    return [a, xor_ctx(a, 1), across, xor_ctx(across, 1)]


def local(inputs, out_grad, norm_gain, w_query, w_key, w_value, w_out, record_lengths, block_order):
    ids = jnp.stack([lax.axis_index("ctx"), lax.axis_index("head")]).astype(jnp.int32)
    gain = norm_gain.reshape(1, D)
    xs = [xor_head(inputs, k) if k else inputs for k in KS]
    ready = touch([w_key, w_value, gain, inputs, out_grad])
    kv, normed, mean, mean_row = call(
        norm_kernel,
        [ids],
        [*xs, gain, w_key, w_value, ready],
        [
            shape((ROWS, WIDE), bf16),
            shape((ROWS, D), bf16),
            shape((ROWS, ROWS), f32),
            shape((8, ROWS), f32),
        ],
        16,
        flops=2 * ROWS * D * WIDE,
        moved=5 << 20,
        name="norm_kv",
    )
    both = call(join_kernel, [ids], [kv, xor_ctx(kv, 1)], shape((2 * ROWS, WIDE), bf16), 4, moved=1 << 18, name="join")
    near = [apart(both, n) for n in range(1, SIDE + 1)]
    kvs = [kv, turn(kv, RING // 2), *near]
    given = call(sort_kernel, [ids], [*near, kvs[1]], shape((SIDE * ROWS, WIDE), bf16), 4, moved=1 << 19, name="sort")
    kvs.append(xor_ctx(given, 1))
    held = call(
        hold_kernel,
        [],
        [out_grad, xor_head(out_grad, 1), kv],
        shape((2 * ROWS, SHARE), bf16),
        4,
        moved=1 << 19,
        name="hold",
    )
    dys = [held] + [xor_head(held, k) for k in (2, 4, 6)]
    ready_out = touch([w_out, w_query, normed])
    projected, dot_row = call(
        project_kernel,
        [ids],
        [*xs, *dys, w_out, normed, w_query, ready_out, near[1], near[2]],
        [shape((2 * ROWS, SHARE), bf16), shape((8, ROWS), f32)],
        24,
        flops=4 * ROWS * D * SHARE,
        moved=10 << 20,
        name="project",
    )
    projections = spread(projected)
    tall = QUAD * HEADS * ROWS
    powers, stats, key, value = call(
        softmax_kernel,
        [ids, block_order, record_lengths],
        [*projections, *kvs],
        [
            shape((tall, KEYS), bf16),
            shape((ROWS, ROWS), f32),
            shape((KEYS, HEAD_DIM), bf16),
            shape((KEYS, HEAD_DIM), bf16),
        ],
        24,
        flops=4 * tall * KEYS * HEAD_DIM,
        moved=6 << 20,
        exps=tall * KEYS,
        scratch=[pltpu.VMEM((tall, HEAD_DIM), bf16)],
        name="softmax",
    )
    parts = spread(stats)
    part = shape((WIDE, HEAD_DIM), bf16)
    side = shape((SIDE, WIDE, HEAD_DIM), bf16)
    own, across, near, others, dq_own, dq_send = call(
        gradient_kernel,
        [],
        [*projections, key, value, powers, *parts],
        [part, part, side, side, shape((2 * ROWS, SHARE), f32), shape((2 * ROWS, SHARE), bf16)],
        32,
        flops=8 * tall * KEYS * HEAD_DIM,
        moved=6 << 20,
        scratch=[
            pltpu.VMEM((tall, KEYS), bf16),
            pltpu.VMEM((HEAD_DIM, tall), bf16),
            pltpu.VMEM((tall, HEAD_DIM), bf16),
            pltpu.VMEM((HEAD_DIM, tall), bf16),
        ],
        name="gradient",
    )
    far_part = turn(across, RING // 2)
    sends = call(
        pair_kernel,
        [ids],
        [near, xor_ctx(others, 1)],
        [shape((2, WIDE, HEAD_DIM), bf16)] * SIDE,
        8,
        moved=1 << 20,
        name="pair",
    )
    keep, give = call(
        sum_kernel,
        [ids],
        [far_part, *[apart(a, -n) for n, a in enumerate(sends, 1)], own],
        [shape((WIDE, HEAD_DIM), f32), part],
        8,
        moved=1 << 20,
        name="sum",
    )
    grads = [keep, xor_ctx(give, 1)]
    stay, dq_far = call(
        add_kernel,
        [],
        [dq_own, xor_ctx(dq_send, 1), far_part],
        [shape((ROWS, SHARE), f32), shape((ROWS, SHARE), bf16)],
        16,
        flops=4 * ROWS * SHARE,
        moved=2 << 20,
        name="add",
    )
    hidden = call(
        back_query_kernel,
        [],
        [stay, xor_ctx(dq_far, 2), w_query],
        shape((ROWS, D), f32),
        16,
        flops=2 * ROWS * D * SHARE,
        moved=6 << 20,
        name="back_query",
    )
    own, own_row, *sends = call(
        back_kernel,
        [ids],
        [*grads, *xs, gain, hidden, w_key, w_value],
        [shape((ROWS, SHARE), f32), shape((EXTRA, WIDE), bf16)]
        + [shape((ROWS + EXTRA, SHARE), bf16)] * (GROUPS - 1),
        24,
        flops=2 * ROWS * D * WIDE,
        moved=7 << 20,
        name="back_kv",
    )
    home = [xor_head(sends[k - 1], k) for k in BACK]
    input_grad, saliency = call(
        last_kernel,
        [ids],
        [own, own_row, *home, inputs, out_grad, gain, mean, mean_row, dot_row],
        [shape((ROWS, SHARE), bf16), shape((1, ROWS), f32)],
        16,
        flops=10 * ROWS * SHARE,
        moved=3 << 20,
        name="last",
    )
    return (input_grad, saliency.reshape(ROWS))


def solution(mesh):
    placed = (
        P("ctx", "head"),
        P("ctx", "head"),
        P(),
        P(None, "head"),
        P(None, "head"),
        P(None, "head"),
        P("head", None),
        P(),
        P(),
    )
    return jax.shard_map(
        local, mesh=mesh, in_specs=placed, out_specs=(P("ctx", "head"), P("ctx")), check_vma=False
    )
```

```python
import functools

import jax
import jax.numpy as jnp
from jax import lax
from jax.experimental import pallas as pl
from jax.experimental.pallas import tpu as pltpu
from jax.sharding import PartitionSpec as P

D = 4096
HEAD_DIM = 128
BLOCK = 64
ROWS = 128
SHARE = 512
HEADS = 4
GROUPS = 8
RECORDS = 8
KEYS = 1024
WIDE = 2 * HEAD_DIM
EPS = 1e-05
SCALE = HEAD_DIM ** (-0.5)
LOG2E = 1.4426950408889634
NEG = -1e30
KS = (0, 7, 6, 3, 5, 4, 2, 1)
BACK = (1, 2, 4, 5, 3, 6, 7)
EXTRA = 16
QUAD, RING = 4, 8
SIDE = 3

f32, bf16 = jnp.float32, jnp.bfloat16
NT = (((1,), (1,)), ((), ()))
NN = (((1,), (0,)), ((), ()))
TT = (((0,), (1,)), ((), ()))


def mm(a, b, dims=NN):
    return lax.dot_general(a, b, dims, preferred_element_type=f32)


def tree(parts):
    while len(parts) > 1:
        parts = [parts[i] + parts[i + 1] for i in range(0, len(parts), 2)]
    return parts[0]


def vmem(n):
    return [pl.BlockSpec(memory_space=pltpu.VMEM)] * n


def smem(n):
    return [pl.BlockSpec(memory_space=pltpu.SMEM)] * n


def call(body, scalars, arrays, outs, mib, flops=0, moved=0, exps=0, scratch=(), name=None):
    return pl.pallas_call(
        body,
        out_shape=outs,
        in_specs=smem(len(scalars)) + vmem(len(arrays)),
        out_specs=jax.tree.map(lambda _: pl.BlockSpec(memory_space=pltpu.VMEM), outs),
        scratch_shapes=list(scratch),
        compiler_params=pltpu.CompilerParams(vmem_limit_bytes=mib << 20),
        cost_estimate=pl.CostEstimate(flops=flops, bytes_accessed=moved, transcendentals=exps),
        name=name,
    )(*scalars, *arrays)


def shape(dims, dtype):
    return jax.ShapeDtypeStruct(dims, dtype)


def spot(head, k):
    return pl.multiple_of(lax.bitwise_xor(head, k) * SHARE, SHARE)


def in_order(ks, refs):
    return [ref for _, ref in sorted(zip(ks, refs), key=lambda pair: pair[0])]


def as_row(column):
    return jnp.transpose(jnp.broadcast_to(column, (ROWS, ROWS)))[:8]


def touch_kernel(*refs):
    refs[-1][...] = jnp.zeros((8, ROWS), f32)


def hold_kernel(own, other, *refs):
    both = refs[-1]
    both[:ROWS, :] = own[...]
    both[ROWS:, :] = other[...]


def norm_kernel(ids, *refs):
    xs = in_order(KS, refs[:GROUPS])
    gain, w_key, w_value, _, kv, normed, mean, mean_row = refs[GROUPS:]
    head = ids[1]
    squares = []
    for x in xs:
        wide = x[...].astype(f32)
        squares.append(jnp.sum(wide * wide, axis=1, keepdims=True))
    average = tree(squares) * (1.0 / D)
    mean[...] = jnp.broadcast_to(average, (ROWS, ROWS))
    mean_row[...] = as_row(average)
    inverse = 1.0 / jnp.sqrt(average + EPS)
    for k, x in enumerate(xs):
        at = pl.ds(spot(head, k), SHARE)
        normed[:, at] = (x[...].astype(f32) * inverse * gain[:, at]).astype(bf16)
    kv[:, :HEAD_DIM] = mm(normed[...], w_key[...]).astype(bf16)
    kv[:, HEAD_DIM:] = mm(normed[...], w_value[...]).astype(bf16)


def project_kernel(ids, *refs):
    xs, dys, (w_out, normed, w_query) = in_order(KS, refs[:GROUPS]), refs[GROUPS : GROUPS + 4], refs[GROUPS + 4 : GROUPS + 7]
    both, dot_row = refs[-2:]
    head = ids[1]
    total = jnp.zeros((ROWS, SHARE), f32)
    parts = []
    for k, x in enumerate(xs):
        dy = dys[k // 2][(k % 2) * ROWS : (k % 2 + 1) * ROWS, :]
        total = total + mm(dy, w_out[:, pl.ds(spot(head, k), SHARE)], NT)
        parts.append(jnp.sum(x[...].astype(f32) * dy.astype(f32), axis=1, keepdims=True))
    both[:ROWS, :] = mm(normed[...], w_query[...]).astype(bf16)
    both[ROWS:, :] = total.astype(bf16)
    dot_row[...] = as_row(tree(parts))


def group(n):
    return slice(n * ROWS, (n + 1) * ROWS)


def lanes(x, op):
    return functools.reduce(op, [x[:, group(n)] for n in range(x.shape[1] // ROWS)])


def stack(ref, blocks):
    for b, block in enumerate(blocks):
        for h in range(HEADS):
            ref[group(b * HEADS + h), :] = block[:, group(h)]


def slot(core):
    return pl.ds(pl.multiple_of(core * ROWS, ROWS), ROWS)


def join_kernel(ids, mine, other, both):
    core = ids[0] % 2
    both[slot(core), :] = mine[...]
    both[slot(1 - core), :] = other[...]


def sort_kernel(ids, *refs):
    core = ids[0] % 2
    for n, ref in enumerate(refs[:SIDE]):
        refs[-1][group(n), :] = ref[slot(1 - core), :]


def softmax_kernel(ids, order, lengths, *refs):
    projections, (kv, across, *near, others) = refs[:QUAD], refs[QUAD : QUAD + SIDE + 3]
    powers, stats, key, value, stacked = refs[QUAD + SIDE + 3 :]
    ctx = ids[0]
    z, place_in_quad, core = ctx // QUAD, ctx % QUAD, ctx % 2
    lane = lax.broadcasted_iota(jnp.int32, (1, ROWS), 1)
    row = lax.broadcasted_iota(jnp.int32, (ROWS, 1), 0)

    def places(owner, i):
        first, second = order[2 * owner] * BLOCK, order[2 * owner + 1] * BLOCK - BLOCK
        return jnp.where(i < BLOCK, first + i, second + i)

    sign = 1 - 2 * core
    blocks = [(kv[...], 0), (across[...], RING // 2)]
    blocks += [(ref[slot(core), :], sign * (n + 1)) for n, ref in enumerate(near)]
    blocks += [(others[group(n), :], -sign * (n + 1)) for n in range(SIDE)]
    found = []
    for n, (block, hop) in enumerate(blocks):
        key[group(n), :] = block[:, :HEAD_DIM]
        value[group(n), :] = block[:, HEAD_DIM:]
        found.append(places(((z + RING - hop) % RING) * QUAD + place_in_quad, lane))
    place = jnp.concatenate(found, axis=1)
    stack(stacked, [p.at[:ROWS, :] for p in projections])
    packed = jnp.zeros((ROWS, ROWS), f32)
    spots = lax.broadcasted_iota(jnp.int32, (ROWS, ROWS), 1)
    for b in range(QUAD):
        mine = places(lax.bitwise_xor(ctx, b), row)
        low = jnp.zeros((ROWS, 1), jnp.int32)
        start = 0
        for r in range(RECORDS):
            low = jnp.where(mine >= start, start, low)
            start = start + lengths[r]
        seen = (place <= mine) & (place >= low)
        scores = mm(stacked[b * SHARE : (b + 1) * SHARE, :], key[...], NT)
        for h in range(HEADS):
            n = b * HEADS + h
            masked = jnp.where(seen, scores[group(h)], NEG)
            shift = jnp.max(lanes(masked, jnp.maximum), axis=1, keepdims=True) * (SCALE * LOG2E)
            power = jnp.exp2(masked * (SCALE * LOG2E) - shift)
            total = jnp.sum(lanes(power, jnp.add), axis=1, keepdims=True)
            half = power.astype(bf16)
            powers[group(n), :] = half
            mixed = mm(half, value[...])
            dot = jnp.sum(projections[b][ROWS:, group(h)].astype(f32) * mixed, axis=1, keepdims=True)
            for m, column in enumerate((shift, total, dot)):
                packed = jnp.where(spots == QUAD * HEADS * m + n, column, packed)
    stats[...] = packed


def gradient_kernel(*refs):
    projections, (key, value, powers), parts = refs[:QUAD], refs[QUAD : QUAD + 3], refs[QUAD + 3 : 2 * QUAD + 3]
    queries, dirs = [p.at[:ROWS, :] for p in projections], [p.at[ROWS:, :] for p in projections]
    own, across, near, others, dq_own, dq_send, grad, query_t, dirs_n, dirs_t = refs[2 * QUAD + 3 :]
    outs = [own, across] + [near.at[n] for n in range(SIDE)] + [others.at[n] for n in range(SIDE)]
    lane = lax.broadcasted_iota(jnp.int32, (ROWS, ROWS), 1)
    groups = QUAD * HEADS

    def toward(x, n):
        return pltpu.roll(x, (ROWS - n) % ROWS, 1)

    def swap(x, n):
        return jnp.where(lane & n == 0, toward(x, n), toward(x, -n))

    same = []
    for r in range(QUAD):
        x = parts[r][...]
        for bit in (1, 2):
            if r & bit:
                x = swap(x, bit * HEADS)
        same.append(x)
    top = functools.reduce(jnp.maximum, same)
    weights = [jnp.exp2(jnp.where(lane < groups, x - top, 0.0)) for x in same]
    total = functools.reduce(jnp.add, [w * toward(x, groups) for w, x in zip(weights, same)])
    total = jnp.where(lane < groups, total, 1.0)
    dot = functools.reduce(jnp.add, [w * toward(x, 2 * groups) for w, x in zip(weights, same)])
    factors = weights[0] / total
    shifts = dot / total * factors
    shifted = []
    for b in range(QUAD):
        for h in range(HEADS):
            n = b * HEADS + h
            shifted.append(shifts[:, n : n + 1])
            scaled = dirs[b][:, group(h)].astype(f32) * factors[:, n : n + 1]
            dirs_n[group(n), :] = scaled.astype(bf16)
            dirs_t[:, group(n)] = jnp.transpose(scaled).astype(bf16)
            query_t[:, group(n)] = jnp.transpose(queries[b][:, group(h)].astype(f32)).astype(bf16)
    for b in (1, 3, 0, 2):
        rows = slice(b * SHARE, (b + 1) * SHARE)
        slope = mm(dirs_n[rows, :], value[...], NT)
        for h in range(HEADS):
            n = b * HEADS + h
            grad[group(n), :] = (powers[group(n), :].astype(f32) * (slope[group(h)] - shifted[n])).astype(bf16)
        query_grad = mm(grad[rows, :], key[...]) * SCALE
        for h in range(HEADS):
            if b % 2:
                dq_send[group(b // 2), group(h)] = query_grad[group(h)].astype(bf16)
            else:
                dq_own[group(b // 2), group(h)] = query_grad[group(h)]
    for t in range(2):
        at = slice(t * SHARE, (t + 1) * SHARE)
        key_part = mm(query_t[...], grad[:, at]) * SCALE
        value_part = mm(dirs_t[...], powers[:, at])
        for n in range(SHARE // ROWS):
            out = outs[t * (SHARE // ROWS) + n]
            out[:HEAD_DIM, :] = key_part[:, group(n)].astype(bf16)
            out[HEAD_DIM:, :] = value_part[:, group(n)].astype(bf16)


def pair_kernel(ids, near, got, *sends):
    core = ids[0] % 2
    for n, send in enumerate(sends):
        send[core] = near[n]
        send[1 - core] = got[n]


def sum_kernel(ids, *refs):
    core = ids[0] % 2
    across, *parts = refs[: 1 + SIDE]
    own, keep, send = refs[1 + SIDE :]
    mine = functools.reduce(jnp.add, [p[core].astype(f32) for p in parts])
    keep[...] = own[...].astype(f32) + across[...].astype(f32) + mine
    send[...] = functools.reduce(jnp.add, [p[1 - core].astype(f32) for p in parts]).astype(bf16)


def add_kernel(own, got, _, stay, send):
    stay[...] = own[:ROWS, :] + got[:ROWS, :].astype(f32)
    send[...] = (own[ROWS:, :] + got[ROWS:, :].astype(f32)).astype(bf16)


def back_query_kernel(stay, got, w_query, hidden):
    query_grad = (stay[...] + got[...].astype(f32)).astype(bf16)
    for k in range(GROUPS):
        at = slice(k * SHARE, (k + 1) * SHARE)
        hidden[:, at] = mm(query_grad, w_query[at, :], NT)


def back_kernel(ids, *refs):
    grads, xs = refs[:2], in_order(KS, refs[2 : 2 + GROUPS])
    gain, hidden, w_key, w_value, own, own_row, *sends = refs[2 + GROUPS :]
    head = ids[1]
    both = functools.reduce(lambda a, b: a + b, [g[...].astype(f32) for g in grads]).astype(bf16)
    key_grad, value_grad = both[:HEAD_DIM], both[HEAD_DIM:]
    inner = []
    for k, x in enumerate(xs):
        at = pl.ds(spot(head, k), SHARE)
        block = hidden[:, at] + mm(key_grad, w_key[at, :], TT) + mm(value_grad, w_value[at, :], TT)
        inner.append(jnp.sum(x[...].astype(f32) * gain[:, at] * block, axis=1, keepdims=True))
        if k == 0:
            own[...] = block
        else:
            sends[k - 1][:ROWS, :] = block.astype(bf16)
    row = jnp.transpose(jnp.broadcast_to(tree(inner), (ROWS, ROWS)))[:EXTRA]
    high = row.astype(bf16)
    lower = (row - high.astype(f32)).astype(bf16)
    own_row[:, :ROWS] = high
    own_row[:, ROWS:] = lower
    for send in sends:
        send[ROWS:, :] = jnp.zeros((EXTRA, SHARE), bf16)
        send[ROWS:, :ROWS] = high
        send[ROWS:, ROWS : 2 * ROWS] = lower


def last_kernel(ids, own, own_row, *refs):
    got = in_order(BACK, refs[: GROUPS - 1])
    x, dy, gain, mean, mean_row, dot_row, input_grad, saliency = refs[GROUPS - 1 :]
    head = ids[1]
    hidden = functools.reduce(lambda a, b: a + b, [g[:ROWS, :].astype(f32) for g in got], own[...])

    def term(ref, at):
        return ref[at : at + EXTRA, :ROWS].astype(f32) + ref[at : at + EXTRA, ROWS : 2 * ROWS].astype(f32)

    total_row = tree([term(own_row, 0)] + [term(g, ROWS) for g in got])[:8]
    root_row = jnp.sqrt(mean_row[...] + EPS)
    inner_row = total_row / (root_row * D)
    sums = dot_row[...] + (total_row - inner_row * (mean_row[...] * D) / root_row) / root_row
    saliency[...] = sums[:1]
    inner = jnp.transpose(jnp.broadcast_to(inner_row[:1], (ROWS, ROWS)))
    inverse = 1.0 / jnp.sqrt(mean[...] + EPS)
    for n in range(SHARE // ROWS):
        at = slice(n * ROWS, (n + 1) * ROWS)
        unit = x[:, at].astype(f32) * inverse
        scaled = hidden[:, at] * gain[:, pl.ds(pl.multiple_of(head * SHARE + n * ROWS, ROWS), ROWS)]
        input_grad[:, at] = (dy[:, at].astype(f32) + (scaled - unit * inner) * inverse).astype(bf16)


def xor_head(a, k):
    return lax.ppermute(a, "head", [(i, i ^ k) for i in range(GROUPS)])


def xor_ctx(a, k):
    return lax.ppermute(a, "ctx", [(i, i ^ k) for i in range(32)])


def touch(arrays):
    return call(touch_kernel, [], arrays, shape((8, ROWS), f32), 16, moved=6 << 20, name="touch")


def turn(a, k):
    return lax.ppermute(a, "ctx", [(i, (i + 4 * k) % 32) for i in range(32)])


def apart(a, k):
    return lax.ppermute(a, "ctx", [(i, (i + 4 * k * (1 - 2 * (i % 2))) % 32) for i in range(32)])


def spread(a):
    across = xor_ctx(a, 2)
    return [a, xor_ctx(a, 1), across, xor_ctx(across, 1)]


def local(inputs, out_grad, norm_gain, w_query, w_key, w_value, w_out, record_lengths, block_order):
    ids = jnp.stack([lax.axis_index("ctx"), lax.axis_index("head")]).astype(jnp.int32)
    gain = norm_gain.reshape(1, D)
    xs = [xor_head(inputs, k) if k else inputs for k in KS]
    ready = touch([w_key, w_value, gain, inputs])
    kv, normed, mean, mean_row = call(
        norm_kernel,
        [ids],
        [*xs, gain, w_key, w_value, ready],
        [
            shape((ROWS, WIDE), bf16),
            shape((ROWS, D), bf16),
            shape((ROWS, ROWS), f32),
            shape((8, ROWS), f32),
        ],
        16,
        flops=2 * ROWS * D * WIDE,
        moved=5 << 20,
        name="norm_kv",
    )
    both = call(join_kernel, [ids], [kv, xor_ctx(kv, 1)], shape((2 * ROWS, WIDE), bf16), 4, moved=1 << 18, name="join")
    near = [apart(both, n) for n in range(1, SIDE + 1)]
    kvs = [kv, turn(kv, RING // 2), *near]
    given = call(sort_kernel, [ids], [*near, kvs[1]], shape((SIDE * ROWS, WIDE), bf16), 4, moved=1 << 19, name="sort")
    kvs.append(xor_ctx(given, 1))
    held = call(
        hold_kernel,
        [],
        [out_grad, xor_head(out_grad, 1), kv],
        shape((2 * ROWS, SHARE), bf16),
        4,
        moved=1 << 19,
        name="hold",
    )
    dys = [held] + [xor_head(held, k) for k in (2, 4, 6)]
    ready_out = touch([w_out, w_query, normed])
    projected, dot_row = call(
        project_kernel,
        [ids],
        [*xs, *dys, w_out, normed, w_query, ready_out, kvs[1], near[2]],
        [shape((2 * ROWS, SHARE), bf16), shape((8, ROWS), f32)],
        24,
        flops=4 * ROWS * D * SHARE,
        moved=10 << 20,
        name="project",
    )
    projections = spread(projected)
    tall = QUAD * HEADS * ROWS
    powers, stats, key, value = call(
        softmax_kernel,
        [ids, block_order, record_lengths],
        [*projections, *kvs],
        [
            shape((tall, KEYS), bf16),
            shape((ROWS, ROWS), f32),
            shape((KEYS, HEAD_DIM), bf16),
            shape((KEYS, HEAD_DIM), bf16),
        ],
        24,
        flops=4 * tall * KEYS * HEAD_DIM,
        moved=6 << 20,
        exps=tall * KEYS,
        scratch=[pltpu.VMEM((tall, HEAD_DIM), bf16)],
        name="softmax",
    )
    parts = spread(stats)
    part = shape((WIDE, HEAD_DIM), bf16)
    side = shape((SIDE, WIDE, HEAD_DIM), bf16)
    own, across, near, others, dq_own, dq_send = call(
        gradient_kernel,
        [],
        [*projections, key, value, powers, *parts],
        [part, part, side, side, shape((2 * ROWS, SHARE), f32), shape((2 * ROWS, SHARE), bf16)],
        32,
        flops=8 * tall * KEYS * HEAD_DIM,
        moved=6 << 20,
        scratch=[
            pltpu.VMEM((tall, KEYS), bf16),
            pltpu.VMEM((HEAD_DIM, tall), bf16),
            pltpu.VMEM((tall, HEAD_DIM), bf16),
            pltpu.VMEM((HEAD_DIM, tall), bf16),
        ],
        name="gradient",
    )
    far_part = turn(across, RING // 2)
    sends = call(
        pair_kernel,
        [ids],
        [near, xor_ctx(others, 1)],
        [shape((2, WIDE, HEAD_DIM), bf16)] * SIDE,
        8,
        moved=1 << 20,
        name="pair",
    )
    keep, give = call(
        sum_kernel,
        [ids],
        [far_part, *[apart(a, -n) for n, a in enumerate(sends, 1)], own],
        [shape((WIDE, HEAD_DIM), f32), part],
        8,
        moved=1 << 20,
        name="sum",
    )
    grads = [keep, xor_ctx(give, 1)]
    stay, dq_far = call(
        add_kernel,
        [],
        [dq_own, xor_ctx(dq_send, 1), far_part],
        [shape((ROWS, SHARE), f32), shape((ROWS, SHARE), bf16)],
        16,
        flops=4 * ROWS * SHARE,
        moved=2 << 20,
        name="add",
    )
    hidden = call(
        back_query_kernel,
        [],
        [stay, xor_ctx(dq_far, 2), w_query],
        shape((ROWS, D), f32),
        16,
        flops=2 * ROWS * D * SHARE,
        moved=6 << 20,
        name="back_query",
    )
    own, own_row, *sends = call(
        back_kernel,
        [ids],
        [*grads, *xs, gain, hidden, w_key, w_value],
        [shape((ROWS, SHARE), f32), shape((EXTRA, WIDE), bf16)]
        + [shape((ROWS + EXTRA, SHARE), bf16)] * (GROUPS - 1),
        24,
        flops=2 * ROWS * D * WIDE,
        moved=7 << 20,
        name="back_kv",
    )
    home = [xor_head(sends[k - 1], k) for k in BACK]
    input_grad, saliency = call(
        last_kernel,
        [ids],
        [own, own_row, *home, inputs, out_grad, gain, mean, mean_row, dot_row],
        [shape((ROWS, SHARE), bf16), shape((1, ROWS), f32)],
        16,
        flops=10 * ROWS * SHARE,
        moved=3 << 20,
        name="last",
    )
    return (input_grad, saliency.reshape(ROWS))


def solution(mesh):
    placed = (
        P("ctx", "head"),
        P("ctx", "head"),
        P(),
        P(None, "head"),
        P(None, "head"),
        P(None, "head"),
        P("head", None),
        P(),
        P(),
    )
    return jax.shard_map(
        local, mesh=mesh, in_specs=placed, out_specs=(P("ctx", "head"), P("ctx")), check_vma=False
    )
```

```python
import functools

import jax
import jax.numpy as jnp
from jax import lax
from jax.experimental import pallas as pl
from jax.experimental.pallas import tpu as pltpu
from jax.sharding import PartitionSpec as P

D = 4096
HEAD_DIM = 128
BLOCK = 64
ROWS = 128
SHARE = 512
HEADS = 4
GROUPS = 8
RECORDS = 8
KEYS = 1024
WIDE = 2 * HEAD_DIM
EPS = 1e-05
SCALE = HEAD_DIM ** (-0.5)
LOG2E = 1.4426950408889634
NEG = -1e30
KS = (0, 7, 6, 3, 5, 4, 2, 1)
BACK = (1, 2, 4, 5, 3, 6, 7)
EXTRA = 16
QUAD, RING = 4, 8
SIDE = 3

f32, bf16 = jnp.float32, jnp.bfloat16
NT = (((1,), (1,)), ((), ()))
NN = (((1,), (0,)), ((), ()))
TT = (((0,), (1,)), ((), ()))


def mm(a, b, dims=NN):
    return lax.dot_general(a, b, dims, preferred_element_type=f32)


def tree(parts):
    while len(parts) > 1:
        parts = [parts[i] + parts[i + 1] for i in range(0, len(parts), 2)]
    return parts[0]


def vmem(n):
    return [pl.BlockSpec(memory_space=pltpu.VMEM)] * n


def smem(n):
    return [pl.BlockSpec(memory_space=pltpu.SMEM)] * n


def call(body, scalars, arrays, outs, mib, flops=0, moved=0, exps=0, scratch=(), name=None):
    return pl.pallas_call(
        body,
        out_shape=outs,
        in_specs=smem(len(scalars)) + vmem(len(arrays)),
        out_specs=jax.tree.map(lambda _: pl.BlockSpec(memory_space=pltpu.VMEM), outs),
        scratch_shapes=list(scratch),
        compiler_params=pltpu.CompilerParams(vmem_limit_bytes=mib << 20),
        cost_estimate=pl.CostEstimate(flops=flops, bytes_accessed=moved, transcendentals=exps),
        name=name,
    )(*scalars, *arrays)


def shape(dims, dtype):
    return jax.ShapeDtypeStruct(dims, dtype)


def spot(head, k):
    return pl.multiple_of(lax.bitwise_xor(head, k) * SHARE, SHARE)


def in_order(ks, refs):
    return [ref for _, ref in sorted(zip(ks, refs), key=lambda pair: pair[0])]


def as_row(column):
    return jnp.transpose(jnp.broadcast_to(column, (ROWS, ROWS)))[:8]


def touch_kernel(*refs):
    refs[-1][...] = jnp.zeros((8, ROWS), f32)


def hold_kernel(own, other, *refs):
    both = refs[-1]
    both[:ROWS, :] = own[...]
    both[ROWS:, :] = other[...]


def norm_kernel(ids, *refs):
    xs = in_order(KS, refs[:GROUPS])
    gain, w_key, w_value, _, kv, normed, mean, mean_row = refs[GROUPS:]
    head = ids[1]
    squares = []
    for x in xs:
        wide = x[...].astype(f32)
        squares.append(jnp.sum(wide * wide, axis=1, keepdims=True))
    average = tree(squares) * (1.0 / D)
    mean[...] = jnp.broadcast_to(average, (ROWS, ROWS))
    mean_row[...] = as_row(average)
    inverse = 1.0 / jnp.sqrt(average + EPS)
    for k, x in enumerate(xs):
        at = pl.ds(spot(head, k), SHARE)
        normed[:, at] = (x[...].astype(f32) * inverse * gain[:, at]).astype(bf16)
    kv[:, :HEAD_DIM] = mm(normed[...], w_key[...]).astype(bf16)
    kv[:, HEAD_DIM:] = mm(normed[...], w_value[...]).astype(bf16)


def project_kernel(ids, *refs):
    xs, dys, (w_out, normed, w_query) = in_order(KS, refs[:GROUPS]), refs[GROUPS : GROUPS + 4], refs[GROUPS + 4 : GROUPS + 7]
    both, dot_row = refs[-2:]
    head = ids[1]
    total = jnp.zeros((ROWS, SHARE), f32)
    parts = []
    for k, x in enumerate(xs):
        dy = dys[k // 2][(k % 2) * ROWS : (k % 2 + 1) * ROWS, :]
        total = total + mm(dy, w_out[:, pl.ds(spot(head, k), SHARE)], NT)
        parts.append(jnp.sum(x[...].astype(f32) * dy.astype(f32), axis=1, keepdims=True))
    both[:ROWS, :] = mm(normed[...], w_query[...]).astype(bf16)
    both[ROWS:, :] = total.astype(bf16)
    dot_row[...] = as_row(tree(parts))


def group(n):
    return slice(n * ROWS, (n + 1) * ROWS)


def lanes(x, op):
    return functools.reduce(op, [x[:, group(n)] for n in range(x.shape[1] // ROWS)])


def stack(ref, blocks):
    for b, block in enumerate(blocks):
        for h in range(HEADS):
            ref[group(b * HEADS + h), :] = block[:, group(h)]


def slot(core):
    return pl.ds(pl.multiple_of(core * ROWS, ROWS), ROWS)


def join_kernel(ids, mine, other, both):
    core = ids[0] % 2
    both[slot(core), :] = mine[...]
    both[slot(1 - core), :] = other[...]


def sort_kernel(ids, *refs):
    core = ids[0] % 2
    for n, ref in enumerate(refs[:SIDE]):
        refs[-1][group(n), :] = ref[slot(1 - core), :]


def softmax_kernel(ids, order, lengths, *refs):
    projections, (kv, across, *near, others) = refs[:QUAD], refs[QUAD : QUAD + SIDE + 3]
    powers, stats, key, value, stacked = refs[QUAD + SIDE + 3 :]
    ctx = ids[0]
    z, place_in_quad, core = ctx // QUAD, ctx % QUAD, ctx % 2
    lane = lax.broadcasted_iota(jnp.int32, (1, ROWS), 1)
    row = lax.broadcasted_iota(jnp.int32, (ROWS, 1), 0)

    def places(owner, i):
        first, second = order[2 * owner] * BLOCK, order[2 * owner + 1] * BLOCK - BLOCK
        return jnp.where(i < BLOCK, first + i, second + i)

    sign = 1 - 2 * core
    blocks = [(kv[...], 0), (across[...], RING // 2)]
    blocks += [(ref[slot(core), :], sign * (n + 1)) for n, ref in enumerate(near)]
    blocks += [(others[group(n), :], -sign * (n + 1)) for n in range(SIDE)]
    found = []
    for n, (block, hop) in enumerate(blocks):
        key[group(n), :] = block[:, :HEAD_DIM]
        value[group(n), :] = block[:, HEAD_DIM:]
        found.append(places(((z + RING - hop) % RING) * QUAD + place_in_quad, lane))
    place = jnp.concatenate(found, axis=1)
    stack(stacked, [p.at[:ROWS, :] for p in projections])
    packed = jnp.zeros((ROWS, ROWS), f32)
    spots = lax.broadcasted_iota(jnp.int32, (ROWS, ROWS), 1)
    for b in range(QUAD):
        mine = places(lax.bitwise_xor(ctx, b), row)
        low = jnp.zeros((ROWS, 1), jnp.int32)
        start = 0
        for r in range(RECORDS):
            low = jnp.where(mine >= start, start, low)
            start = start + lengths[r]
        seen = (place <= mine) & (place >= low)
        scores = mm(stacked[b * SHARE : (b + 1) * SHARE, :], key[...], NT)
        for h in range(HEADS):
            n = b * HEADS + h
            masked = jnp.where(seen, scores[group(h)], NEG)
            shift = jnp.max(lanes(masked, jnp.maximum), axis=1, keepdims=True) * (SCALE * LOG2E)
            power = jnp.exp2(masked * (SCALE * LOG2E) - shift)
            total = jnp.sum(lanes(power, jnp.add), axis=1, keepdims=True)
            half = power.astype(bf16)
            powers[group(n), :] = half
            mixed = mm(half, value[...])
            dot = jnp.sum(projections[b][ROWS:, group(h)].astype(f32) * mixed, axis=1, keepdims=True)
            for m, column in enumerate((shift, total, dot)):
                packed = jnp.where(spots == QUAD * HEADS * m + n, column, packed)
    stats[...] = packed


def gradient_kernel(*refs):
    projections, (key, value, powers), parts = refs[:QUAD], refs[QUAD : QUAD + 3], refs[QUAD + 3 : 2 * QUAD + 3]
    queries, dirs = [p.at[:ROWS, :] for p in projections], [p.at[ROWS:, :] for p in projections]
    own, across, near, others, dq_own, dq_send, grad, query_t, dirs_n, dirs_t = refs[2 * QUAD + 3 :]
    outs = [own, across] + [near.at[n] for n in range(SIDE)] + [others.at[n] for n in range(SIDE)]
    lane = lax.broadcasted_iota(jnp.int32, (ROWS, ROWS), 1)
    groups = QUAD * HEADS

    def toward(x, n):
        return pltpu.roll(x, (ROWS - n) % ROWS, 1)

    def swap(x, n):
        return jnp.where(lane & n == 0, toward(x, n), toward(x, -n))

    same = []
    for r in range(QUAD):
        x = parts[r][...]
        for bit in (1, 2):
            if r & bit:
                x = swap(x, bit * HEADS)
        same.append(x)
    top = functools.reduce(jnp.maximum, same)
    weights = [jnp.exp2(jnp.where(lane < groups, x - top, 0.0)) for x in same]
    total = functools.reduce(jnp.add, [w * toward(x, groups) for w, x in zip(weights, same)])
    total = jnp.where(lane < groups, total, 1.0)
    dot = functools.reduce(jnp.add, [w * toward(x, 2 * groups) for w, x in zip(weights, same)])
    factors = weights[0] / total
    shifts = dot / total * factors
    shifted = []
    for b in range(QUAD):
        for h in range(HEADS):
            n = b * HEADS + h
            shifted.append(shifts[:, n : n + 1])
            scaled = dirs[b][:, group(h)].astype(f32) * factors[:, n : n + 1]
            dirs_n[group(n), :] = scaled.astype(bf16)
            dirs_t[:, group(n)] = jnp.transpose(scaled).astype(bf16)
            query_t[:, group(n)] = jnp.transpose(queries[b][:, group(h)].astype(f32)).astype(bf16)
    for b in (1, 3, 0, 2):
        rows = slice(b * SHARE, (b + 1) * SHARE)
        slope = mm(dirs_n[rows, :], value[...], NT)
        for h in range(HEADS):
            n = b * HEADS + h
            grad[group(n), :] = (powers[group(n), :].astype(f32) * (slope[group(h)] - shifted[n])).astype(bf16)
        query_grad = mm(grad[rows, :], key[...]) * SCALE
        for h in range(HEADS):
            if b % 2:
                dq_send[group(b // 2), group(h)] = query_grad[group(h)].astype(bf16)
            else:
                dq_own[group(b // 2), group(h)] = query_grad[group(h)]
    for t in range(2):
        at = slice(t * SHARE, (t + 1) * SHARE)
        key_part = mm(query_t[...], grad[:, at]) * SCALE
        value_part = mm(dirs_t[...], powers[:, at])
        for n in range(SHARE // ROWS):
            out = outs[t * (SHARE // ROWS) + n]
            out[:HEAD_DIM, :] = key_part[:, group(n)].astype(bf16)
            out[HEAD_DIM:, :] = value_part[:, group(n)].astype(bf16)


def pair_kernel(ids, near, got, *sends):
    core = ids[0] % 2
    for n, send in enumerate(sends):
        send[core] = near[n]
        send[1 - core] = got[n]


def sum_kernel(ids, *refs):
    core = ids[0] % 2
    across, *parts = refs[: 1 + SIDE]
    own, keep, send = refs[1 + SIDE :]
    mine = functools.reduce(jnp.add, [p[core].astype(f32) for p in parts])
    keep[...] = own[...].astype(f32) + across[...].astype(f32) + mine
    send[...] = functools.reduce(jnp.add, [p[1 - core].astype(f32) for p in parts]).astype(bf16)


def add_kernel(own, got, _, stay, send):
    stay[...] = own[:ROWS, :] + got[:ROWS, :].astype(f32)
    send[...] = (own[ROWS:, :] + got[ROWS:, :].astype(f32)).astype(bf16)


def back_query_kernel(stay, got, w_query, hidden):
    query_grad = (stay[...] + got[...].astype(f32)).astype(bf16)
    for k in range(GROUPS):
        at = slice(k * SHARE, (k + 1) * SHARE)
        hidden[:, at] = mm(query_grad, w_query[at, :], NT)


def back_kernel(ids, *refs):
    grads, xs = refs[:2], in_order(KS, refs[2 : 2 + GROUPS])
    gain, hidden, w_key, w_value, own, own_row, *sends = refs[2 + GROUPS :]
    head = ids[1]
    both = functools.reduce(lambda a, b: a + b, [g[...].astype(f32) for g in grads]).astype(bf16)
    key_grad, value_grad = both[:HEAD_DIM], both[HEAD_DIM:]
    inner = []
    for k, x in enumerate(xs):
        at = pl.ds(spot(head, k), SHARE)
        block = hidden[:, at] + mm(key_grad, w_key[at, :], TT) + mm(value_grad, w_value[at, :], TT)
        inner.append(jnp.sum(x[...].astype(f32) * gain[:, at] * block, axis=1, keepdims=True))
        if k == 0:
            own[...] = block
        else:
            sends[k - 1][:ROWS, :] = block.astype(bf16)
    row = jnp.transpose(jnp.broadcast_to(tree(inner), (ROWS, ROWS)))[:EXTRA]
    high = row.astype(bf16)
    lower = (row - high.astype(f32)).astype(bf16)
    own_row[:, :ROWS] = high
    own_row[:, ROWS:] = lower
    for send in sends:
        send[ROWS:, :] = jnp.zeros((EXTRA, SHARE), bf16)
        send[ROWS:, :ROWS] = high
        send[ROWS:, ROWS : 2 * ROWS] = lower


def last_kernel(ids, own, own_row, *refs):
    got = in_order(BACK, refs[: GROUPS - 1])
    x, dy, gain, mean, mean_row, dot_row, input_grad, saliency = refs[GROUPS - 1 :]
    head = ids[1]
    hidden = functools.reduce(lambda a, b: a + b, [g[:ROWS, :].astype(f32) for g in got], own[...])

    def term(ref, at):
        return ref[at : at + EXTRA, :ROWS].astype(f32) + ref[at : at + EXTRA, ROWS : 2 * ROWS].astype(f32)

    total_row = tree([term(own_row, 0)] + [term(g, ROWS) for g in got])[:8]
    root_row = jnp.sqrt(mean_row[...] + EPS)
    inner_row = total_row / (root_row * D)
    sums = dot_row[...] + (total_row - inner_row * (mean_row[...] * D) / root_row) / root_row
    saliency[...] = sums[:1]
    inner = jnp.transpose(jnp.broadcast_to(inner_row[:1], (ROWS, ROWS)))
    inverse = 1.0 / jnp.sqrt(mean[...] + EPS)
    for n in range(SHARE // ROWS):
        at = slice(n * ROWS, (n + 1) * ROWS)
        unit = x[:, at].astype(f32) * inverse
        scaled = hidden[:, at] * gain[:, pl.ds(pl.multiple_of(head * SHARE + n * ROWS, ROWS), ROWS)]
        input_grad[:, at] = (dy[:, at].astype(f32) + (scaled - unit * inner) * inverse).astype(bf16)


def xor_head(a, k):
    return lax.ppermute(a, "head", [(i, i ^ k) for i in range(GROUPS)])


def xor_ctx(a, k):
    return lax.ppermute(a, "ctx", [(i, i ^ k) for i in range(32)])


def touch(arrays):
    return call(touch_kernel, [], arrays, shape((8, ROWS), f32), 16, moved=6 << 20, name="touch")


def turn(a, k):
    return lax.ppermute(a, "ctx", [(i, (i + 4 * k) % 32) for i in range(32)])


def apart(a, k):
    return lax.ppermute(a, "ctx", [(i, (i + 4 * k * (1 - 2 * (i % 2))) % 32) for i in range(32)])


def spread(a):
    across = xor_ctx(a, 2)
    return [a, xor_ctx(a, 1), across, xor_ctx(across, 1)]


def local(inputs, out_grad, norm_gain, w_query, w_key, w_value, w_out, record_lengths, block_order):
    ids = jnp.stack([lax.axis_index("ctx"), lax.axis_index("head")]).astype(jnp.int32)
    gain = norm_gain.reshape(1, D)
    xs = [xor_head(inputs, k) if k else inputs for k in KS]
    ready = touch([w_key, w_value, gain, inputs])
    kv, normed, mean, mean_row = call(
        norm_kernel,
        [ids],
        [*xs, gain, w_key, w_value, ready],
        [
            shape((ROWS, WIDE), bf16),
            shape((ROWS, D), bf16),
            shape((ROWS, ROWS), f32),
            shape((8, ROWS), f32),
        ],
        16,
        flops=2 * ROWS * D * WIDE,
        moved=5 << 20,
        name="norm_kv",
    )
    both = call(join_kernel, [ids], [kv, xor_ctx(kv, 1)], shape((2 * ROWS, WIDE), bf16), 4, moved=1 << 18, name="join")
    near = [apart(both, n) for n in range(1, SIDE + 1)]
    kvs = [kv, turn(kv, RING // 2), *near]
    given = call(sort_kernel, [ids], [*near, kvs[1]], shape((SIDE * ROWS, WIDE), bf16), 4, moved=1 << 19, name="sort")
    kvs.append(xor_ctx(given, 1))
    held = call(
        hold_kernel,
        [],
        [out_grad, xor_head(out_grad, 1), kv],
        shape((2 * ROWS, SHARE), bf16),
        4,
        moved=1 << 19,
        name="hold",
    )
    dys = [held] + [xor_head(held, k) for k in (2, 4, 6)]
    ready_out = touch([w_out, w_query, normed])
    projected, dot_row = call(
        project_kernel,
        [ids],
        [*xs, *dys, w_out, normed, w_query, ready_out, near[2]],
        [shape((2 * ROWS, SHARE), bf16), shape((8, ROWS), f32)],
        24,
        flops=4 * ROWS * D * SHARE,
        moved=10 << 20,
        name="project",
    )
    projections = spread(projected)
    tall = QUAD * HEADS * ROWS
    powers, stats, key, value = call(
        softmax_kernel,
        [ids, block_order, record_lengths],
        [*projections, *kvs],
        [
            shape((tall, KEYS), bf16),
            shape((ROWS, ROWS), f32),
            shape((KEYS, HEAD_DIM), bf16),
            shape((KEYS, HEAD_DIM), bf16),
        ],
        24,
        flops=4 * tall * KEYS * HEAD_DIM,
        moved=6 << 20,
        exps=tall * KEYS,
        scratch=[pltpu.VMEM((tall, HEAD_DIM), bf16)],
        name="softmax",
    )
    parts = spread(stats)
    part = shape((WIDE, HEAD_DIM), bf16)
    side = shape((SIDE, WIDE, HEAD_DIM), bf16)
    own, across, near, others, dq_own, dq_send = call(
        gradient_kernel,
        [],
        [*projections, key, value, powers, *parts],
        [part, part, side, side, shape((2 * ROWS, SHARE), f32), shape((2 * ROWS, SHARE), bf16)],
        32,
        flops=8 * tall * KEYS * HEAD_DIM,
        moved=6 << 20,
        scratch=[
            pltpu.VMEM((tall, KEYS), bf16),
            pltpu.VMEM((HEAD_DIM, tall), bf16),
            pltpu.VMEM((tall, HEAD_DIM), bf16),
            pltpu.VMEM((HEAD_DIM, tall), bf16),
        ],
        name="gradient",
    )
    far_part = turn(across, RING // 2)
    sends = call(
        pair_kernel,
        [ids],
        [near, xor_ctx(others, 1)],
        [shape((2, WIDE, HEAD_DIM), bf16)] * SIDE,
        8,
        moved=1 << 20,
        name="pair",
    )
    keep, give = call(
        sum_kernel,
        [ids],
        [far_part, *[apart(a, -n) for n, a in enumerate(sends, 1)], own],
        [shape((WIDE, HEAD_DIM), f32), part],
        8,
        moved=1 << 20,
        name="sum",
    )
    grads = [keep, xor_ctx(give, 1)]
    stay, dq_far = call(
        add_kernel,
        [],
        [dq_own, xor_ctx(dq_send, 1), far_part],
        [shape((ROWS, SHARE), f32), shape((ROWS, SHARE), bf16)],
        16,
        flops=4 * ROWS * SHARE,
        moved=2 << 20,
        name="add",
    )
    hidden = call(
        back_query_kernel,
        [],
        [stay, xor_ctx(dq_far, 2), w_query],
        shape((ROWS, D), f32),
        16,
        flops=2 * ROWS * D * SHARE,
        moved=6 << 20,
        name="back_query",
    )
    own, own_row, *sends = call(
        back_kernel,
        [ids],
        [*grads, *xs, gain, hidden, w_key, w_value],
        [shape((ROWS, SHARE), f32), shape((EXTRA, WIDE), bf16)]
        + [shape((ROWS + EXTRA, SHARE), bf16)] * (GROUPS - 1),
        24,
        flops=2 * ROWS * D * WIDE,
        moved=7 << 20,
        name="back_kv",
    )
    home = [xor_head(sends[k - 1], k) for k in BACK]
    input_grad, saliency = call(
        last_kernel,
        [ids],
        [own, own_row, *home, inputs, out_grad, gain, mean, mean_row, dot_row],
        [shape((ROWS, SHARE), bf16), shape((1, ROWS), f32)],
        16,
        flops=10 * ROWS * SHARE,
        moved=3 << 20,
        name="last",
    )
    return (input_grad, saliency.reshape(ROWS))


def solution(mesh):
    placed = (
        P("ctx", "head"),
        P("ctx", "head"),
        P(),
        P(None, "head"),
        P(None, "head"),
        P(None, "head"),
        P("head", None),
        P(),
        P(),
    )
    return jax.shard_map(
        local, mesh=mesh, in_specs=placed, out_specs=(P("ctx", "head"), P("ctx")), check_vma=False
    )
```

```python
import functools

import jax
import jax.numpy as jnp
from jax import lax
from jax.experimental import pallas as pl
from jax.experimental.pallas import tpu as pltpu
from jax.sharding import PartitionSpec as P

D = 4096
HEAD_DIM = 128
BLOCK = 64
ROWS = 128
SHARE = 512
HEADS = 4
GROUPS = 8
RECORDS = 8
KEYS = 1024
WIDE = 2 * HEAD_DIM
EPS = 1e-05
SCALE = HEAD_DIM ** (-0.5)
LOG2E = 1.4426950408889634
NEG = -1e30
KS = (0, 7, 6, 3, 5, 4, 2, 1)
BACK = (1, 2, 4, 5, 3, 6, 7)
EXTRA = 16
QUAD, RING = 4, 8
SIDE = 3

f32, bf16 = jnp.float32, jnp.bfloat16
NT = (((1,), (1,)), ((), ()))
NN = (((1,), (0,)), ((), ()))
TT = (((0,), (1,)), ((), ()))


def mm(a, b, dims=NN):
    return lax.dot_general(a, b, dims, preferred_element_type=f32)


def tree(parts):
    while len(parts) > 1:
        parts = [parts[i] + parts[i + 1] for i in range(0, len(parts), 2)]
    return parts[0]


def vmem(n):
    return [pl.BlockSpec(memory_space=pltpu.VMEM)] * n


def smem(n):
    return [pl.BlockSpec(memory_space=pltpu.SMEM)] * n


def call(body, scalars, arrays, outs, mib, flops=0, moved=0, exps=0, scratch=(), name=None):
    return pl.pallas_call(
        body,
        out_shape=outs,
        in_specs=smem(len(scalars)) + vmem(len(arrays)),
        out_specs=jax.tree.map(lambda _: pl.BlockSpec(memory_space=pltpu.VMEM), outs),
        scratch_shapes=list(scratch),
        compiler_params=pltpu.CompilerParams(vmem_limit_bytes=mib << 20),
        cost_estimate=pl.CostEstimate(flops=flops, bytes_accessed=moved, transcendentals=exps),
        name=name,
    )(*scalars, *arrays)


def shape(dims, dtype):
    return jax.ShapeDtypeStruct(dims, dtype)


def spot(head, k):
    return pl.multiple_of(lax.bitwise_xor(head, k) * SHARE, SHARE)


def in_order(ks, refs):
    return [ref for _, ref in sorted(zip(ks, refs), key=lambda pair: pair[0])]


def as_row(column):
    return jnp.transpose(jnp.broadcast_to(column, (ROWS, ROWS)))[:8]


def touch_kernel(*refs):
    refs[-1][...] = jnp.zeros((8, ROWS), f32)


def copy_kernel(x, out):
    out[...] = x[...]


def hold_kernel(own, other, *refs):
    both = refs[-1]
    both[:ROWS, :] = own[...]
    both[ROWS:, :] = other[...]


def norm_kernel(ids, *refs):
    xs = in_order(KS, refs[:GROUPS])
    gain, w_key, w_value, _, kv, normed, mean, mean_row = refs[GROUPS:]
    head = ids[1]
    squares = []
    for x in xs:
        wide = x[...].astype(f32)
        squares.append(jnp.sum(wide * wide, axis=1, keepdims=True))
    average = tree(squares) * (1.0 / D)
    mean[...] = jnp.broadcast_to(average, (ROWS, ROWS))
    mean_row[...] = as_row(average)
    inverse = 1.0 / jnp.sqrt(average + EPS)
    for k, x in enumerate(xs):
        at = pl.ds(spot(head, k), SHARE)
        normed[:, at] = (x[...].astype(f32) * inverse * gain[:, at]).astype(bf16)
    kv[:, :HEAD_DIM] = mm(normed[...], w_key[...]).astype(bf16)
    kv[:, HEAD_DIM:] = mm(normed[...], w_value[...]).astype(bf16)


def project_kernel(ids, *refs):
    xs, dys, (w_out, normed, w_query) = in_order(KS, refs[:GROUPS]), refs[GROUPS : GROUPS + 4], refs[GROUPS + 4 : GROUPS + 7]
    both, dot_row = refs[-2:]
    head = ids[1]
    total = jnp.zeros((ROWS, SHARE), f32)
    parts = []
    for k, x in enumerate(xs):
        dy = dys[k // 2][(k % 2) * ROWS : (k % 2 + 1) * ROWS, :]
        total = total + mm(dy, w_out[:, pl.ds(spot(head, k), SHARE)], NT)
        parts.append(jnp.sum(x[...].astype(f32) * dy.astype(f32), axis=1, keepdims=True))
    both[:ROWS, :] = mm(normed[...], w_query[...]).astype(bf16)
    both[ROWS:, :] = total.astype(bf16)
    dot_row[...] = as_row(tree(parts))


def group(n):
    return slice(n * ROWS, (n + 1) * ROWS)


def lanes(x, op):
    return functools.reduce(op, [x[:, group(n)] for n in range(x.shape[1] // ROWS)])


def stack(ref, blocks):
    for b, block in enumerate(blocks):
        for h in range(HEADS):
            ref[group(b * HEADS + h), :] = block[:, group(h)]


def slot(core):
    return pl.ds(pl.multiple_of(core * ROWS, ROWS), ROWS)


def join_kernel(ids, mine, other, both):
    core = ids[0] % 2
    both[slot(core), :] = mine[...]
    both[slot(1 - core), :] = other[...]


def sort_kernel(ids, *refs):
    core = ids[0] % 2
    for n, ref in enumerate(refs[:SIDE]):
        refs[-1][group(n), :] = ref[slot(1 - core), :]


def softmax_kernel(ids, order, lengths, *refs):
    projections, (kv, across, *near, others) = refs[:QUAD], refs[QUAD : QUAD + SIDE + 3]
    powers, stats, key, value, stacked = refs[QUAD + SIDE + 3 :]
    ctx = ids[0]
    z, place_in_quad, core = ctx // QUAD, ctx % QUAD, ctx % 2
    lane = lax.broadcasted_iota(jnp.int32, (1, ROWS), 1)
    row = lax.broadcasted_iota(jnp.int32, (ROWS, 1), 0)

    def places(owner, i):
        first, second = order[2 * owner] * BLOCK, order[2 * owner + 1] * BLOCK - BLOCK
        return jnp.where(i < BLOCK, first + i, second + i)

    sign = 1 - 2 * core
    blocks = [(kv[...], 0), (across[...], RING // 2)]
    blocks += [(ref[slot(core), :], sign * (n + 1)) for n, ref in enumerate(near)]
    blocks += [(others[group(n), :], -sign * (n + 1)) for n in range(SIDE)]
    found = []
    for n, (block, hop) in enumerate(blocks):
        key[group(n), :] = block[:, :HEAD_DIM]
        value[group(n), :] = block[:, HEAD_DIM:]
        found.append(places(((z + RING - hop) % RING) * QUAD + place_in_quad, lane))
    place = jnp.concatenate(found, axis=1)
    stack(stacked, [p.at[:ROWS, :] for p in projections])
    packed = jnp.zeros((ROWS, ROWS), f32)
    spots = lax.broadcasted_iota(jnp.int32, (ROWS, ROWS), 1)
    for b in range(QUAD):
        mine = places(lax.bitwise_xor(ctx, b), row)
        low = jnp.zeros((ROWS, 1), jnp.int32)
        start = 0
        for r in range(RECORDS):
            low = jnp.where(mine >= start, start, low)
            start = start + lengths[r]
        seen = (place <= mine) & (place >= low)
        scores = mm(stacked[b * SHARE : (b + 1) * SHARE, :], key[...], NT)
        for h in range(HEADS):
            n = b * HEADS + h
            masked = jnp.where(seen, scores[group(h)], NEG)
            shift = jnp.max(lanes(masked, jnp.maximum), axis=1, keepdims=True) * (SCALE * LOG2E)
            power = jnp.exp2(masked * (SCALE * LOG2E) - shift)
            total = jnp.sum(lanes(power, jnp.add), axis=1, keepdims=True)
            half = power.astype(bf16)
            powers[group(n), :] = half
            mixed = mm(half, value[...])
            dot = jnp.sum(projections[b][ROWS:, group(h)].astype(f32) * mixed, axis=1, keepdims=True)
            for m, column in enumerate((shift, total, dot)):
                packed = jnp.where(spots == QUAD * HEADS * m + n, column, packed)
    stats[...] = packed


def gradient_kernel(*refs):
    projections, (key, value, powers), parts = refs[:QUAD], refs[QUAD : QUAD + 3], refs[QUAD + 3 : 2 * QUAD + 3]
    queries, dirs = [p.at[:ROWS, :] for p in projections], [p.at[ROWS:, :] for p in projections]
    own, across, near, others, dq_own, dq_send, grad, query_t, dirs_n, dirs_t = refs[2 * QUAD + 3 :]
    outs = [own, across] + [near.at[n] for n in range(SIDE)] + [others.at[n] for n in range(SIDE)]
    lane = lax.broadcasted_iota(jnp.int32, (ROWS, ROWS), 1)
    groups = QUAD * HEADS

    def toward(x, n):
        return pltpu.roll(x, (ROWS - n) % ROWS, 1)

    def swap(x, n):
        return jnp.where(lane & n == 0, toward(x, n), toward(x, -n))

    same = []
    for r in range(QUAD):
        x = parts[r][...]
        for bit in (1, 2):
            if r & bit:
                x = swap(x, bit * HEADS)
        same.append(x)
    top = functools.reduce(jnp.maximum, same)
    weights = [jnp.exp2(jnp.where(lane < groups, x - top, 0.0)) for x in same]
    total = functools.reduce(jnp.add, [w * toward(x, groups) for w, x in zip(weights, same)])
    total = jnp.where(lane < groups, total, 1.0)
    dot = functools.reduce(jnp.add, [w * toward(x, 2 * groups) for w, x in zip(weights, same)])
    factors = weights[0] / total
    shifts = dot / total * factors
    shifted = []
    for b in range(QUAD):
        for h in range(HEADS):
            n = b * HEADS + h
            shifted.append(shifts[:, n : n + 1])
            scaled = dirs[b][:, group(h)].astype(f32) * factors[:, n : n + 1]
            dirs_n[group(n), :] = scaled.astype(bf16)
            dirs_t[:, group(n)] = jnp.transpose(scaled).astype(bf16)
            query_t[:, group(n)] = jnp.transpose(queries[b][:, group(h)].astype(f32)).astype(bf16)
    for b in (1, 3, 0, 2):
        rows = slice(b * SHARE, (b + 1) * SHARE)
        slope = mm(dirs_n[rows, :], value[...], NT)
        for h in range(HEADS):
            n = b * HEADS + h
            grad[group(n), :] = (powers[group(n), :].astype(f32) * (slope[group(h)] - shifted[n])).astype(bf16)
        query_grad = mm(grad[rows, :], key[...]) * SCALE
        for h in range(HEADS):
            if b % 2:
                dq_send[group(b // 2), group(h)] = query_grad[group(h)].astype(bf16)
            else:
                dq_own[group(b // 2), group(h)] = query_grad[group(h)]
    for t in range(2):
        at = slice(t * SHARE, (t + 1) * SHARE)
        key_part = mm(query_t[...], grad[:, at]) * SCALE
        value_part = mm(dirs_t[...], powers[:, at])
        for n in range(SHARE // ROWS):
            out = outs[t * (SHARE // ROWS) + n]
            out[:HEAD_DIM, :] = key_part[:, group(n)].astype(bf16)
            out[HEAD_DIM:, :] = value_part[:, group(n)].astype(bf16)


def pair_kernel(ids, near, got, *sends):
    core = ids[0] % 2
    for n, send in enumerate(sends):
        send[core] = near[n]
        send[1 - core] = got[n]


def sum_kernel(ids, *refs):
    core = ids[0] % 2
    across, *parts = refs[: 1 + SIDE]
    own, keep, send = refs[1 + SIDE :]
    mine = functools.reduce(jnp.add, [p[core].astype(f32) for p in parts])
    keep[...] = own[...].astype(f32) + across[...].astype(f32) + mine
    send[...] = functools.reduce(jnp.add, [p[1 - core].astype(f32) for p in parts]).astype(bf16)


def add_kernel(own, got, _, stay, send):
    stay[...] = own[:ROWS, :] + got[:ROWS, :].astype(f32)
    send[...] = (own[ROWS:, :] + got[ROWS:, :].astype(f32)).astype(bf16)


def back_query_kernel(stay, got, w_query, hidden):
    query_grad = (stay[...] + got[...].astype(f32)).astype(bf16)
    for k in range(GROUPS):
        at = slice(k * SHARE, (k + 1) * SHARE)
        hidden[:, at] = mm(query_grad, w_query[at, :], NT)


def back_kernel(ids, *refs):
    grads, xs = refs[:2], in_order(KS, refs[2 : 2 + GROUPS])
    gain, hidden, w_key, w_value, own, own_row, *sends = refs[2 + GROUPS :]
    head = ids[1]
    both = functools.reduce(lambda a, b: a + b, [g[...].astype(f32) for g in grads]).astype(bf16)
    key_grad, value_grad = both[:HEAD_DIM], both[HEAD_DIM:]
    inner = []
    for k, x in enumerate(xs):
        at = pl.ds(spot(head, k), SHARE)
        block = hidden[:, at] + mm(key_grad, w_key[at, :], TT) + mm(value_grad, w_value[at, :], TT)
        inner.append(jnp.sum(x[...].astype(f32) * gain[:, at] * block, axis=1, keepdims=True))
        if k == 0:
            own[...] = block
        else:
            sends[k - 1][:ROWS, :] = block.astype(bf16)
    row = jnp.transpose(jnp.broadcast_to(tree(inner), (ROWS, ROWS)))[:EXTRA]
    high = row.astype(bf16)
    lower = (row - high.astype(f32)).astype(bf16)
    own_row[:, :ROWS] = high
    own_row[:, ROWS:] = lower
    for send in sends:
        send[ROWS:, :] = jnp.zeros((EXTRA, SHARE), bf16)
        send[ROWS:, :ROWS] = high
        send[ROWS:, ROWS : 2 * ROWS] = lower


def last_kernel(ids, own, own_row, *refs):
    got = in_order(BACK, refs[: GROUPS - 1])
    x, dy, gain, mean, mean_row, dot_row, input_grad, saliency = refs[GROUPS - 1 :]
    head = ids[1]
    hidden = functools.reduce(lambda a, b: a + b, [g[:ROWS, :].astype(f32) for g in got], own[...])

    def term(ref, at):
        return ref[at : at + EXTRA, :ROWS].astype(f32) + ref[at : at + EXTRA, ROWS : 2 * ROWS].astype(f32)

    total_row = tree([term(own_row, 0)] + [term(g, ROWS) for g in got])[:8]
    root_row = jnp.sqrt(mean_row[...] + EPS)
    inner_row = total_row / (root_row * D)
    sums = dot_row[...] + (total_row - inner_row * (mean_row[...] * D) / root_row) / root_row
    saliency[...] = sums[:1]
    inner = jnp.transpose(jnp.broadcast_to(inner_row[:1], (ROWS, ROWS)))
    inverse = 1.0 / jnp.sqrt(mean[...] + EPS)
    for n in range(SHARE // ROWS):
        at = slice(n * ROWS, (n + 1) * ROWS)
        unit = x[:, at].astype(f32) * inverse
        scaled = hidden[:, at] * gain[:, pl.ds(pl.multiple_of(head * SHARE + n * ROWS, ROWS), ROWS)]
        input_grad[:, at] = (dy[:, at].astype(f32) + (scaled - unit * inner) * inverse).astype(bf16)


def xor_head(a, k):
    return lax.ppermute(a, "head", [(i, i ^ k) for i in range(GROUPS)])


def xor_ctx(a, k):
    return lax.ppermute(a, "ctx", [(i, i ^ k) for i in range(32)])


def touch(arrays):
    return call(touch_kernel, [], arrays, shape((8, ROWS), f32), 16, moved=6 << 20, name="touch")


def turn(a, k):
    return lax.ppermute(a, "ctx", [(i, (i + 4 * k) % 32) for i in range(32)])


def apart(a, k):
    return lax.ppermute(a, "ctx", [(i, (i + 4 * k * (1 - 2 * (i % 2))) % 32) for i in range(32)])


def spread(a):
    across = xor_ctx(a, 2)
    return [a, xor_ctx(a, 1), across, xor_ctx(across, 1)]


def local(inputs, out_grad, norm_gain, w_query, w_key, w_value, w_out, record_lengths, block_order):
    ids = jnp.stack([lax.axis_index("ctx"), lax.axis_index("head")]).astype(jnp.int32)
    gain = norm_gain.reshape(1, D)
    xs = [xor_head(inputs, k) if k else inputs for k in KS]
    ready = touch([w_key, w_value, gain, inputs])
    kv, normed, mean, mean_row = call(
        norm_kernel,
        [ids],
        [*xs, gain, w_key, w_value, ready],
        [
            shape((ROWS, WIDE), bf16),
            shape((ROWS, D), bf16),
            shape((ROWS, ROWS), f32),
            shape((8, ROWS), f32),
        ],
        16,
        flops=2 * ROWS * D * WIDE,
        moved=5 << 20,
        name="norm_kv",
    )
    both = call(join_kernel, [ids], [kv, xor_ctx(kv, 1)], shape((2 * ROWS, WIDE), bf16), 4, moved=1 << 18, name="join")
    near = [apart(both, n) for n in range(1, SIDE + 1)]
    kvs = [kv, turn(kv, RING // 2), *near]
    given = call(sort_kernel, [ids], [*near, kvs[1]], shape((SIDE * ROWS, WIDE), bf16), 4, moved=1 << 19, name="sort")
    kvs.append(xor_ctx(given, 1))
    grad = call(copy_kernel, [], [out_grad], shape((ROWS, SHARE), bf16), 4, moved=1 << 18, name="copy")
    held = call(
        hold_kernel,
        [],
        [grad, xor_head(grad, 1), kv],
        shape((2 * ROWS, SHARE), bf16),
        4,
        moved=1 << 19,
        name="hold",
    )
    dys = [held] + [xor_head(held, k) for k in (2, 4, 6)]
    ready_out = touch([w_out, w_query, normed])
    projected, dot_row = call(
        project_kernel,
        [ids],
        [*xs, *dys, w_out, normed, w_query, ready_out, kvs[1], near[2]],
        [shape((2 * ROWS, SHARE), bf16), shape((8, ROWS), f32)],
        24,
        flops=4 * ROWS * D * SHARE,
        moved=10 << 20,
        name="project",
    )
    projections = spread(projected)
    tall = QUAD * HEADS * ROWS
    powers, stats, key, value = call(
        softmax_kernel,
        [ids, block_order, record_lengths],
        [*projections, *kvs],
        [
            shape((tall, KEYS), bf16),
            shape((ROWS, ROWS), f32),
            shape((KEYS, HEAD_DIM), bf16),
            shape((KEYS, HEAD_DIM), bf16),
        ],
        24,
        flops=4 * tall * KEYS * HEAD_DIM,
        moved=6 << 20,
        exps=tall * KEYS,
        scratch=[pltpu.VMEM((tall, HEAD_DIM), bf16)],
        name="softmax",
    )
    parts = spread(stats)
    part = shape((WIDE, HEAD_DIM), bf16)
    side = shape((SIDE, WIDE, HEAD_DIM), bf16)
    own, across, near, others, dq_own, dq_send = call(
        gradient_kernel,
        [],
        [*projections, key, value, powers, *parts],
        [part, part, side, side, shape((2 * ROWS, SHARE), f32), shape((2 * ROWS, SHARE), bf16)],
        32,
        flops=8 * tall * KEYS * HEAD_DIM,
        moved=6 << 20,
        scratch=[
            pltpu.VMEM((tall, KEYS), bf16),
            pltpu.VMEM((HEAD_DIM, tall), bf16),
            pltpu.VMEM((tall, HEAD_DIM), bf16),
            pltpu.VMEM((HEAD_DIM, tall), bf16),
        ],
        name="gradient",
    )
    far_part = turn(across, RING // 2)
    sends = call(
        pair_kernel,
        [ids],
        [near, xor_ctx(others, 1)],
        [shape((2, WIDE, HEAD_DIM), bf16)] * SIDE,
        8,
        moved=1 << 20,
        name="pair",
    )
    keep, give = call(
        sum_kernel,
        [ids],
        [far_part, *[apart(a, -n) for n, a in enumerate(sends, 1)], own],
        [shape((WIDE, HEAD_DIM), f32), part],
        8,
        moved=1 << 20,
        name="sum",
    )
    grads = [keep, xor_ctx(give, 1)]
    stay, dq_far = call(
        add_kernel,
        [],
        [dq_own, xor_ctx(dq_send, 1), far_part],
        [shape((ROWS, SHARE), f32), shape((ROWS, SHARE), bf16)],
        16,
        flops=4 * ROWS * SHARE,
        moved=2 << 20,
        name="add",
    )
    hidden = call(
        back_query_kernel,
        [],
        [stay, xor_ctx(dq_far, 2), w_query],
        shape((ROWS, D), f32),
        16,
        flops=2 * ROWS * D * SHARE,
        moved=6 << 20,
        name="back_query",
    )
    own, own_row, *sends = call(
        back_kernel,
        [ids],
        [*grads, *xs, gain, hidden, w_key, w_value],
        [shape((ROWS, SHARE), f32), shape((EXTRA, WIDE), bf16)]
        + [shape((ROWS + EXTRA, SHARE), bf16)] * (GROUPS - 1),
        24,
        flops=2 * ROWS * D * WIDE,
        moved=7 << 20,
        name="back_kv",
    )
    home = [xor_head(sends[k - 1], k) for k in BACK]
    input_grad, saliency = call(
        last_kernel,
        [ids],
        [own, own_row, *home, inputs, out_grad, gain, mean, mean_row, dot_row],
        [shape((ROWS, SHARE), bf16), shape((1, ROWS), f32)],
        16,
        flops=10 * ROWS * SHARE,
        moved=3 << 20,
        name="last",
    )
    return (input_grad, saliency.reshape(ROWS))


def solution(mesh):
    placed = (
        P("ctx", "head"),
        P("ctx", "head"),
        P(),
        P(None, "head"),
        P(None, "head"),
        P(None, "head"),
        P("head", None),
        P(),
        P(),
    )
    return jax.shard_map(
        local, mesh=mesh, in_specs=placed, out_specs=(P("ctx", "head"), P("ctx")), check_vma=False
    )
```
